128 devices in a mesh: grp: 2 (over x_hi), row: 32 (over y, z, x_lo), col: 2 (over core).
Axes of the slice: x: 4 (x_hi: 2, x_lo: 2; x = x_hi * 2 + x_lo), y: 4, z: 4, core: 2. Of those that a mesh axis runs over, the one named last changes fastest.
Arguments:
- order_field: float32 [4, 16, 1024, 1024], P('grp', None, 'row', 'col'), may hold values from 0 to 1
- grain_label: int32 [4, 1024, 1024], P('grp', 'row', 'col'), may hold values from 0 to 31
- phase_label: int32 [4, 1024, 1024], P('grp', 'row', 'col'), may hold values from 0 to 7
- grain_mobility: float32 [32], replicated, may hold values from 0.25 to 1
- stiff_index: int32 [8], replicated, may hold values from 0 to 3
- stiff_table: float32 [4, 2], replicated, may hold values from 0.5 to 2
- eigen_strain: float32 [16, 3], replicated, may hold values from -1.5 to 1.5
- macro_strain: float32 [3], replicated, may hold values from -2 to 2
Outputs:
- order_next: float32 [4, 16, 1024, 1024], P('grp', None, 'row', 'col')
- strain_field: float32 [4, 3, 1024, 1024], P('grp', None, 'row', 'col')
The draws below stay inside these ranges and needn't reach their ends.
All inputs are finite; a program needn't handle non-finite values.
Results may differ from the reference program's by a relative error of at most 0.00014.
Values sent between devices are 32-bit elements; how exact they have to be, the bound alone decides.
A program may use at most 128 MiB of HBM per device.

```python
import math
import jax
import jax.numpy as jnp
from jax import lax

NX = 1024
NY = 1024
NP = 16
ITERS = 2
GRAINS = 32
PHASES = 8
SETS = 4
LAYERS = 4


def draw_order_field(key, part):
    jitter_key = jax.random.fold_in(jax.random.fold_in(key, 11), 0)
    jitter = jax.random.uniform(jitter_key, (LAYERS, NP, NX, NY), jnp.float32)
    return jitter


def plant(values, key, smallest, largest):
    index_at = [jax.random.randint(jax.random.fold_in(key, axis), (), 0, length) for axis, length in enumerate(values.shape)]
    longest = values.shape.index(max(values.shape))
    next_to = index_at[:longest] + [(index_at[longest] + 1) % values.shape[longest]] + index_at[longest + 1:]
    return values.at[tuple(index_at)].set(smallest).at[tuple(next_to)].set(largest)


def gaussian(key, dims, width, limit, kind=jnp.bfloat16):
    values = jax.random.normal(key, dims, jnp.float32) * width
    return jnp.minimum(jnp.maximum(values, -limit), limit).astype(kind)


def setup_inputs(seed: int = 0) -> dict:
    streams_of = jax.random.split(jax.random.key(seed), 9)
    return {
        "order_field": draw_order_field(jax.random.fold_in(streams_of[8], 71), 0),
        "grain_label": plant(jax.random.randint(streams_of[1], (LAYERS, NX, NY), 0, GRAINS), jax.random.fold_in(streams_of[1], 1), 0, GRAINS - 1).astype(jnp.int32),
        "phase_label": plant(jax.random.randint(streams_of[2], (LAYERS, NX, NY), 0, PHASES), jax.random.fold_in(streams_of[2], 1), 0, PHASES - 1).astype(jnp.int32),
        "grain_mobility": jnp.clip(jnp.exp(jax.random.uniform(streams_of[3], (GRAINS,), jnp.float32, math.log(0.25), math.log(1.0))), 0.25, 1.0),
        "stiff_index": plant(jax.random.randint(streams_of[4], (PHASES,), 0, SETS), jax.random.fold_in(streams_of[4], 1), 0, SETS - 1).astype(jnp.int32),
        "stiff_table": jnp.clip(jnp.exp(jax.random.uniform(streams_of[5], (SETS, 2), jnp.float32, math.log(0.5), math.log(2.0))), 0.5, 2.0),
        "eigen_strain": gaussian(streams_of[6], (NP, 3), 0.3, 1.5, jnp.float32),
        "macro_strain": gaussian(streams_of[7], (3,), 0.5, 2.0, jnp.float32),
    }


GAMMA_MIX = 1.5
KAPPA_GRAD = 1.0
STEP_TIME = 0.1
LAYER_COUPLE = 0.5
LAMBDA_REF = 1.25
SHEAR_REF = 1.25
BETA_REF = (LAMBDA_REF + SHEAR_REF) / (SHEAR_REF * (LAMBDA_REF + 2.0 * SHEAR_REF))
PRECISE = lax.Precision.HIGHEST

def advance(fields, mobility, pad_fields, pad_mobility, below, above, driving_term):
    extent_rows = fields.shape[2]
    extent_cols = fields.shape[3]
    diffuse = jnp.zeros_like(fields)
    for offset_rows, offset_cols in ((0, 1), (2, 1), (1, 0), (1, 2)):
        beside = pad_fields[:, :, offset_rows:offset_rows + extent_rows, offset_cols:offset_cols + extent_cols]
        mob_beside = pad_mobility[:, None, offset_rows:offset_rows + extent_rows, offset_cols:offset_cols + extent_cols]
        diffuse = diffuse + 0.5 * (mobility[:, None] + mob_beside) * (beside - fields)
    squares = fields * fields
    totals = lax.optimization_barrier(jnp.sum(squares, axis=1, keepdims=True))
    bulk_term = squares * fields - fields + 2.0 * GAMMA_MIX * fields * (totals - squares)
    layered = LAYER_COUPLE * (below + above - 2.0 * fields)
    return fields + STEP_TIME * (KAPPA_GRAD * diffuse + mobility[:, None] * (layered - bulk_term + driving_term))

def directions(freq_rows, freq_cols, extent_rows, extent_cols):
    signed_rows = jnp.where(freq_rows >= extent_rows // 2, freq_rows - extent_rows, freq_rows).astype(jnp.float32)
    signed_cols = jnp.where(freq_cols >= extent_cols // 2, freq_cols - extent_cols, freq_cols).astype(jnp.float32)
    keeper = ((freq_rows != extent_rows // 2) & (freq_cols != extent_cols // 2)).astype(jnp.float32)
    radius = signed_rows * signed_rows + signed_cols * signed_cols
    inverse = keeper * lax.rsqrt(jnp.where(radius > 0, radius, 1.0))
    return (signed_rows * inverse, signed_cols * inverse)

def green(stress_rr, stress_cc, stress_rc, unit_row, unit_col):
    push_row = stress_rr * unit_row + stress_rc * unit_col
    push_col = stress_rc * unit_row + stress_cc * unit_col
    normal_part = unit_row * push_row + unit_col * push_col
    out_rr = unit_row * push_row / SHEAR_REF - BETA_REF * unit_row * unit_row * normal_part
    out_cc = unit_col * push_col / SHEAR_REF - BETA_REF * unit_col * unit_col * normal_part
    out_rc = 0.5 * (unit_row * push_col + unit_col * push_row) / SHEAR_REF - BETA_REF * unit_row * unit_col * normal_part
    return (out_rr, out_cc, out_rc)

def stress_of(strain, eigen_field, lambda_cell, shear_cell):
    elastic = strain - eigen_field
    along_rr = (lambda_cell + 2.0 * shear_cell) * elastic[:, 0] + lambda_cell * elastic[:, 1]
    along_cc = lambda_cell * elastic[:, 0] + (lambda_cell + 2.0 * shear_cell) * elastic[:, 1]
    along_rc = 2.0 * shear_cell * elastic[:, 2]
    return jnp.stack([along_rr, along_cc, along_rc], axis=1)

def driving(stress, fields, eigen_strain):
    weighted = jnp.stack([stress[:, 0], stress[:, 1], 2.0 * stress[:, 2]], axis=1)
    project = jnp.einsum('lcxy,ic->lixy', weighted, eigen_strain, precision=PRECISE)
    return 2.0 * fields * project

def reference(order_field, grain_label, phase_label, grain_mobility, stiff_index, stiff_table, eigen_strain, macro_strain):
    mobility = grain_mobility[grain_label]
    chosen = stiff_index[phase_label]
    lambda_cell = stiff_table[chosen, 0]
    shear_cell = stiff_table[chosen, 1]

    def step_fields(fields, driving_term):
        pad_fields = jnp.pad(fields, ((0, 0), (0, 0), (1, 1), (1, 1)), mode='wrap')
        pad_mobility = jnp.pad(mobility, ((0, 0), (1, 1), (1, 1)), mode='wrap')
        stacked = jnp.pad(fields, ((1, 1), (0, 0), (0, 0), (0, 0)))
        return advance(fields, mobility, pad_fields, pad_mobility, stacked[:-2], stacked[2:], driving_term)
    middle = step_fields(order_field, 0.0)
    eigen_field = jnp.einsum('lixy,ic->lcxy', middle * middle, eigen_strain, precision=PRECISE)
    freq_rows = jnp.arange(NX, dtype=jnp.int32)[:, None]
    freq_cols = jnp.arange(NY, dtype=jnp.int32)[None, :]
    unit_row, unit_col = directions(freq_rows, freq_cols, NX, NY)
    strain = jnp.broadcast_to(macro_strain[None, :, None, None], eigen_field.shape)
    for sweep_index in range(ITERS):
        stress = stress_of(strain, eigen_field, lambda_cell, shear_cell)
        spectrum = jnp.fft.fft2(stress)
        corrected = green(spectrum[:, 0], spectrum[:, 1], spectrum[:, 2], unit_row, unit_col)
        strain = strain - jnp.real(jnp.fft.ifft2(jnp.stack(corrected, axis=1)))
    stress = stress_of(strain, eigen_field, lambda_cell, shear_cell)
    updated = step_fields(middle, driving(stress, middle, eigen_strain))
    return (updated, strain)
```

```python
import jax
import jax.numpy as jnp
import ml_dtypes
import numpy as np
from jax import lax
from jax.experimental import pallas as pl
from jax.experimental.pallas import tpu as pltpu
from jax.sharding import PartitionSpec as P

MESH = pl.DeviceIdType.MESH
ITERS = 2
ROWS = 32
HALF = 0.7071067811865476
LAMBDA_REF = 1.25
SHEAR_REF = 1.25
BETA_REF = (LAMBDA_REF + SHEAR_REF) / (SHEAR_REF * (LAMBDA_REF + 2.0 * SHEAR_REF))
F32 = jnp.float32
BF16 = jnp.bfloat16
CHUNK = 4
CHUNKS = 16 // CHUNK


def split_table(values):
    high = values.astype(np.float32).astype(ml_dtypes.bfloat16)
    low = (values - high.astype(np.float64)).astype(np.float32).astype(ml_dtypes.bfloat16)
    return high, low


def tables():
    place = np.arange(128, dtype=np.float64)
    forward = np.zeros((4, 256, 256))
    inverse = np.zeros((4, 256, 256))
    scale = 1.0 / 1048576.0
    half = np.arange(64, dtype=np.float64)
    for first, base in ((0, 0), (64, 4)):
        angle = 2.0 * np.pi * np.outer(base + 8 * half, place) / 1024.0
        source = slice(0, 128) if base == 0 else slice(128, 256)
        forward[0, first : first + 64, source] = np.cos(angle)
        forward[0, 128 + first : 192 + first, source] = -np.sin(angle)
        weight = np.full((64, 1), 2.0 * scale)
        if base == 0:
            weight[0] = scale
        inverse[0, source, first : first + 64] = (weight * np.cos(angle)).T
        inverse[0, source, 128 + first : 192 + first] = (-weight * np.sin(angle)).T
    for kind in (1, 2, 3):
        angle = 2.0 * np.pi * np.outer(kind + 8 * place, place) / 1024.0
        cosine, sine = np.cos(angle), np.sin(angle)
        forward[kind] = np.block([[cosine, sine], [-sine, cosine]])
        inverse[kind] = 2.0 * scale * np.block([[cosine.T, -sine.T], [sine.T, cosine.T]])
    small = np.arange(32, dtype=np.float64)
    angle = 2.0 * np.pi * np.outer(small, small) / 32.0
    cosine, sine = np.kron(np.eye(4), np.cos(angle)), np.kron(np.eye(4), np.sin(angle))
    rows_forward = np.block([[cosine, -sine], [sine, cosine]])
    rows_inverse = np.block([[cosine, sine], [-sine, cosine]])
    angle = 2.0 * np.pi * np.outer(small, np.tile(small, 4)) / 1024.0
    turn = np.stack([np.cos(angle), np.sin(angle)], axis=1).astype(np.float32)
    return (
        split_table(forward)
        + split_table(inverse)
        + split_table(rows_forward)
        + split_table(rows_inverse)
        + (turn,)
    )


def times(value, angle_index, length, sign):
    real, imag = value
    angle_index = angle_index % length
    if angle_index == 0:
        return value
    angle = 2.0 * np.pi * angle_index / length
    cosine, sine = float(np.cos(angle)), float(sign * np.sin(angle))
    if 4 * angle_index == length or 4 * angle_index == 3 * length:
        return (-imag, real) if sine > 0 else (imag, -real)
    if 2 * angle_index == length:
        return (-real, -imag)
    return (real * cosine - imag * sine, imag * cosine + real * sine)


def plus(first, second):
    return (first[0] + second[0], first[1] + second[1])


def minus(first, second):
    return (first[0] - second[0], first[1] - second[1])


def four(x, sign):
    a, b, c, d = plus(x[0], x[2]), minus(x[0], x[2]), plus(x[1], x[3]), minus(x[1], x[3])
    d = (-d[1], d[0]) if sign > 0 else (d[1], -d[0])
    return [plus(a, c), plus(b, d), minus(a, c), minus(b, d)]


def eight(x, sign):
    even, odd = four(x[0::2], sign), four(x[1::2], sign)
    odd = [odd[0], times(odd[1], 1, 8, sign), times(odd[2], 2, 8, sign), times(odd[3], 3, 8, sign)]
    return [plus(e, o) for e, o in zip(even, odd)] + [minus(e, o) for e, o in zip(even, odd)]


def parts(value):
    high = value.astype(BF16)
    return high, (value - high.astype(F32)).astype(BF16)


def dot(a, b):
    return jnp.dot(a, b, preferred_element_type=F32)


def dot3(a_high, a_low, b_high, b_low):
    return dot(a_high, b_high) + dot(a_high, b_low) + dot(a_low, b_high)


def kernel(
    order_hbm, grain_hbm, phase_hbm, tfh_hbm, tfl_hbm, tih_hbm, til_hbm, bfh_hbm, bfl_hbm, bih_hbm,
    bil_hbm, turn_hbm, mob_s, index_s, stiff_s, eigen_s, macro_s,
    out_ref, strain_ref,
    first, middle, mob, grain, phase, tfh, tfl, tih, til, bfh, bfl, bih, bil, turn,
    row_out, row_in, row_out2, row_in2, col_out, col_in, col_out2, col_in2,
    outer_in, outer_in2, lame, lame_in, eig, eig_in, final,
    strain, eig_t, m1_t, m2_t, green, send1, recv1, send2, recv2, work, high, low, flat, lxh, lxl,
    load_sem, halo_send, halo_recv, outer_send, outer_recv, core_send, core_recv, all_send, all_recv,
):
    g, r, c = lax.axis_index("grp"), lax.axis_index("row"), lax.axis_index("col")
    inner, outer = g, 1 - g
    mine = jnp.where(c == 0, inner, outer)
    other = 1 - mine
    core_peer = (g, r, 1 - c)
    grp_peer = (1 - g, r, c)
    row_up = (g, (r + ROWS - 1) % ROWS, c)
    row_down = (g, (r + 1) % ROWS, c)

    def remote(source, target, send, recv, device):
        return pltpu.make_async_remote_copy(
            source, target, send, recv, device_id=device, device_id_type=MESH
        )

    loads = [
        pltpu.make_async_copy(grain_hbm, grain, load_sem.at[0]),
        pltpu.make_async_copy(phase_hbm, phase, load_sem.at[1]),
        pltpu.make_async_copy(order_hbm, first.at[:, :, pl.ds(8, 32), :], load_sem.at[2]),
    ]
    pairs = (
        (tfh_hbm, tfh), (tfl_hbm, tfl), (tih_hbm, tih), (til_hbm, til), (bfh_hbm, bfh),
        (bfl_hbm, bfl), (bih_hbm, bih), (bil_hbm, bil), (turn_hbm, turn),
    )
    for place, (source, target) in enumerate(pairs):
        loads.append(pltpu.make_async_copy(source, target, load_sem.at[3 + place]))
    for load in loads:
        load.start()

    barrier = pltpu.get_barrier_semaphore()
    pl.semaphore_signal(barrier, inc=1, device_id=grp_peer, device_id_type=MESH)
    pl.semaphore_signal(barrier, inc=1, device_id=core_peer, device_id_type=MESH)

    def greet(step, carry):
        pl.semaphore_signal(
            barrier, inc=1, device_id=(g, (r + step) % ROWS, c), device_id_type=MESH
        )
        return carry

    lax.fori_loop(1, ROWS, greet, 0)

    loads[0].wait()
    loads[1].wait()
    for layer in range(2):
        labels = grain[layer]

        def look(k, value):
            return jnp.where(labels == k, mob_s[k], value)

        mob[layer, 8:40, :] = lax.fori_loop(0, 32, look, jnp.zeros((32, 512), F32))
        labels2 = phase[layer]

        def look2(k, values):
            chosen = index_s[k]
            hit = labels2 == k
            return (
                jnp.where(hit, stiff_s[chosen, 0], values[0]),
                jnp.where(hit, stiff_s[chosen, 1], values[1]),
            )

        empty = jnp.zeros((32, 512), F32)
        lam, shear = lax.fori_loop(0, 8, look2, (empty, empty))
        lame[layer, 0] = lam
        lame[layer, 1] = shear

    lane = lax.broadcasted_iota(jnp.int32, (32, 128), 1)

    def pack(source, rows_to, cols_to):
        def step(i, carry):
            for layer in range(2):
                k = layer * 16 + i
                rows_to[0, k] = source[layer, i, 8:9, :]
                rows_to[1, k] = source[layer, i, 39:40, :]
                cols_to[k] = jnp.where(
                    lane < 64, source[layer, i, 8:40, 0:128], source[layer, i, 8:40, 384:512]
                )
            return carry

        lax.fori_loop(0, 16, step, 0)

    def unpack(target, rows_from):
        def step(i, carry):
            for layer in range(2):
                k = layer * 16 + i
                target[layer, i, 40:41, :] = rows_from[0, k]
                target[layer, i, 7:8, :] = rows_from[1, k]
            return carry

        lax.fori_loop(0, 16, step, 0)

    loads[2].wait()
    pack(first, row_out, col_out)
    for layer in range(2):
        row_out[0, 32 + layer] = mob[layer, 8:9, :]
        row_out[1, 32 + layer] = mob[layer, 39:40, :]
        col_out[32 + layer] = jnp.where(lane < 64, mob[layer, 8:40, 0:128], mob[layer, 8:40, 384:512])

    pl.semaphore_wait(barrier, ROWS + 1)

    halo = [
        remote(row_out.at[0], row_in.at[0], halo_send.at[0], halo_recv.at[0], row_up),
        remote(row_out.at[1], row_in.at[1], halo_send.at[1], halo_recv.at[1], row_down),
        remote(col_out, col_in, halo_send.at[2], halo_recv.at[2], core_peer),
    ]
    for copy in halo:
        copy.start()

    def outer_copy(k):
        at = pl.ds(k * CHUNK, CHUNK)
        return remote(
            order_hbm.at[outer, at], outer_in.at[at], outer_send.at[k], outer_recv.at[k], grp_peer
        )

    def outer_copy2(k):
        at = pl.ds(k * CHUNK, CHUNK)
        return remote(
            middle.at[outer, at, pl.ds(8, 32), :], outer_in2.at[at],
            outer_send.at[CHUNKS + k], outer_recv.at[CHUNKS + k], grp_peer,
        )

    for k in range(CHUNKS):
        outer_copy(k).start()
    lame_copy = remote(lame.at[other], lame_in.at[c], core_send.at[0], core_recv.at[0], core_peer)
    lame_copy.start()

    sub16 = lax.broadcasted_iota(jnp.int32, (16, 128), 0)
    lane16 = lax.broadcasted_iota(jnp.int32, (16, 128), 1)
    slot = lane16 // 32
    place = (r % 8) * 16 + sub16
    kind = r // 8
    col_freq = jnp.where(
        kind > 0, kind + 8 * place, jnp.where(place < 64, 8 * place, 4 + 8 * (place - 64))
    )
    col_signed = jnp.where(col_freq >= 512, col_freq - 1024, col_freq).astype(F32)

    def green_step(k1, carry):
        row_freq = k1 + 32 * (lane16 % 32)
        row_signed = jnp.where(row_freq >= 512, row_freq - 1024, row_freq).astype(F32)
        keeper = jnp.where((row_freq != 512) & (col_freq != 512), 1.0, 0.0)
        radius = row_signed * row_signed + col_signed * col_signed
        inverse = keeper * lax.rsqrt(jnp.where(radius > 0, radius, 1.0))
        n1, n2 = row_signed * inverse, col_signed * inverse
        a, b, d = n1 * n1, n2 * n2, n1 * n2
        own = jnp.where(
            slot == 0,
            a / SHEAR_REF - BETA_REF * a * a,
            jnp.where(
                slot == 2,
                b / SHEAR_REF - BETA_REF * b * b,
                0.5 * (a + b) / SHEAR_REF - 2.0 * BETA_REF * d * d,
            ),
        )
        toward_rr = 0.5 * d / SHEAR_REF - BETA_REF * a * d
        toward_cc = 0.5 * d / SHEAR_REF - BETA_REF * b * d
        across = -BETA_REF * d * d
        green[0, k1] = own
        green[1, k1] = jnp.where(
            slot == 1, toward_cc, jnp.where(slot == 3, toward_rr, across)
        )
        green[2, k1] = jnp.where(
            slot == 0,
            2.0 * toward_rr,
            jnp.where(slot == 1, toward_rr, jnp.where(slot == 2, 2.0 * toward_cc, toward_cc)),
        )
        return carry

    lax.fori_loop(0, 32, green_step, 0)

    def to_columns(target, half, slots):
        for j in range(4):
            block = jnp.concatenate([field[:, 128 * j : 128 * j + 128] for field in slots], axis=0)
            target[4 * half + j] = block.T

    def stiff_columns(half, lam, shear):
        double = 2.0 * shear
        straight = lam + double
        to_columns(m1_t, half, (straight, double, straight, double))
        empty = jnp.zeros_like(lam)
        to_columns(m2_t, half, (lam, empty, lam, empty))

    stiff_columns(c, lame[mine, 0], lame[mine, 1])

    for copy in halo:
        copy.wait_recv()
    unpack(first, row_in)
    for layer in range(2):
        mob[layer, 40:41, :] = row_in[0, 32 + layer]
        mob[layer, 7:8, :] = row_in[1, 32 + layer]

    def update(source, cols, layer, beyond, stress, write):
        for s in range(4):
            r0, r1 = 8 + 8 * s, 8 * s
            m = mob[layer, r0 : r0 + 8, :]
            edge = jnp.concatenate([col_in[32 + layer, r1 : r1 + 8, :], m], axis=1)
            w_up = 0.05 * (m + mob[layer, r0 - 1 : r0 + 7, :])
            w_down = 0.05 * (m + mob[layer, r0 + 1 : r0 + 9, :])
            w_left = 0.05 * (m + pltpu.roll(edge, 1, 1)[:, 128:])
            w_right = 0.05 * (m + pltpu.roll(edge, 639, 1)[:, 128:])

            def square(i, total):
                v = source[layer, i, r0 : r0 + 8, :]
                return total + v * v

            total = lax.fori_loop(0, 16, square, jnp.zeros((8, 512), F32))
            c0 = 1.0 - (w_up + w_down + w_left + w_right) - 0.3 * m * total
            c1 = 0.2 * m
            m05 = 0.05 * m
            push = None if stress is None else [c1 * p for p in stress(s)]

            def step(i, carry):
                v = source[layer, i, r0 : r0 + 8, :]
                e = jnp.concatenate([cols[layer * 16 + i, r1 : r1 + 8, :], v], axis=1)
                left = pltpu.roll(e, 1, 1)[:, 128:]
                right = pltpu.roll(e, 639, 1)[:, 128:]
                near = source[1 - layer, i, r0 : r0 + 8, :]
                if beyond is not None:
                    near = near + beyond[i, r1 : r1 + 8, :]
                factor = c0 + c1 * v * v
                if push is not None:
                    factor = factor + (
                        push[0] * eigen_s[i, 0] + push[1] * eigen_s[i, 1] + push[2] * eigen_s[i, 2]
                    )
                value = (
                    v * factor
                    + w_up * source[layer, i, r0 - 1 : r0 + 7, :]
                    + w_down * source[layer, i, r0 + 1 : r0 + 9, :]
                    + w_left * left
                    + w_right * right
                    + m05 * near
                )
                write(layer, i, s, value)
                return carry

            lax.fori_loop(0, 16, step, 0)

    def to_middle(layer, i, s, value):
        middle[layer, i, 8 + 8 * s : 16 + 8 * s, :] = value

    update(first, col_in, outer, None, None, to_middle)
    update(first, col_in, inner, None, None, to_middle)

    lame_copy.wait_recv()
    stiff_columns(1 - c, lame_in[1 - c, 0], lame_in[1 - c, 1])

    for k in range(CHUNKS):
        outer_copy(k).wait_recv()

        def add(i, carry):
            j = k * CHUNK + i
            middle[outer, j, 8:40, :] += 0.05 * mob[outer, 8:40, :] * outer_in[j]
            return carry

        lax.fori_loop(0, CHUNK, add, 0)
        outer_copy2(k).start()

    def eigen(layer):
        for s in range(4):
            rows = slice(8 + 8 * s, 16 + 8 * s)

            def step(i, totals):
                v = middle[layer, i, rows, :]
                v = v * v
                return tuple(totals[k] + v * eigen_s[i, k] for k in range(3))

            empty = jnp.zeros((8, 512), F32)
            totals = lax.fori_loop(0, 16, step, (empty, empty, empty))
            for k in range(3):
                eig[layer, k, 8 * s : 8 * s + 8, :] = totals[k]

    eigen(other)
    eig_copy = remote(eig.at[other], eig_in.at[c], core_send.at[1], core_recv.at[1], core_peer)
    eig_copy.start()
    eigen(mine)
    to_columns(eig_t, c, (eig[mine, 0], eig[mine, 2], eig[mine, 1], eig[mine, 2]))

    pack(middle, row_out2, col_out2)
    halo2 = [
        remote(row_out2.at[0], row_in2.at[0], halo_send.at[3], halo_recv.at[3], row_up),
        remote(row_out2.at[1], row_in2.at[1], halo_send.at[4], halo_recv.at[4], row_down),
        remote(col_out2, col_in2, halo_send.at[5], halo_recv.at[5], core_peer),
    ]
    for copy in halo2:
        copy.start()

    eig_copy.wait_recv()
    far = [eig_in[1 - c, k] for k in range(3)]
    to_columns(eig_t, 1 - c, (far[0], far[2], far[1], far[2]))

    lane1 = lax.broadcasted_iota(jnp.int32, (128, 128), 1)
    start = jnp.where(
        lane1 < 32, macro_s[0], jnp.where((lane1 >= 64) & (lane1 < 96), macro_s[1], macro_s[2])
    )
    for n1 in range(8):
        strain[n1] = start
    for load in loads[3:]:
        load.wait()

    even16 = (lane16 // 32) % 2 == 0
    lane_all = lax.broadcasted_iota(jnp.int32, (128, 128), 1)
    even = (lane_all // 32) % 2 == 0

    def sweep(it, carry):
        def stage(t, carry):
            rows = pl.ds(pl.multiple_of(t * 16, 16), 16)
            x = []
            for n1 in range(8):
                d = strain[n1, rows, :] - eig_t[n1, rows, :]
                x.append(m1_t[n1, rows, :] * d + m2_t[n1, rows, :] * pltpu.roll(d, 64, 1))
            s04, d04, s26, d26 = x[0] + x[4], x[0] - x[4], x[2] + x[6], x[2] - x[6]
            s15, d15, s37, d37 = x[1] + x[5], x[1] - x[5], x[3] + x[7], x[3] - x[7]
            evens, odds = s04 + s26, s15 + s37
            turned = HALF * (d15 - d37)
            summed = HALF * (d15 + d37)
            values = (
                (evens + odds, evens - odds),
                (d04 + turned, -d26 - summed),
                (s04 - s26, s37 - s15),
                (d04 - turned, d26 - summed),
            )
            rows2 = pl.ds(pl.multiple_of(128 + t * 16, 16), 16)
            for kind, (real, imag) in enumerate(values):
                high[kind, rows, :], low[kind, rows, :] = parts(real)
                high[kind, rows2, :], low[kind, rows2, :] = parts(imag)
            return carry

        lax.fori_loop(0, 8, stage, 0)

        def forward(kk, carry):
            kind = (r // 8 + kk) % 4
            result = dot3(tfh[kind], tfl[kind], high[kind], low[kind])
            send1[it, pl.ds(8 * kind, 8), 0] = result[0:128].reshape(8, 16, 128)
            send1[it, pl.ds(8 * kind, 8), 1] = result[128:256].reshape(8, 16, 128)

            def post(j, carry):
                peer = 8 * kind + (r % 8 + j) % 8

                @pl.when(peer != r)
                def _():
                    remote(
                        send1.at[it, peer], recv1.at[it, r],
                        all_send.at[2 * it], all_recv.at[2 * it], (g, peer, c),
                    ).start()

                return carry

            lax.fori_loop(0, 8, post, 0)
            return carry

        lax.fori_loop(0, 4, forward, 0)
        pltpu.make_async_copy(send1.at[it, r], recv1.at[it, r], all_recv.at[2 * it]).start()
        pltpu.make_async_copy(recv1.at[it], recv1.at[it], all_recv.at[2 * it]).wait()

        for b in range(8):
            x = [(recv1[it, 8 * a + b, 0], recv1[it, 8 * a + b, 1]) for a in range(4)]
            y = four(x, -1)
            for ka in range(4):
                work[ka, b, 0], work[ka, b, 1] = times(y[ka], b * ka, 32, -1)
        for ka in range(4):
            y = eight([(work[ka, b, 0], work[ka, b, 1]) for b in range(8)], -1)
            for kb in range(8):
                k1 = ka + 4 * kb
                cosine, sine = turn[k1, 0:1, :], turn[k1, 1:2, :]
                real, imag = y[kb]
                z = (real * cosine + imag * sine, imag * cosine - real * sine)
                for half in range(2):
                    at = (slice(16 * k1, 16 * k1 + 16), slice(128 * half, 128 * half + 128))
                    lxh[at], lxl[at] = parts(z[half])

        def middle_stage(q, carry):
            rows = pl.ds(pl.multiple_of(q * 128, 128), 128)
            spectrum = dot3(lxh[rows, :], lxl[rows, :], bfh[...], bfl[...])
            group = pl.ds(8 * q, 8)
            g0 = green[0, group].reshape(128, 128)
            g1 = green[1, group].reshape(128, 128)
            g2 = green[2, group].reshape(128, 128)
            pieces = []
            for half in range(2):
                s = spectrum[:, 128 * half : 128 * half + 128]
                z = jnp.where(even, pltpu.roll(s, 64, 1), pltpu.roll(s, 96, 1))
                pieces.append(parts(g0 * s + g1 * z + g2 * pltpu.roll(s, 32, 1)))
            oh = jnp.concatenate([pieces[0][0], pieces[1][0]], axis=1)
            ol = jnp.concatenate([pieces[0][1], pieces[1][1]], axis=1)
            back = dot3(oh, ol, bih[...], bil[...])
            for j in range(8):
                k1 = 8 * q + j
                cosine, sine = turn[k1, 0:1, :], turn[k1, 1:2, :]
                real, imag = back[16 * j : 16 * j + 16, 0:128], back[16 * j : 16 * j + 16, 128:256]
                flat[k1, 0] = real * cosine - imag * sine
                flat[k1, 1] = imag * cosine + real * sine
            return carry

        lax.fori_loop(0, 4, middle_stage, 0)

        for ka in range(4):
            y = eight([(flat[ka + 4 * kb, 0], flat[ka + 4 * kb, 1]) for kb in range(8)], 1)
            for b in range(8):
                work[ka, b, 0], work[ka, b, 1] = times(y[b], b * ka, 32, 1)

        def backward(bb, carry):
            b = (r + bb) % 8
            y = four([(work[ka, b, 0], work[ka, b, 1]) for ka in range(4)], 1)
            for a in range(4):
                send2[it, 8 * a + b, 0], send2[it, 8 * a + b, 1] = y[a]

            def post(j, carry):
                peer = 8 * ((r // 8 + j) % 4) + b

                @pl.when(peer != r)
                def _():
                    remote(
                        send2.at[it, peer], recv2.at[it, r],
                        all_send.at[2 * it + 1], all_recv.at[2 * it + 1], (g, peer, c),
                    ).start()

                return carry

            lax.fori_loop(0, 4, post, 0)
            return carry

        lax.fori_loop(0, 8, backward, 0)
        pltpu.make_async_copy(send2.at[it, r], recv2.at[it, r], all_recv.at[2 * it + 1]).start()
        pltpu.make_async_copy(recv2.at[it], recv2.at[it], all_recv.at[2 * it + 1]).wait()

        def inverse(kind, carry):
            group = pl.ds(8 * kind, 8)
            real = parts(recv2[it, group, 0].reshape(128, 128))
            imag = parts(recv2[it, group, 1].reshape(128, 128))
            high[kind, 0:128], low[kind, 0:128] = real
            high[kind, 128:256], low[kind, 128:256] = imag
            result = dot3(tih[kind], til[kind], high[kind], low[kind])
            flat[pl.ds(8 * kind, 8), 0] = result[0:128].reshape(8, 16, 128)
            flat[pl.ds(8 * kind, 8), 1] = result[128:256].reshape(8, 16, 128)
            return carry

        lax.fori_loop(0, 4, inverse, 0)

        def unstage(t, carry):
            rows = pl.ds(pl.multiple_of(t * 16, 16), 16)
            z0, z4 = flat[t, 0], flat[t, 1]
            a1, b1 = flat[8 + t, 0], flat[8 + t, 1]
            a2, b2 = flat[16 + t, 0], flat[16 + t, 1]
            a3, b3 = flat[24 + t, 0], flat[24 + t, 1]
            zp, zm = z0 + z4, z0 - z4
            sa, db, da, sb = a1 + a3, b3 - b1, a1 - a3, b1 + b3
            p1, p2 = HALF * (da - sb), HALF * (da + sb)
            values = (
                zp + a2 + sa,
                zm - b2 + p1,
                zp - a2 + db,
                zm + b2 - p2,
                zp + a2 - sa,
                zm - b2 - p1,
                zp - a2 - db,
                zm + b2 + p2,
            )
            for n1 in range(8):
                strain[n1, rows, :] -= values[n1]
            return carry

        lax.fori_loop(0, 8, unstage, 0)
        return carry

    lax.fori_loop(0, ITERS, sweep, 0)

    def to_rows(half, layer, target):
        for j in range(4):
            block = strain[4 * half + j].T
            lanes = slice(128 * j, 128 * j + 128)
            target[layer, 0, :, lanes] = block[0:32]
            target[layer, 1, :, lanes] = block[64:96]
            target[layer, 2, :, lanes] = block[32:64]

    to_rows(1 - c, 0, eig_in)
    final_copy = remote(eig_in.at[0], final.at[mine], core_send.at[2], core_recv.at[2], core_peer)
    final_copy.start()
    to_rows(c, mine, final)
    for copy in halo2:
        copy.wait_recv()
    unpack(middle, row_in2)
    remote(eig_in.at[0], final.at[other], core_send.at[2], core_recv.at[2], core_peer).wait_recv()
    strain_ref[...] = final[...]

    def stress_of(layer):
        def at(s):
            rows = slice(8 * s, 8 * s + 8)
            d = [final[layer, k, rows, :] - eig[layer, k, rows, :] for k in range(3)]
            lam, double = lame[layer, 0, rows, :], 2.0 * lame[layer, 1, rows, :]
            return (
                (lam + double) * d[0] + lam * d[1],
                lam * d[0] + (lam + double) * d[1],
                2.0 * (double * d[2]),
            )

        return at

    def to_out(layer, i, s, value):
        out_ref[layer, i, 8 * s : 8 * s + 8, :] = value

    update(middle, col_in2, inner, None, stress_of(inner), to_out)
    for k in range(CHUNKS):
        outer_copy2(k).wait_recv()
    update(middle, col_in2, outer, outer_in2, stress_of(outer), to_out)

    for copy in halo + halo2 + [lame_copy, eig_copy, final_copy]:
        copy.wait_send()
    for k in range(CHUNKS):
        outer_copy(k).wait_send()
        outer_copy2(k).wait_send()
    for it in range(ITERS):
        for sent, sem in ((send1, 2 * it), (send2, 2 * it + 1)):
            whole = sent.at[it, pl.ds(0, ROWS - 1)]
            pltpu.make_async_copy(whole, whole, all_send.at[sem]).wait()


def body(order, grain, phase, mobility, index, stiff, eigen, macro):
    constants = tables()
    any_spec = pl.BlockSpec(memory_space=pl.ANY)
    smem = pl.BlockSpec(memory_space=pltpu.SMEM)
    vmem = pl.BlockSpec(memory_space=pltpu.VMEM)
    big = (2, 16, 48, 512)
    every = (ITERS, ROWS, 2, 16, 128)
    columns = (8, 128, 128)
    return pl.pallas_call(
        kernel,
        out_shape=(
            jax.ShapeDtypeStruct((2, 16, 32, 512), F32),
            jax.ShapeDtypeStruct((2, 3, 32, 512), F32),
        ),
        in_specs=[any_spec] * 12 + [smem] * 5,
        out_specs=(vmem, vmem),
        scratch_shapes=[
            pltpu.VMEM(big, F32),
            pltpu.VMEM(big, F32),
            pltpu.VMEM((2, 48, 512), F32),
            pltpu.VMEM((2, 32, 512), jnp.int32),
            pltpu.VMEM((2, 32, 512), jnp.int32),
        ]
        + [pltpu.VMEM((4, 256, 256), BF16)] * 4
        + [pltpu.VMEM((256, 256), BF16)] * 4
        + [pltpu.VMEM((32, 2, 128), F32)]
        + [
            pltpu.VMEM((2, 34, 1, 512), F32),
            pltpu.VMEM((2, 34, 1, 512), F32),
            pltpu.VMEM((2, 32, 1, 512), F32),
            pltpu.VMEM((2, 32, 1, 512), F32),
            pltpu.VMEM((34, 32, 128), F32),
            pltpu.VMEM((34, 32, 128), F32),
            pltpu.VMEM((32, 32, 128), F32),
            pltpu.VMEM((32, 32, 128), F32),
            pltpu.VMEM((16, 32, 512), F32),
            pltpu.VMEM((16, 32, 512), F32),
            pltpu.VMEM((2, 2, 32, 512), F32),
            pltpu.VMEM((2, 2, 32, 512), F32),
            pltpu.VMEM((2, 3, 32, 512), F32),
            pltpu.VMEM((2, 3, 32, 512), F32),
            pltpu.VMEM((2, 3, 32, 512), F32),
        ]
        + [pltpu.VMEM(columns, F32)] * 4
        + [pltpu.VMEM((3, 32, 16, 128), F32)]
        + [pltpu.VMEM(every, F32)] * 4
        + [pltpu.VMEM((4, 8, 2, 16, 128), F32)]
        + [pltpu.VMEM((4, 256, 128), BF16)] * 2
        + [pltpu.VMEM((32, 2, 16, 128), F32)]
        + [pltpu.VMEM((512, 256), BF16)] * 2
        + [pltpu.SemaphoreType.DMA((n,)) for n in (12, 6, 6, 2 * CHUNKS, 2 * CHUNKS, 3, 3, 2 * ITERS, 2 * ITERS)],
        compiler_params=pltpu.CompilerParams(
            collective_id=0, has_side_effects=True, vmem_limit_bytes=56 * 1024 * 1024
        ),
        name="step",
    )(order, grain, phase, *[jnp.asarray(t) for t in constants], mobility, index, stiff, eigen, macro)


def solution(mesh):
    fields = P("grp", None, "row", "col")
    labels = P("grp", "row", "col")
    return jax.shard_map(
        body,
        mesh=mesh,
        in_specs=(fields, labels, labels, P(), P(), P(), P(), P()),
        out_specs=(fields, fields),
        check_vma=False,
    )
```

```python
import jax
import jax.numpy as jnp
import ml_dtypes
import numpy as np
from jax import lax
from jax.experimental import pallas as pl
from jax.experimental.pallas import tpu as pltpu
from jax.sharding import PartitionSpec as P

MESH = pl.DeviceIdType.MESH
ITERS = 2
ROWS = 32
HALF = 0.7071067811865476
LAMBDA_REF = 1.25
SHEAR_REF = 1.25
BETA_REF = (LAMBDA_REF + SHEAR_REF) / (SHEAR_REF * (LAMBDA_REF + 2.0 * SHEAR_REF))
F32 = jnp.float32
BF16 = jnp.bfloat16
CHUNK = 4
CHUNKS = 16 // CHUNK
UNROLL = 4


def split_table(values):
    high = values.astype(np.float32).astype(ml_dtypes.bfloat16)
    low = (values - high.astype(np.float64)).astype(np.float32).astype(ml_dtypes.bfloat16)
    return high, low


def tables():
    place = np.arange(128, dtype=np.float64)
    forward = np.zeros((4, 256, 256))
    inverse = np.zeros((4, 256, 256))
    scale = 1.0 / 1048576.0
    half = np.arange(64, dtype=np.float64)
    for first, base in ((0, 0), (64, 4)):
        angle = 2.0 * np.pi * np.outer(base + 8 * half, place) / 1024.0
        source = slice(0, 128) if base == 0 else slice(128, 256)
        forward[0, first : first + 64, source] = np.cos(angle)
        forward[0, 128 + first : 192 + first, source] = -np.sin(angle)
        weight = np.full((64, 1), 2.0 * scale)
        if base == 0:
            weight[0] = scale
        inverse[0, source, first : first + 64] = (weight * np.cos(angle)).T
        inverse[0, source, 128 + first : 192 + first] = (-weight * np.sin(angle)).T
    for kind in (1, 2, 3):
        angle = 2.0 * np.pi * np.outer(kind + 8 * place, place) / 1024.0
        cosine, sine = np.cos(angle), np.sin(angle)
        forward[kind] = np.block([[cosine, sine], [-sine, cosine]])
        inverse[kind] = 2.0 * scale * np.block([[cosine.T, -sine.T], [sine.T, cosine.T]])
    small = np.arange(32, dtype=np.float64)
    angle = 2.0 * np.pi * np.outer(small, small) / 32.0
    cosine, sine = np.kron(np.eye(4), np.cos(angle)), np.kron(np.eye(4), np.sin(angle))
    rows_forward = np.block([[cosine, -sine], [sine, cosine]])
    rows_inverse = np.block([[cosine, sine], [-sine, cosine]])
    angle = 2.0 * np.pi * np.outer(small, np.tile(small, 4)) / 1024.0
    turn = np.stack([np.cos(angle), np.sin(angle)], axis=1).astype(np.float32)
    return (
        split_table(forward)
        + split_table(inverse)
        + split_table(rows_forward)
        + split_table(rows_inverse)
        + (turn,)
    )


def times(value, angle_index, length, sign):
    real, imag = value
    angle_index = angle_index % length
    if angle_index == 0:
        return value
    angle = 2.0 * np.pi * angle_index / length
    cosine, sine = float(np.cos(angle)), float(sign * np.sin(angle))
    if 4 * angle_index == length or 4 * angle_index == 3 * length:
        return (-imag, real) if sine > 0 else (imag, -real)
    if 2 * angle_index == length:
        return (-real, -imag)
    return (real * cosine - imag * sine, imag * cosine + real * sine)


def plus(first, second):
    return (first[0] + second[0], first[1] + second[1])


def minus(first, second):
    return (first[0] - second[0], first[1] - second[1])


def four(x, sign):
    a, b, c, d = plus(x[0], x[2]), minus(x[0], x[2]), plus(x[1], x[3]), minus(x[1], x[3])
    d = (-d[1], d[0]) if sign > 0 else (d[1], -d[0])
    return [plus(a, c), plus(b, d), minus(a, c), minus(b, d)]


def eight(x, sign):
    even, odd = four(x[0::2], sign), four(x[1::2], sign)
    odd = [odd[0], times(odd[1], 1, 8, sign), times(odd[2], 2, 8, sign), times(odd[3], 3, 8, sign)]
    return [plus(e, o) for e, o in zip(even, odd)] + [minus(e, o) for e, o in zip(even, odd)]


def parts(value):
    high = value.astype(BF16)
    return high, (value - high.astype(F32)).astype(BF16)


def dot(a, b):
    return jnp.dot(a, b, preferred_element_type=F32)


def dot3(a_high, a_low, b_high, b_low):
    return dot(a_high, b_high) + dot(a_high, b_low) + dot(a_low, b_high)


def kernel(
    order_hbm, grain_hbm, phase_hbm, tfh_hbm, tfl_hbm, tih_hbm, til_hbm, bfh_hbm, bfl_hbm, bih_hbm,
    bil_hbm, turn_hbm, mob_s, index_s, stiff_s, eigen_s, macro_s,
    out_ref, strain_ref,
    first, middle, mob, grain, phase, tfh, tfl, tih, til, bfh, bfl, bih, bil, turn,
    row_out, row_in, row_out2, row_in2, col_out, col_in, col_out2, col_in2,
    base, outer_in, outer_in2, lame, lame_in, eig, eig_in, final,
    strain, eig_t, m1_t, m2_t, green, send1, recv1, send2, recv2, work, high, low, flat, lxh, lxl,
    load_sem, halo_send, halo_recv, outer_send, outer_recv, core_send, core_recv, all_send, all_recv,
):
    g, r, c = lax.axis_index("grp"), lax.axis_index("row"), lax.axis_index("col")
    inner, outer = g, 1 - g
    mine = jnp.where(c == 0, inner, outer)
    other = 1 - mine
    core_peer = (g, r, 1 - c)
    grp_peer = (1 - g, r, c)
    row_up = (g, (r + ROWS - 1) % ROWS, c)
    row_down = (g, (r + 1) % ROWS, c)

    def remote(source, target, send, recv, device):
        return pltpu.make_async_remote_copy(
            source, target, send, recv, device_id=device, device_id_type=MESH
        )

    loads = [
        pltpu.make_async_copy(grain_hbm, grain, load_sem.at[0]),
        pltpu.make_async_copy(phase_hbm, phase, load_sem.at[1]),
        pltpu.make_async_copy(order_hbm, first.at[:, :, pl.ds(8, 32), :], load_sem.at[2]),
    ]
    pairs = (
        (tfh_hbm, tfh), (tfl_hbm, tfl), (tih_hbm, tih), (til_hbm, til), (bfh_hbm, bfh),
        (bfl_hbm, bfl), (bih_hbm, bih), (bil_hbm, bil), (turn_hbm, turn),
    )
    for place, (source, target) in enumerate(pairs):
        loads.append(pltpu.make_async_copy(source, target, load_sem.at[3 + place]))
    for load in loads:
        load.start()

    barrier = pltpu.get_barrier_semaphore()
    pl.semaphore_signal(barrier, inc=1, device_id=grp_peer, device_id_type=MESH)
    pl.semaphore_signal(barrier, inc=1, device_id=core_peer, device_id_type=MESH)

    def greet(step, carry):
        pl.semaphore_signal(
            barrier, inc=1, device_id=(g, (r + step) % ROWS, c), device_id_type=MESH
        )
        return carry

    lax.fori_loop(1, ROWS, greet, 0)

    loads[0].wait()
    loads[1].wait()
    for layer in range(2):
        labels = grain[layer]

        def look(k, value):
            return jnp.where(labels == k, mob_s[k], value)

        mob[layer, 8:40, :] = lax.fori_loop(0, 32, look, jnp.zeros((32, 512), F32))
        labels2 = phase[layer]

        def look2(k, values):
            chosen = index_s[k]
            hit = labels2 == k
            return (
                jnp.where(hit, stiff_s[0, chosen], values[0]),
                jnp.where(hit, stiff_s[1, chosen], values[1]),
            )

        empty = jnp.zeros((32, 512), F32)
        lam, shear = lax.fori_loop(0, 8, look2, (empty, empty))
        lame[layer, 0] = lam
        lame[layer, 1] = shear

    lane = lax.broadcasted_iota(jnp.int32, (32, 128), 1)

    def pack(source, rows_to, cols_to):
        def step(i, carry):
            for layer in range(2):
                k = layer * 16 + i
                rows_to[0, k] = source[layer, i, 8:9, :]
                rows_to[1, k] = source[layer, i, 39:40, :]
                cols_to[k] = jnp.where(
                    lane < 64, source[layer, i, 8:40, 0:128], source[layer, i, 8:40, 384:512]
                )
            return carry

        lax.fori_loop(0, 16, step, 0)

    def unpack(target, rows_from):
        def step(i, carry):
            for layer in range(2):
                k = layer * 16 + i
                target[layer, i, 40:41, :] = rows_from[0, k]
                target[layer, i, 7:8, :] = rows_from[1, k]
            return carry

        lax.fori_loop(0, 16, step, 0)

    loads[2].wait()
    pack(first, row_out, col_out)
    for layer in range(2):
        row_out[0, 32 + layer] = mob[layer, 8:9, :]
        row_out[1, 32 + layer] = mob[layer, 39:40, :]
        col_out[32 + layer] = jnp.where(lane < 64, mob[layer, 8:40, 0:128], mob[layer, 8:40, 384:512])

    pl.semaphore_wait(barrier, ROWS + 1)

    halo = [
        remote(row_out.at[0], row_in.at[0], halo_send.at[0], halo_recv.at[0], row_up),
        remote(row_out.at[1], row_in.at[1], halo_send.at[1], halo_recv.at[1], row_down),
        remote(col_out, col_in, halo_send.at[2], halo_recv.at[2], core_peer),
    ]
    for copy in halo:
        copy.start()

    def outer_copy(k):
        at = pl.ds(k * CHUNK, CHUNK)
        return remote(
            order_hbm.at[outer, at], outer_in.at[at], outer_send.at[k], outer_recv.at[k], grp_peer
        )

    def outer_copy2(k):
        at = pl.ds(k * CHUNK, CHUNK)
        return remote(
            middle.at[outer, at, pl.ds(8, 32), :], outer_in2.at[at],
            outer_send.at[CHUNKS + k], outer_recv.at[CHUNKS + k], grp_peer,
        )

    for k in range(CHUNKS):
        outer_copy(k).start()
    lame_copy = remote(lame.at[other], lame_in.at[c], core_send.at[0], core_recv.at[0], core_peer)
    lame_copy.start()

    sub16 = lax.broadcasted_iota(jnp.int32, (16, 128), 0)
    lane16 = lax.broadcasted_iota(jnp.int32, (16, 128), 1)
    slot = lane16 // 32
    place = (r % 8) * 16 + sub16
    kind = r // 8
    col_freq = jnp.where(
        kind > 0, kind + 8 * place, jnp.where(place < 64, 8 * place, 4 + 8 * (place - 64))
    )
    col_signed = jnp.where(col_freq >= 512, col_freq - 1024, col_freq).astype(F32)

    def green_step(k1, carry):
        row_freq = k1 + 32 * (lane16 % 32)
        row_signed = jnp.where(row_freq >= 512, row_freq - 1024, row_freq).astype(F32)
        keeper = jnp.where((row_freq != 512) & (col_freq != 512), 1.0, 0.0)
        radius = row_signed * row_signed + col_signed * col_signed
        inverse = keeper * lax.rsqrt(jnp.where(radius > 0, radius, 1.0))
        n1, n2 = row_signed * inverse, col_signed * inverse
        a, b, d = n1 * n1, n2 * n2, n1 * n2
        own = jnp.where(
            slot == 0,
            a / SHEAR_REF - BETA_REF * a * a,
            jnp.where(
                slot == 2,
                b / SHEAR_REF - BETA_REF * b * b,
                0.5 * (a + b) / SHEAR_REF - 2.0 * BETA_REF * d * d,
            ),
        )
        toward_rr = 0.5 * d / SHEAR_REF - BETA_REF * a * d
        toward_cc = 0.5 * d / SHEAR_REF - BETA_REF * b * d
        across = -BETA_REF * d * d
        green[0, k1] = own
        green[1, k1] = jnp.where(
            slot == 1, toward_cc, jnp.where(slot == 3, toward_rr, across)
        )
        green[2, k1] = jnp.where(
            slot == 0,
            2.0 * toward_rr,
            jnp.where(slot == 1, toward_rr, jnp.where(slot == 2, 2.0 * toward_cc, toward_cc)),
        )
        return carry

    lax.fori_loop(0, 32, green_step, 0)

    def to_columns(target, half, slots):
        for j in range(4):
            block = jnp.concatenate([field[:, 128 * j : 128 * j + 128] for field in slots], axis=0)
            target[4 * half + j] = block.T

    def stiff_columns(half, lam, shear):
        double = 2.0 * shear
        straight = lam + double
        to_columns(m1_t, half, (straight, double, straight, double))
        empty = jnp.zeros_like(lam)
        to_columns(m2_t, half, (lam, empty, lam, empty))

    stiff_columns(c, lame[mine, 0], lame[mine, 1])

    for copy in halo:
        copy.wait_recv()
    unpack(first, row_in)
    for layer in range(2):
        mob[layer, 40:41, :] = row_in[0, 32 + layer]
        mob[layer, 7:8, :] = row_in[1, 32 + layer]

    def update(source, cols, layer, write):
        for s in range(4):
            r0, r1 = 8 + 8 * s, 8 * s
            m = mob[layer, r0 : r0 + 8, :]
            edge = jnp.concatenate([col_in[32 + layer, r1 : r1 + 8, :], m], axis=1)
            w_up = 0.05 * (m + mob[layer, r0 - 1 : r0 + 7, :])
            w_down = 0.05 * (m + mob[layer, r0 + 1 : r0 + 9, :])
            w_left = 0.05 * (m + pltpu.roll(edge, 1, 1)[:, 128:])
            w_right = 0.05 * (m + pltpu.roll(edge, 639, 1)[:, 128:])
            total = jnp.zeros((8, 512), F32)
            for i in range(16):
                v = source[layer, i, r0 : r0 + 8, :]
                total = total + v * v
            c0 = 1.0 - (w_up + w_down + w_left + w_right) - 0.3 * m * total
            c1 = 0.2 * m
            m05 = 0.05 * m

            def step(n, carry):
                for i4 in range(UNROLL):
                    i = n * UNROLL + i4
                    v = source[layer, i, r0 : r0 + 8, :]
                    e = jnp.concatenate([cols[layer * 16 + i, r1 : r1 + 8, :], v], axis=1)
                    write(
                        layer,
                        i,
                        s,
                        v * (c0 + c1 * v * v)
                        + w_up * source[layer, i, r0 - 1 : r0 + 7, :]
                        + w_down * source[layer, i, r0 + 1 : r0 + 9, :]
                        + w_left * pltpu.roll(e, 1, 1)[:, 128:]
                        + w_right * pltpu.roll(e, 639, 1)[:, 128:]
                        + m05 * source[1 - layer, i, r0 : r0 + 8, :],
                    )
                return carry

            lax.fori_loop(0, 16 // UNROLL, step, 0)

    def to_middle(layer, i, s, value):
        middle[layer, i, 8 + 8 * s : 16 + 8 * s, :] = value

    def to_base(layer, i, s, value):
        base[layer, i, 8 * s : 8 * s + 8, :] = value

    update(first, col_in, inner, to_middle)
    for s in range(4):
        totals = [jnp.zeros((8, 512), F32)] * 3
        for i in range(16):
            v = middle[inner, i, 8 + 8 * s : 16 + 8 * s, :]
            v = v * v
            totals = [totals[k] + v * eigen_s[k, i] for k in range(3)]
        for k in range(3):
            eig[inner, k, 8 * s : 8 * s + 8, :] = totals[k]
            eig[outer, k, 8 * s : 8 * s + 8, :] = jnp.zeros((8, 512), F32)
    update(first, col_in, outer, to_middle)

    lame_copy.wait_recv()
    stiff_columns(1 - c, lame_in[1 - c, 0], lame_in[1 - c, 1])

    for k in range(CHUNKS):
        outer_copy(k).wait_recv()

        def add(s, carry):
            at, at2 = pl.ds(pl.multiple_of(8 + 8 * s, 8), 8), pl.ds(pl.multiple_of(8 * s, 8), 8)
            m05 = 0.05 * mob[outer, at, :]
            totals = [eig[outer, n, at2, :] for n in range(3)]
            for i in range(CHUNK):
                j = k * CHUNK + i
                v = middle[outer, j, at, :] + m05 * outer_in[j, at2, :]
                middle[outer, j, at, :] = v
                v = v * v
                totals = [totals[n] + v * eigen_s[n, j] for n in range(3)]
            for n in range(3):
                eig[outer, n, at2, :] = totals[n]
            return carry

        lax.fori_loop(0, 4, add, 0)

    eig_copy = remote(eig.at[other], eig_in.at[c], core_send.at[1], core_recv.at[1], core_peer)
    eig_copy.start()
    to_columns(eig_t, c, (eig[mine, 0], eig[mine, 2], eig[mine, 1], eig[mine, 2]))
    halo2 = [
        remote(row_out2.at[0], row_in2.at[0], halo_send.at[3], halo_recv.at[3], row_up),
        remote(row_out2.at[1], row_in2.at[1], halo_send.at[4], halo_recv.at[4], row_down),
        remote(col_out2, col_in2, halo_send.at[5], halo_recv.at[5], core_peer),
    ]

    eig_copy.wait_recv()
    far = [eig_in[1 - c, k] for k in range(3)]
    to_columns(eig_t, 1 - c, (far[0], far[2], far[1], far[2]))

    lane1 = lax.broadcasted_iota(jnp.int32, (128, 128), 1)
    start = jnp.where(
        lane1 < 32, macro_s[0], jnp.where((lane1 >= 64) & (lane1 < 96), macro_s[1], macro_s[2])
    )
    for n1 in range(8):
        strain[n1] = start
    for load in loads[3:]:
        load.wait()

    even16 = (lane16 // 32) % 2 == 0
    lane_all = lax.broadcasted_iota(jnp.int32, (128, 128), 1)
    even = (lane_all // 32) % 2 == 0

    def sweep(it, carry):
        def stage(t, carry):
            rows = pl.ds(pl.multiple_of(t * 16, 16), 16)
            x = []
            for n1 in range(8):
                d = strain[n1, rows, :] - eig_t[n1, rows, :]
                x.append(m1_t[n1, rows, :] * d + m2_t[n1, rows, :] * pltpu.roll(d, 64, 1))
            s04, d04, s26, d26 = x[0] + x[4], x[0] - x[4], x[2] + x[6], x[2] - x[6]
            s15, d15, s37, d37 = x[1] + x[5], x[1] - x[5], x[3] + x[7], x[3] - x[7]
            evens, odds = s04 + s26, s15 + s37
            turned = HALF * (d15 - d37)
            summed = HALF * (d15 + d37)
            values = (
                (evens + odds, evens - odds),
                (d04 + turned, -d26 - summed),
                (s04 - s26, s37 - s15),
                (d04 - turned, d26 - summed),
            )
            rows2 = pl.ds(pl.multiple_of(128 + t * 16, 16), 16)
            for kind, (real, imag) in enumerate(values):
                high[kind, rows, :], low[kind, rows, :] = parts(real)
                high[kind, rows2, :], low[kind, rows2, :] = parts(imag)
            return carry

        lax.fori_loop(0, 8, stage, 0)

        def forward(kk, carry):
            kind = (r // 8 + kk) % 4
            result = dot3(tfh[kind], tfl[kind], high[kind], low[kind])
            send1[it, pl.ds(8 * kind, 8), 0] = result[0:128].reshape(8, 16, 128)
            send1[it, pl.ds(8 * kind, 8), 1] = result[128:256].reshape(8, 16, 128)

            def post(j, carry):
                peer = 8 * kind + (r % 8 + j) % 8

                @pl.when(peer != r)
                def _():
                    remote(
                        send1.at[it, peer], recv1.at[it, r],
                        all_send.at[2 * it], all_recv.at[2 * it], (g, peer, c),
                    ).start()

                return carry

            lax.fori_loop(0, 8, post, 0)
            return carry

        lax.fori_loop(0, 4, forward, 0)
        pltpu.make_async_copy(send1.at[it, r], recv1.at[it, r], all_recv.at[2 * it]).start()
        outer_copy2(2 * it).start()

        @pl.when(it == 0)
        def _():
            pack(middle, row_out2, col_out2)
            for copy in halo2:
                copy.start()

        pltpu.make_async_copy(recv1.at[it], recv1.at[it], all_recv.at[2 * it]).wait()

        for b in range(8):
            x = [(recv1[it, 8 * a + b, 0], recv1[it, 8 * a + b, 1]) for a in range(4)]
            y = four(x, -1)
            for ka in range(4):
                work[ka, b, 0], work[ka, b, 1] = times(y[ka], b * ka, 32, -1)
        for ka in range(4):
            y = eight([(work[ka, b, 0], work[ka, b, 1]) for b in range(8)], -1)
            for kb in range(8):
                k1 = ka + 4 * kb
                cosine, sine = turn[k1, 0:1, :], turn[k1, 1:2, :]
                real, imag = y[kb]
                z = (real * cosine + imag * sine, imag * cosine - real * sine)
                for half in range(2):
                    at = (slice(16 * k1, 16 * k1 + 16), slice(128 * half, 128 * half + 128))
                    lxh[at], lxl[at] = parts(z[half])

        def middle_stage(q, carry):
            rows = pl.ds(pl.multiple_of(q * 128, 128), 128)
            spectrum = dot3(lxh[rows, :], lxl[rows, :], bfh[...], bfl[...])
            group = pl.ds(8 * q, 8)
            g0 = green[0, group].reshape(128, 128)
            g1 = green[1, group].reshape(128, 128)
            g2 = green[2, group].reshape(128, 128)
            pieces = []
            for half in range(2):
                s = spectrum[:, 128 * half : 128 * half + 128]
                z = jnp.where(even, pltpu.roll(s, 64, 1), pltpu.roll(s, 96, 1))
                pieces.append(parts(g0 * s + g1 * z + g2 * pltpu.roll(s, 32, 1)))
            oh = jnp.concatenate([pieces[0][0], pieces[1][0]], axis=1)
            ol = jnp.concatenate([pieces[0][1], pieces[1][1]], axis=1)
            back = dot3(oh, ol, bih[...], bil[...])
            for j in range(8):
                k1 = 8 * q + j
                cosine, sine = turn[k1, 0:1, :], turn[k1, 1:2, :]
                real, imag = back[16 * j : 16 * j + 16, 0:128], back[16 * j : 16 * j + 16, 128:256]
                flat[k1, 0] = real * cosine - imag * sine
                flat[k1, 1] = imag * cosine + real * sine
            return carry

        lax.fori_loop(0, 4, middle_stage, 0)

        for ka in range(4):
            y = eight([(flat[ka + 4 * kb, 0], flat[ka + 4 * kb, 1]) for kb in range(8)], 1)
            for b in range(8):
                work[ka, b, 0], work[ka, b, 1] = times(y[b], b * ka, 32, 1)

        def backward(bb, carry):
            b = (r + bb) % 8
            y = four([(work[ka, b, 0], work[ka, b, 1]) for ka in range(4)], 1)
            for a in range(4):
                send2[it, 8 * a + b, 0], send2[it, 8 * a + b, 1] = y[a]

            def post(j, carry):
                peer = 8 * ((r // 8 + j) % 4) + b

                @pl.when(peer != r)
                def _():
                    remote(
                        send2.at[it, peer], recv2.at[it, r],
                        all_send.at[2 * it + 1], all_recv.at[2 * it + 1], (g, peer, c),
                    ).start()

                return carry

            lax.fori_loop(0, 4, post, 0)
            return carry

        lax.fori_loop(0, 8, backward, 0)
        pltpu.make_async_copy(send2.at[it, r], recv2.at[it, r], all_recv.at[2 * it + 1]).start()
        outer_copy2(2 * it + 1).start()

        @pl.when(it == 0)
        def _():
            for copy in halo2:
                copy.wait_recv()
            unpack(middle, row_in2)

        update(middle, col_in2, it, to_base)
        pltpu.make_async_copy(recv2.at[it], recv2.at[it], all_recv.at[2 * it + 1]).wait()

        def inverse(kind, carry):
            group = pl.ds(8 * kind, 8)
            real = parts(recv2[it, group, 0].reshape(128, 128))
            imag = parts(recv2[it, group, 1].reshape(128, 128))
            high[kind, 0:128], low[kind, 0:128] = real
            high[kind, 128:256], low[kind, 128:256] = imag
            result = dot3(tih[kind], til[kind], high[kind], low[kind])
            flat[pl.ds(8 * kind, 8), 0] = result[0:128].reshape(8, 16, 128)
            flat[pl.ds(8 * kind, 8), 1] = result[128:256].reshape(8, 16, 128)
            return carry

        lax.fori_loop(0, 4, inverse, 0)

        def unstage(t, carry):
            rows = pl.ds(pl.multiple_of(t * 16, 16), 16)
            z0, z4 = flat[t, 0], flat[t, 1]
            a1, b1 = flat[8 + t, 0], flat[8 + t, 1]
            a2, b2 = flat[16 + t, 0], flat[16 + t, 1]
            a3, b3 = flat[24 + t, 0], flat[24 + t, 1]
            zp, zm = z0 + z4, z0 - z4
            sa, db, da, sb = a1 + a3, b3 - b1, a1 - a3, b1 + b3
            p1, p2 = HALF * (da - sb), HALF * (da + sb)
            values = (
                zp + a2 + sa,
                zm - b2 + p1,
                zp - a2 + db,
                zm + b2 - p2,
                zp + a2 - sa,
                zm - b2 - p1,
                zp - a2 - db,
                zm + b2 + p2,
            )
            for n1 in range(8):
                strain[n1, rows, :] -= values[n1]
            return carry

        lax.fori_loop(0, 8, unstage, 0)
        return carry

    lax.fori_loop(0, ITERS, sweep, 0)

    def to_rows(half, layer, target):
        for j in range(4):
            block = strain[4 * half + j].T
            lanes = slice(128 * j, 128 * j + 128)
            target[layer, 0, :, lanes] = block[0:32]
            target[layer, 1, :, lanes] = block[64:96]
            target[layer, 2, :, lanes] = block[32:64]

    to_rows(1 - c, 0, eig_in)
    final_copy = remote(eig_in.at[0], final.at[mine], core_send.at[2], core_recv.at[2], core_peer)
    final_copy.start()
    to_rows(c, mine, final)
    remote(eig_in.at[0], final.at[other], core_send.at[2], core_recv.at[2], core_peer).wait_recv()
    strain_ref[...] = final[...]

    def finish(layer, beyond):
        def at(s, carry):
            rows = pl.ds(pl.multiple_of(8 * s, 8), 8)
            d = [final[layer, k, rows, :] - eig[layer, k, rows, :] for k in range(3)]
            lam, double = lame[layer, 0, rows, :], 2.0 * lame[layer, 1, rows, :]
            m = mob[layer, pl.ds(pl.multiple_of(8 + 8 * s, 8), 8), :]
            m05, c1 = 0.05 * m, 0.2 * m
            push = (
                c1 * ((lam + double) * d[0] + lam * d[1]),
                c1 * (lam * d[0] + (lam + double) * d[1]),
                c1 * (2.0 * (double * d[2])),
            )
            for i in range(16):
                v = middle[layer, i, pl.ds(pl.multiple_of(8 + 8 * s, 8), 8), :]
                value = base[layer, i, rows, :] + v * (
                    push[0] * eigen_s[0, i] + push[1] * eigen_s[1, i] + push[2] * eigen_s[2, i]
                )
                if beyond:
                    value = value + m05 * outer_in2[i, rows, :]
                out_ref[layer, i, rows, :] = value
            return carry

        lax.fori_loop(0, 4, at, 0)

    finish(inner, False)
    for k in range(CHUNKS):
        outer_copy2(k).wait_recv()
    finish(outer, True)

    for copy in halo + halo2 + [lame_copy, eig_copy, final_copy]:
        copy.wait_send()
    for k in range(CHUNKS):
        outer_copy(k).wait_send()
        outer_copy2(k).wait_send()
    for it in range(ITERS):
        for sent, sem in ((send1, 2 * it), (send2, 2 * it + 1)):
            whole = sent.at[it, pl.ds(0, ROWS - 1)]
            pltpu.make_async_copy(whole, whole, all_send.at[sem]).wait()


def body(order, grain, phase, mobility, index, stiff, eigen, macro):
    constants = tables()
    any_spec = pl.BlockSpec(memory_space=pl.ANY)
    smem = pl.BlockSpec(memory_space=pltpu.SMEM)
    vmem = pl.BlockSpec(memory_space=pltpu.VMEM)
    big = (2, 16, 48, 512)
    every = (ITERS, ROWS, 2, 16, 128)
    columns = (8, 128, 128)
    return pl.pallas_call(
        kernel,
        out_shape=(
            jax.ShapeDtypeStruct((2, 16, 32, 512), F32),
            jax.ShapeDtypeStruct((2, 3, 32, 512), F32),
        ),
        in_specs=[any_spec] * 12 + [smem] * 5,
        out_specs=(vmem, vmem),
        scratch_shapes=[
            pltpu.VMEM(big, F32),
            pltpu.VMEM(big, F32),
            pltpu.VMEM((2, 48, 512), F32),
            pltpu.VMEM((2, 32, 512), jnp.int32),
            pltpu.VMEM((2, 32, 512), jnp.int32),
        ]
        + [pltpu.VMEM((4, 256, 256), BF16)] * 4
        + [pltpu.VMEM((256, 256), BF16)] * 4
        + [pltpu.VMEM((32, 2, 128), F32)]
        + [
            pltpu.VMEM((2, 34, 1, 512), F32),
            pltpu.VMEM((2, 34, 1, 512), F32),
            pltpu.VMEM((2, 32, 1, 512), F32),
            pltpu.VMEM((2, 32, 1, 512), F32),
            pltpu.VMEM((34, 32, 128), F32),
            pltpu.VMEM((34, 32, 128), F32),
            pltpu.VMEM((32, 32, 128), F32),
            pltpu.VMEM((32, 32, 128), F32),
            pltpu.VMEM((2, 16, 32, 512), F32),
            pltpu.VMEM((16, 32, 512), F32),
            pltpu.VMEM((16, 32, 512), F32),
            pltpu.VMEM((2, 2, 32, 512), F32),
            pltpu.VMEM((2, 2, 32, 512), F32),
            pltpu.VMEM((2, 3, 32, 512), F32),
            pltpu.VMEM((2, 3, 32, 512), F32),
            pltpu.VMEM((2, 3, 32, 512), F32),
        ]
        + [pltpu.VMEM(columns, F32)] * 4
        + [pltpu.VMEM((3, 32, 16, 128), F32)]
        + [pltpu.VMEM(every, F32)] * 4
        + [pltpu.VMEM((4, 8, 2, 16, 128), F32)]
        + [pltpu.VMEM((4, 256, 128), BF16)] * 2
        + [pltpu.VMEM((32, 2, 16, 128), F32)]
        + [pltpu.VMEM((512, 256), BF16)] * 2
        + [pltpu.SemaphoreType.DMA((n,)) for n in (12, 6, 6, 2 * CHUNKS, 2 * CHUNKS, 3, 3, 2 * ITERS, 2 * ITERS)],
        compiler_params=pltpu.CompilerParams(
            collective_id=0, has_side_effects=True, vmem_limit_bytes=56 * 1024 * 1024
        ),
        name="step",
    )(order, grain, phase, *[jnp.asarray(t) for t in constants], mobility, index, stiff.T, eigen.T, macro)


def solution(mesh):
    fields = P("grp", None, "row", "col")
    labels = P("grp", "row", "col")
    return jax.shard_map(
        body,
        mesh=mesh,
        in_specs=(fields, labels, labels, P(), P(), P(), P(), P()),
        out_specs=(fields, fields),
        check_vma=False,
    )
```

```python
import jax
import jax.numpy as jnp
import ml_dtypes
import numpy as np
from jax import lax
from jax.experimental import pallas as pl
from jax.experimental.pallas import tpu as pltpu
from jax.sharding import PartitionSpec as P

MESH = pl.DeviceIdType.MESH
ITERS = 2
ROWS = 32
HALF = 0.7071067811865476
LAMBDA_REF = 1.25
SHEAR_REF = 1.25
BETA_REF = (LAMBDA_REF + SHEAR_REF) / (SHEAR_REF * (LAMBDA_REF + 2.0 * SHEAR_REF))
F32 = jnp.float32
BF16 = jnp.bfloat16
CHUNK = 4
CHUNKS = 16 // CHUNK
UNROLL = 4
EARLY = 1


def split_table(values):
    high = values.astype(np.float32).astype(ml_dtypes.bfloat16)
    low = (values - high.astype(np.float64)).astype(np.float32).astype(ml_dtypes.bfloat16)
    return high, low


def tables():
    place = np.arange(128, dtype=np.float64)
    forward = np.zeros((4, 256, 256))
    inverse = np.zeros((4, 256, 256))
    scale = 1.0 / 1048576.0
    half = np.arange(64, dtype=np.float64)
    for first, base in ((0, 0), (64, 4)):
        angle = 2.0 * np.pi * np.outer(base + 8 * half, place) / 1024.0
        source = slice(0, 128) if base == 0 else slice(128, 256)
        forward[0, first : first + 64, source] = np.cos(angle)
        forward[0, 128 + first : 192 + first, source] = -np.sin(angle)
        weight = np.full((64, 1), 2.0 * scale)
        if base == 0:
            weight[0] = scale
        inverse[0, source, first : first + 64] = (weight * np.cos(angle)).T
        inverse[0, source, 128 + first : 192 + first] = (-weight * np.sin(angle)).T
    for kind in (1, 2, 3):
        angle = 2.0 * np.pi * np.outer(kind + 8 * place, place) / 1024.0
        cosine, sine = np.cos(angle), np.sin(angle)
        forward[kind] = np.block([[cosine, sine], [-sine, cosine]])
        inverse[kind] = 2.0 * scale * np.block([[cosine.T, -sine.T], [sine.T, cosine.T]])
    small = np.arange(32, dtype=np.float64)
    angle = 2.0 * np.pi * np.outer(small, small) / 32.0
    slots = np.eye(4)
    slots[3, 3] = 0.0
    cosine, sine = np.kron(slots, np.cos(angle)), np.kron(slots, np.sin(angle))
    rows_inverse = np.block([[cosine, sine], [-sine, cosine]])
    slots[1, 3] = 1.0
    cosine, sine = np.kron(slots, np.cos(angle)), np.kron(slots, np.sin(angle))
    rows_forward = np.block([[cosine, -sine], [sine, cosine]])
    angle = 2.0 * np.pi * np.outer(small, np.tile(small, 4)) / 1024.0
    turn = np.stack([np.cos(angle), np.sin(angle)], axis=1).astype(np.float32)
    return (
        split_table(forward)
        + split_table(inverse)
        + split_table(rows_forward)
        + split_table(rows_inverse)
        + (turn,)
    )


def times(value, angle_index, length, sign):
    real, imag = value
    angle_index = angle_index % length
    if angle_index == 0:
        return value
    angle = 2.0 * np.pi * angle_index / length
    cosine, sine = float(np.cos(angle)), float(sign * np.sin(angle))
    if 4 * angle_index == length or 4 * angle_index == 3 * length:
        return (-imag, real) if sine > 0 else (imag, -real)
    if 2 * angle_index == length:
        return (-real, -imag)
    return (real * cosine - imag * sine, imag * cosine + real * sine)


def plus(first, second):
    return (first[0] + second[0], first[1] + second[1])


def minus(first, second):
    return (first[0] - second[0], first[1] - second[1])


def four(x, sign):
    a, b, c, d = plus(x[0], x[2]), minus(x[0], x[2]), plus(x[1], x[3]), minus(x[1], x[3])
    d = (-d[1], d[0]) if sign > 0 else (d[1], -d[0])
    return [plus(a, c), plus(b, d), minus(a, c), minus(b, d)]


def eight(x, sign):
    even, odd = four(x[0::2], sign), four(x[1::2], sign)
    odd = [odd[0], times(odd[1], 1, 8, sign), times(odd[2], 2, 8, sign), times(odd[3], 3, 8, sign)]
    return [plus(e, o) for e, o in zip(even, odd)] + [minus(e, o) for e, o in zip(even, odd)]


def parts(value):
    high = value.astype(BF16)
    return high, (value - high.astype(F32)).astype(BF16)


def dot(a, b):
    return jnp.dot(a, b, preferred_element_type=F32)


def dot3(a_high, a_low, b_high, b_low):
    return dot(a_high, b_high) + dot(a_high, b_low) + dot(a_low, b_high)


def kernel(
    order_hbm, grain_hbm, phase_hbm, tfh_hbm, tfl_hbm, tih_hbm, til_hbm, bfh_hbm, bfl_hbm, bih_hbm,
    bil_hbm, turn_hbm, mob_s, index_s, stiff_s, eigen_s, macro_s,
    middle, base, outer_in2, final, eig, lame, mob,
    first, grain, phase, tfh, tfl, tih, til, bfh, bfl, bih, bil, turn,
    row_out, row_in, row_out2, row_in2, col_out, col_in, col_out2, col_in2,
    outer_in, lame_in, eig_in,
    strain, eig_t, m1_t, m2_t, green, send1, recv1, send2, recv2, work, both, flat, lxh, lxl,
    load_sem, halo_send, halo_recv, outer_send, outer_recv, core_send, core_recv, all_send, all_recv, meet_sem,
):
    g, r, c = lax.axis_index("grp"), lax.axis_index("row"), lax.axis_index("col")
    inner, outer = g, 1 - g
    mine = jnp.where(c == 0, inner, outer)
    other = 1 - mine
    core_peer = (g, r, 1 - c)
    grp_peer = (1 - g, r, c)
    row_up = (g, (r + ROWS - 1) % ROWS, c)
    row_down = (g, (r + 1) % ROWS, c)

    def remote(source, target, send, recv, device):
        return pltpu.make_async_remote_copy(
            source, target, send, recv, device_id=device, device_id_type=MESH
        )

    loads = [
        pltpu.make_async_copy(grain_hbm, grain, load_sem.at[0]),
        pltpu.make_async_copy(phase_hbm, phase, load_sem.at[1]),
        pltpu.make_async_copy(order_hbm, first.at[:, :, pl.ds(8, 32), :], load_sem.at[2]),
    ]
    pairs = (
        (tfh_hbm, tfh), (tfl_hbm, tfl), (tih_hbm, tih), (til_hbm, til), (bfh_hbm, bfh),
        (bfl_hbm, bfl), (bih_hbm, bih), (bil_hbm, bil), (turn_hbm, turn),
    )
    for place, (source, target) in enumerate(pairs):
        loads.append(pltpu.make_async_copy(source, target, load_sem.at[3 + place]))
    for load in loads:
        load.start()

    barrier = pltpu.get_barrier_semaphore()
    beyond = jnp.where(r % 2 == 1, row_down[1], row_up[1])
    near = [(g, jnp.bitwise_xor(r, 1 << k), c) for k in range(5)]
    for peer in [grp_peer, core_peer, (g, beyond, c)] + near:
        pl.semaphore_signal(barrier, inc=1, device_id=peer, device_id_type=MESH)

    def meet(k):
        if k > 0:
            pl.semaphore_wait(meet_sem.at[k - 1], 1)
        if k < 5:
            pl.semaphore_signal(meet_sem.at[k], inc=1, device_id=near[k], device_id_type=MESH)

    loads[0].wait()
    loads[1].wait()
    for layer in range(2):
        labels = grain[layer]

        def look(k, value):
            return jnp.where(labels == k, mob_s[k], value)

        mob[layer, 8:40, :] = lax.fori_loop(0, 32, look, jnp.zeros((32, 512), F32))
        labels2 = phase[layer]

        def look2(k, values):
            chosen = index_s[k]
            hit = labels2 == k
            return (
                jnp.where(hit, stiff_s[0, chosen], values[0]),
                jnp.where(hit, stiff_s[1, chosen], values[1]),
            )

        empty = jnp.zeros((32, 512), F32)
        lam, shear = lax.fori_loop(0, 8, look2, (empty, empty))
        lame[layer, 0] = lam
        lame[layer, 1] = shear

    lane = lax.broadcasted_iota(jnp.int32, (32, 128), 1)

    def pack(source, rows_to, cols_to):
        def step(i, carry):
            for layer in range(2):
                k = layer * 16 + i
                rows_to[0, k] = source[layer, i, 8:9, :]
                rows_to[1, k] = source[layer, i, 39:40, :]
                cols_to[k] = jnp.where(
                    lane < 64, source[layer, i, 8:40, 0:128], source[layer, i, 8:40, 384:512]
                )
            return carry

        lax.fori_loop(0, 16, step, 0)

    def unpack(target, rows_from):
        def step(i, carry):
            for layer in range(2):
                k = layer * 16 + i
                target[layer, i, 40:41, :] = rows_from[0, k]
                target[layer, i, 7:8, :] = rows_from[1, k]
            return carry

        lax.fori_loop(0, 16, step, 0)

    loads[2].wait()
    pack(first, row_out, col_out)
    for layer in range(2):
        row_out[0, 32 + layer] = mob[layer, 8:9, :]
        row_out[1, 32 + layer] = mob[layer, 39:40, :]
        col_out[32 + layer] = jnp.where(lane < 64, mob[layer, 8:40, 0:128], mob[layer, 8:40, 384:512])

    pl.semaphore_wait(barrier, 8)
    meet(0)

    halo = [
        remote(row_out.at[0], row_in.at[0], halo_send.at[0], halo_recv.at[0], row_up),
        remote(row_out.at[1], row_in.at[1], halo_send.at[1], halo_recv.at[1], row_down),
        remote(col_out, col_in, halo_send.at[2], halo_recv.at[2], core_peer),
    ]
    for copy in halo:
        copy.start()

    def outer_copy(k):
        at = pl.ds(k * CHUNK, CHUNK)
        return remote(
            order_hbm.at[outer, at], outer_in.at[at], outer_send.at[k], outer_recv.at[k], grp_peer
        )

    def outer_copy2(k):
        at = pl.ds(k * CHUNK, CHUNK)
        return remote(
            middle.at[outer, at, pl.ds(8, 32), :], outer_in2.at[at],
            outer_send.at[CHUNKS + k], outer_recv.at[CHUNKS + k], grp_peer,
        )

    for k in range(CHUNKS):
        outer_copy(k).start()
    lame_copy = remote(lame.at[other], lame_in.at[c], core_send.at[0], core_recv.at[0], core_peer)
    lame_copy.start()

    sub16 = lax.broadcasted_iota(jnp.int32, (16, 128), 0)
    lane16 = lax.broadcasted_iota(jnp.int32, (16, 128), 1)
    slot = lane16 // 32
    place = (r % 8) * 16 + sub16
    kind = r // 8
    col_freq = jnp.where(
        kind > 0, kind + 8 * place, jnp.where(place < 64, 8 * place, 4 + 8 * (place - 64))
    )
    col_signed = jnp.where(col_freq >= 512, col_freq - 1024, col_freq).astype(F32)

    def green_step(k1, carry):
        row_freq = k1 + 32 * (lane16 % 32)
        row_signed = jnp.where(row_freq >= 512, row_freq - 1024, row_freq).astype(F32)
        keeper = jnp.where((row_freq != 512) & (col_freq != 512), 1.0, 0.0)
        radius = row_signed * row_signed + col_signed * col_signed
        inverse = keeper * lax.rsqrt(jnp.where(radius > 0, radius, 1.0))
        n1, n2 = row_signed * inverse, col_signed * inverse
        a, b, d = n1 * n1, n2 * n2, n1 * n2
        own = jnp.where(
            slot == 0,
            a / SHEAR_REF - BETA_REF * a * a,
            jnp.where(
                slot == 2,
                b / SHEAR_REF - BETA_REF * b * b,
                0.5 * (a + b) / SHEAR_REF - 2.0 * BETA_REF * d * d,
            ),
        )
        toward_rr = 0.5 * d / SHEAR_REF - BETA_REF * a * d
        toward_cc = 0.5 * d / SHEAR_REF - BETA_REF * b * d
        across = -BETA_REF * d * d
        green[0, k1] = own
        green[1, k1] = jnp.where(
            slot == 1, toward_cc, jnp.where(slot == 3, toward_rr, across)
        )
        green[2, k1] = jnp.where(
            slot == 0,
            2.0 * toward_rr,
            jnp.where(slot == 1, toward_rr, jnp.where(slot == 2, 2.0 * toward_cc, toward_cc)),
        )
        return carry

    lax.fori_loop(0, 32, green_step, 0)
    meet(1)

    def to_columns(target, half, slots):
        for j in range(4):
            block = jnp.concatenate([field[:, 128 * j : 128 * j + 128] for field in slots], axis=0)
            target[4 * half + j] = block.T

    def stiff_columns(half, lam, shear):
        double = 2.0 * shear
        straight = lam + double
        empty = jnp.zeros_like(lam)
        to_columns(m1_t, half, (straight, double, straight, empty))
        to_columns(m2_t, half, (lam, empty, lam, empty))

    stiff_columns(c, lame[mine, 0], lame[mine, 1])

    for copy in halo:
        copy.wait_recv()
    meet(2)
    unpack(first, row_in)
    for layer in range(2):
        mob[layer, 40:41, :] = row_in[0, 32 + layer]
        mob[layer, 7:8, :] = row_in[1, 32 + layer]

    def update(source, cols, layer, write):
        for s in range(4):
            r0, r1 = 8 + 8 * s, 8 * s
            m = mob[layer, r0 : r0 + 8, :]
            edge = jnp.concatenate([col_in[32 + layer, r1 : r1 + 8, :], m], axis=1)
            w_up = 0.05 * (m + mob[layer, r0 - 1 : r0 + 7, :])
            w_down = 0.05 * (m + mob[layer, r0 + 1 : r0 + 9, :])
            w_left = 0.05 * (m + pltpu.roll(edge, 1, 1)[:, 128:])
            w_right = 0.05 * (m + pltpu.roll(edge, 639, 1)[:, 128:])
            total = jnp.zeros((8, 512), F32)
            for i in range(16):
                v = source[layer, i, r0 : r0 + 8, :]
                total = total + v * v
            c0 = 1.0 - (w_up + w_down + w_left + w_right) - 0.3 * m * total
            c1 = 0.2 * m
            m05 = 0.05 * m

            def step(n, carry):
                for i4 in range(UNROLL):
                    i = n * UNROLL + i4
                    v = source[layer, i, r0 : r0 + 8, :]
                    e = jnp.concatenate([cols[layer * 16 + i, r1 : r1 + 8, :], v], axis=1)
                    write(
                        layer,
                        i,
                        s,
                        v * (c0 + c1 * v * v)
                        + w_up * source[layer, i, r0 - 1 : r0 + 7, :]
                        + w_down * source[layer, i, r0 + 1 : r0 + 9, :]
                        + w_left * pltpu.roll(e, 1, 1)[:, 128:]
                        + w_right * pltpu.roll(e, 639, 1)[:, 128:]
                        + m05 * source[1 - layer, i, r0 : r0 + 8, :],
                    )
                return carry

            lax.fori_loop(0, 16 // UNROLL, step, 0)

    def to_middle(layer, i, s, value):
        middle[layer, i, 8 + 8 * s : 16 + 8 * s, :] = value

    def to_base(layer, i, s, value):
        base[layer, i, 8 * s : 8 * s + 8, :] = value

    update(first, col_in, inner, to_middle)
    meet(3)
    for s in range(4):
        totals = [jnp.zeros((8, 512), F32)] * 3
        for i in range(16):
            v = middle[inner, i, 8 + 8 * s : 16 + 8 * s, :]
            v = v * v
            totals = [totals[k] + v * eigen_s[k, i] for k in range(3)]
        for k in range(3):
            eig[inner, k, 8 * s : 8 * s + 8, :] = totals[k]
            eig[outer, k, 8 * s : 8 * s + 8, :] = jnp.zeros((8, 512), F32)
    update(first, col_in, outer, to_middle)
    meet(4)

    lame_copy.wait_recv()
    stiff_columns(1 - c, lame_in[1 - c, 0], lame_in[1 - c, 1])

    for k in range(CHUNKS):
        outer_copy(k).wait_recv()
        if k == 2:
            meet(5)

        def add(s, carry):
            at, at2 = pl.ds(pl.multiple_of(8 + 8 * s, 8), 8), pl.ds(pl.multiple_of(8 * s, 8), 8)
            m05 = 0.05 * mob[outer, at, :]
            totals = [eig[outer, n, at2, :] for n in range(3)]
            for i in range(CHUNK):
                j = k * CHUNK + i
                v = middle[outer, j, at, :] + m05 * outer_in[j, at2, :]
                middle[outer, j, at, :] = v
                v = v * v
                totals = [totals[n] + v * eigen_s[n, j] for n in range(3)]
            for n in range(3):
                eig[outer, n, at2, :] = totals[n]
            return carry

        lax.fori_loop(0, 4, add, 0)
        if k < EARLY:
            outer_copy2(k).start()

    eig_copy = remote(eig.at[other], eig_in.at[c], core_send.at[1], core_recv.at[1], core_peer)
    eig_copy.start()
    to_columns(eig_t, c, (eig[mine, 0], eig[mine, 2], eig[mine, 1], eig[mine, 2]))
    halo2 = [
        remote(row_out2.at[0], row_in2.at[0], halo_send.at[3], halo_recv.at[3], row_up),
        remote(row_out2.at[1], row_in2.at[1], halo_send.at[4], halo_recv.at[4], row_down),
        remote(col_out2, col_in2, halo_send.at[5], halo_recv.at[5], core_peer),
    ]

    eig_copy.wait_recv()
    far = [eig_in[1 - c, k] for k in range(3)]
    to_columns(eig_t, 1 - c, (far[0], far[2], far[1], far[2]))

    lane1 = lax.broadcasted_iota(jnp.int32, (128, 128), 1)
    start = jnp.where(
        lane1 < 32, macro_s[0], jnp.where((lane1 >= 64) & (lane1 < 96), macro_s[1], macro_s[2])
    )
    for n1 in range(8):
        strain[n1] = start
    for load in loads[3:]:
        load.wait()

    even16 = (lane16 // 32) % 2 == 0
    lane_all = lax.broadcasted_iota(jnp.int32, (128, 128), 1)
    even = (lane_all // 32) % 2 == 0

    def product(table_high, table_low, kind):
        wide = dot(table_high[kind], both[kind])
        return wide[:, 0:128] + wide[:, 128:256] + dot(table_low[kind], both[kind, :, 0:128])

    def pack3(a):
        slot = lax.broadcasted_iota(jnp.int32, a[0].shape, 1) // 32
        return [jnp.where(slot == 3, pltpu.roll(a[3], 96 - 32 * k, 1), a[k]) for k in range(3)]

    def unpack3(p):
        slot = lax.broadcasted_iota(jnp.int32, p[0].shape, 1) // 32
        x, y, z = (pltpu.roll(p[k], 32 + 32 * k, 1) for k in range(3))
        return list(p) + [jnp.where(slot == 0, x, jnp.where(slot == 1, y, z))]

    def sweep(it, carry):
        def stage(t, carry):
            rows = pl.ds(pl.multiple_of(t * 16, 16), 16)
            x = []
            for n1 in range(8):
                d = strain[n1, rows, :] - eig_t[n1, rows, :]
                x.append(m1_t[n1, rows, :] * d + m2_t[n1, rows, :] * pltpu.roll(d, 64, 1))
            s04, d04, s26, d26 = x[0] + x[4], x[0] - x[4], x[2] + x[6], x[2] - x[6]
            s15, d15, s37, d37 = x[1] + x[5], x[1] - x[5], x[3] + x[7], x[3] - x[7]
            evens, odds = s04 + s26, s15 + s37
            turned = HALF * (d15 - d37)
            summed = HALF * (d15 + d37)
            values = (
                (evens + odds, evens - odds),
                (d04 + turned, -d26 - summed),
                (s04 - s26, s37 - s15),
                (d04 - turned, d26 - summed),
            )
            rows2 = pl.ds(pl.multiple_of(128 + t * 16, 16), 16)
            for kind, (real, imag) in enumerate(values):
                both[kind, rows, 0:128], both[kind, rows, 128:256] = parts(real)
                both[kind, rows2, 0:128], both[kind, rows2, 128:256] = parts(imag)
            return carry

        lax.fori_loop(0, 8, stage, 0)

        def forward(kk, carry):
            kind = (r // 8 + kk) % 4
            result = product(tfh, tfl, kind).reshape(2, 8, 2, 8, 128)
            packed = pack3([result[n // 2, :, n % 2].reshape(64, 128) for n in range(4)])
            for n in range(3):
                send1[it, pl.ds(8 * kind, 8), n] = packed[n].reshape(8, 8, 128)

            def post(j, carry):
                peer = 8 * kind + (r % 8 + j) % 8

                @pl.when(peer != r)
                def _():
                    remote(
                        send1.at[it, peer], recv1.at[it, r],
                        all_send.at[2 * it], all_recv.at[2 * it], (g, peer, c),
                    ).start()

                return carry

            lax.fori_loop(0, 8, post, 0)
            return carry

        lax.fori_loop(0, 4, forward, 0)
        pltpu.make_async_copy(send1.at[it, r], recv1.at[it, r], all_recv.at[2 * it]).start()
        outer_copy2(2 * it + 1).start()

        @pl.when(it == 0)
        def _():
            pack(middle, row_out2, col_out2)
            for copy in halo2:
                copy.start()

        pltpu.make_async_copy(recv1.at[it], recv1.at[it], all_recv.at[2 * it]).wait()

        for b in range(8):
            x = []
            for a in range(4):
                v = unpack3([recv1[it, 8 * a + b, n] for n in range(3)])
                x.append((jnp.concatenate(v[0:2], axis=0), jnp.concatenate(v[2:4], axis=0)))
            y = four(x, -1)
            for ka in range(4):
                work[ka, b, 0], work[ka, b, 1] = times(y[ka], b * ka, 32, -1)
        for ka in range(4):
            y = eight([(work[ka, b, 0], work[ka, b, 1]) for b in range(8)], -1)
            for kb in range(8):
                k1 = ka + 4 * kb
                cosine, sine = turn[k1, 0:1, :], turn[k1, 1:2, :]
                real, imag = y[kb]
                z = (real * cosine + imag * sine, imag * cosine - real * sine)
                for half in range(2):
                    at = (slice(16 * k1, 16 * k1 + 16), slice(128 * half, 128 * half + 128))
                    lxh[at], lxl[at] = parts(z[half])

        def middle_stage(q, carry):
            rows = pl.ds(pl.multiple_of(q * 128, 128), 128)
            spectrum = dot3(lxh[rows, :], lxl[rows, :], bfh[...], bfl[...])
            group = pl.ds(8 * q, 8)
            g0 = green[0, group].reshape(128, 128)
            g1 = green[1, group].reshape(128, 128)
            g2 = green[2, group].reshape(128, 128)
            pieces = []
            for half in range(2):
                s = spectrum[:, 128 * half : 128 * half + 128]
                z = jnp.where(even, pltpu.roll(s, 64, 1), pltpu.roll(s, 96, 1))
                pieces.append(parts(g0 * s + g1 * z + g2 * pltpu.roll(s, 32, 1)))
            oh = jnp.concatenate([pieces[0][0], pieces[1][0]], axis=1)
            ol = jnp.concatenate([pieces[0][1], pieces[1][1]], axis=1)
            back = dot3(oh, ol, bih[...], bil[...])
            for j in range(8):
                k1 = 8 * q + j
                cosine, sine = turn[k1, 0:1, :], turn[k1, 1:2, :]
                real, imag = back[16 * j : 16 * j + 16, 0:128], back[16 * j : 16 * j + 16, 128:256]
                flat[k1, 0] = real * cosine - imag * sine
                flat[k1, 1] = imag * cosine + real * sine
            return carry

        lax.fori_loop(0, 4, middle_stage, 0)

        for ka in range(4):
            y = eight([(flat[ka + 4 * kb, 0], flat[ka + 4 * kb, 1]) for kb in range(8)], 1)
            for b in range(8):
                work[ka, b, 0], work[ka, b, 1] = times(y[b], b * ka, 32, 1)

        def backward(bb, carry):
            b = (r + bb) % 8
            y = four([(work[ka, b, 0], work[ka, b, 1]) for ka in range(4)], 1)
            for a in range(4):
                packed = pack3([y[a][n // 2][8 * (n % 2) : 8 * (n % 2) + 8] for n in range(4)])
                for n in range(3):
                    send2[it, 8 * a + b, n] = packed[n]

            def post(j, carry):
                peer = 8 * ((r // 8 + j) % 4) + b

                @pl.when(peer != r)
                def _():
                    remote(
                        send2.at[it, peer], recv2.at[it, r],
                        all_send.at[2 * it + 1], all_recv.at[2 * it + 1], (g, peer, c),
                    ).start()

                return carry

            lax.fori_loop(0, 4, post, 0)
            return carry

        lax.fori_loop(0, 8, backward, 0)
        pltpu.make_async_copy(send2.at[it, r], recv2.at[it, r], all_recv.at[2 * it + 1]).start()

        @pl.when(it == 0)
        def _():
            outer_copy2(2).start()
            for copy in halo2:
                copy.wait_recv()
            unpack(middle, row_in2)

        update(middle, col_in2, it, to_base)
        pltpu.make_async_copy(recv2.at[it], recv2.at[it], all_recv.at[2 * it + 1]).wait()

        def inverse(kind, carry):
            group = pl.ds(8 * kind, 8)
            v = unpack3([recv2[it, group, n].reshape(64, 128) for n in range(3)])
            for half in range(2):
                at = slice(128 * half, 128 * half + 128)
                pair = [v[2 * half + n].reshape(8, 1, 8, 128) for n in range(2)]
                value = parts(jnp.concatenate(pair, axis=1).reshape(128, 128))
                both[kind, at, 0:128], both[kind, at, 128:256] = value
            result = product(tih, til, kind)
            flat[pl.ds(8 * kind, 8), 0] = result[0:128].reshape(8, 16, 128)
            flat[pl.ds(8 * kind, 8), 1] = result[128:256].reshape(8, 16, 128)
            return carry

        lax.fori_loop(0, 4, inverse, 0)

        def unstage(t, carry):
            rows = pl.ds(pl.multiple_of(t * 16, 16), 16)
            z0, z4 = flat[t, 0], flat[t, 1]
            a1, b1 = flat[8 + t, 0], flat[8 + t, 1]
            a2, b2 = flat[16 + t, 0], flat[16 + t, 1]
            a3, b3 = flat[24 + t, 0], flat[24 + t, 1]
            zp, zm = z0 + z4, z0 - z4
            sa, db, da, sb = a1 + a3, b3 - b1, a1 - a3, b1 + b3
            p1, p2 = HALF * (da - sb), HALF * (da + sb)
            values = (
                zp + a2 + sa,
                zm - b2 + p1,
                zp - a2 + db,
                zm + b2 - p2,
                zp + a2 - sa,
                zm - b2 - p1,
                zp - a2 - db,
                zm + b2 + p2,
            )
            for n1 in range(8):
                strain[n1, rows, :] -= values[n1]
            return carry

        lax.fori_loop(0, 8, unstage, 0)
        return carry

    lax.fori_loop(0, ITERS, sweep, 0)

    def to_rows(half, layer, target):
        for j in range(4):
            block = strain[4 * half + j].T
            lanes = slice(128 * j, 128 * j + 128)
            target[layer, 0, :, lanes] = block[0:32]
            target[layer, 1, :, lanes] = block[64:96]
            target[layer, 2, :, lanes] = block[32:64]

    to_rows(1 - c, 0, eig_in)
    final_copy = remote(eig_in.at[0], final.at[mine], core_send.at[2], core_recv.at[2], core_peer)
    final_copy.start()
    to_rows(c, mine, final)
    remote(eig_in.at[0], final.at[other], core_send.at[2], core_recv.at[2], core_peer).wait_recv()
    for k in range(CHUNKS):
        outer_copy2(k).wait_recv()
    for copy in halo + halo2 + [lame_copy, eig_copy, final_copy]:
        copy.wait_send()
    for k in range(CHUNKS):
        outer_copy(k).wait_send()
        outer_copy2(k).wait_send()
    for it in range(ITERS):
        for sent, sem in ((send1, 2 * it), (send2, 2 * it + 1)):
            whole = sent.at[it, pl.ds(0, ROWS - 1)]
            pltpu.make_async_copy(whole, whole, all_send.at[sem]).wait()


def finish(
    middle, base, outer_in2, final, eig, lame, mob, eigen_s, out_hbm, strain_hbm, out, sem
):
    g = lax.axis_index("grp")
    strain_copy = pltpu.make_async_copy(final, strain_hbm, sem.at[8])
    strain_copy.start()
    for place in range(2):
        layer = g if place == 0 else 1 - g

        def at(s, carry):
            rows = pl.ds(pl.multiple_of(8 * s, 8), 8)
            rows2 = pl.ds(pl.multiple_of(8 + 8 * s, 8), 8)
            d = [final[layer, k, rows, :] - eig[layer, k, rows, :] for k in range(3)]
            lam, double = lame[layer, 0, rows, :], 2.0 * lame[layer, 1, rows, :]
            m = mob[layer, rows2, :]
            m05, c1 = 0.05 * m, 0.2 * m
            push = (
                c1 * ((lam + double) * d[0] + lam * d[1]),
                c1 * (lam * d[0] + (lam + double) * d[1]),
                c1 * (2.0 * (double * d[2])),
            )
            for i in range(16):
                v = middle[layer, i, rows2, :]
                value = base[layer, i, rows, :] + v * (
                    push[0] * eigen_s[0, i] + push[1] * eigen_s[1, i] + push[2] * eigen_s[2, i]
                )
                if place == 1:
                    value = value + m05 * outer_in2[i, rows, :]
                out[layer, i, rows, :] = value
            pltpu.make_async_copy(
                out.at[layer, :, rows, :], out_hbm.at[layer, :, rows, :], sem.at[4 * place + s]
            ).start()
            return carry

        lax.fori_loop(0, 4, at, 0)
    for place in range(2):
        layer = g if place == 0 else 1 - g
        for s in range(4):
            rows = pl.ds(8 * s, 8)
            pltpu.make_async_copy(
                out.at[layer, :, rows, :], out_hbm.at[layer, :, rows, :], sem.at[4 * place + s]
            ).wait()
    strain_copy.wait()


def body(order, grain, phase, mobility, index, stiff, eigen, macro):
    constants = tables()
    any_spec = pl.BlockSpec(memory_space=pl.ANY)
    smem = pl.BlockSpec(memory_space=pltpu.SMEM)
    vmem = pl.BlockSpec(memory_space=pltpu.VMEM)
    big = (2, 16, 48, 512)
    every = (ITERS, ROWS, 3, 8, 128)
    columns = (8, 128, 128)
    kept = (
        big, (2, 16, 32, 512), (16, 32, 512), (2, 3, 32, 512), (2, 3, 32, 512), (2, 2, 32, 512),
        (2, 48, 512),
    )
    values = pl.pallas_call(
        kernel,
        out_shape=tuple(pltpu.VMEM(shape, F32) for shape in kept),
        in_specs=[any_spec] * 12 + [smem] * 5,
        out_specs=(vmem,) * len(kept),
        scratch_shapes=[
            pltpu.VMEM(big, F32),
            pltpu.VMEM((2, 32, 512), jnp.int32),
            pltpu.VMEM((2, 32, 512), jnp.int32),
        ]
        + [pltpu.VMEM((4, 256, 256), BF16)] * 4
        + [pltpu.VMEM((256, 256), BF16)] * 4
        + [pltpu.VMEM((32, 2, 128), F32)]
        + [
            pltpu.VMEM((2, 34, 1, 512), F32),
            pltpu.VMEM((2, 34, 1, 512), F32),
            pltpu.VMEM((2, 32, 1, 512), F32),
            pltpu.VMEM((2, 32, 1, 512), F32),
            pltpu.VMEM((34, 32, 128), F32),
            pltpu.VMEM((34, 32, 128), F32),
            pltpu.VMEM((32, 32, 128), F32),
            pltpu.VMEM((32, 32, 128), F32),
            pltpu.VMEM((16, 32, 512), F32),
            pltpu.VMEM((2, 2, 32, 512), F32),
            pltpu.VMEM((2, 3, 32, 512), F32),
        ]
        + [pltpu.VMEM(columns, F32)] * 4
        + [pltpu.VMEM((3, 32, 16, 128), F32)]
        + [pltpu.VMEM(every, F32)] * 4
        + [pltpu.VMEM((4, 8, 2, 16, 128), F32)]
        + [pltpu.VMEM((4, 256, 256), BF16)]
        + [pltpu.VMEM((32, 2, 16, 128), F32)]
        + [pltpu.VMEM((512, 256), BF16)] * 2
        + [
            pltpu.SemaphoreType.DMA((n,))
            for n in (12, 6, 6, 2 * CHUNKS, 2 * CHUNKS, 3, 3, 2 * ITERS, 2 * ITERS)
        ]
        + [pltpu.SemaphoreType.REGULAR((5,))],
        compiler_params=pltpu.CompilerParams(
            collective_id=0, has_side_effects=True, vmem_limit_bytes=48 * 1024 * 1024
        ),
        name="step",
    )(order, grain, phase, *[jnp.asarray(t) for t in constants], mobility, index, stiff.T, eigen.T, macro)
    return pl.pallas_call(
        finish,
        out_shape=(
            jax.ShapeDtypeStruct((2, 16, 32, 512), F32),
            jax.ShapeDtypeStruct((2, 3, 32, 512), F32),
        ),
        in_specs=[vmem] * len(kept) + [smem],
        out_specs=(any_spec, any_spec),
        scratch_shapes=[pltpu.VMEM((2, 16, 32, 512), F32), pltpu.SemaphoreType.DMA((9,))],
        compiler_params=pltpu.CompilerParams(vmem_limit_bytes=6 * 1024 * 1024),
        name="finish",
    )(*values, eigen.T)


def solution(mesh):
    fields = P("grp", None, "row", "col")
    labels = P("grp", "row", "col")
    return jax.shard_map(
        body,
        mesh=mesh,
        in_specs=(fields, labels, labels, P(), P(), P(), P(), P()),
        out_specs=(fields, fields),
        check_vma=False,
    )
```

```python
import jax
import jax.numpy as jnp
import ml_dtypes
import numpy as np
from jax import lax
from jax.experimental import pallas as pl
from jax.experimental.pallas import tpu as pltpu
from jax.sharding import PartitionSpec as P

MESH = pl.DeviceIdType.MESH
ITERS = 2
ROWS = 32
HALF = 0.7071067811865476
LAMBDA_REF = 1.25
SHEAR_REF = 1.25
BETA_REF = (LAMBDA_REF + SHEAR_REF) / (SHEAR_REF * (LAMBDA_REF + 2.0 * SHEAR_REF))
F32 = jnp.float32
BF16 = jnp.bfloat16
CHUNK = 4
CHUNKS = 16 // CHUNK
UNROLL = 4
EARLY = 1


def split_table(values):
    high = values.astype(np.float32).astype(ml_dtypes.bfloat16)
    low = (values - high.astype(np.float64)).astype(np.float32).astype(ml_dtypes.bfloat16)
    return high, low


def tables():
    place = np.arange(128, dtype=np.float64)
    forward = np.zeros((4, 256, 256))
    inverse = np.zeros((4, 256, 256))
    scale = 1.0 / 1048576.0
    half = np.arange(64, dtype=np.float64)
    for first, base in ((0, 0), (64, 4)):
        angle = 2.0 * np.pi * np.outer(base + 8 * half, place) / 1024.0
        source = slice(0, 128) if base == 0 else slice(128, 256)
        forward[0, first : first + 64, source] = np.cos(angle)
        forward[0, 128 + first : 192 + first, source] = -np.sin(angle)
        weight = np.full((64, 1), 2.0 * scale)
        if base == 0:
            weight[0] = scale
        inverse[0, source, first : first + 64] = (weight * np.cos(angle)).T
        inverse[0, source, 128 + first : 192 + first] = (-weight * np.sin(angle)).T
    for kind in (1, 2, 3):
        angle = 2.0 * np.pi * np.outer(kind + 8 * place, place) / 1024.0
        cosine, sine = np.cos(angle), np.sin(angle)
        forward[kind] = np.block([[cosine, sine], [-sine, cosine]])
        inverse[kind] = 2.0 * scale * np.block([[cosine.T, -sine.T], [sine.T, cosine.T]])
    small = np.arange(32, dtype=np.float64)
    angle = 2.0 * np.pi * np.outer(small, small) / 32.0
    slots = np.eye(4)
    slots[3, 3] = 0.0
    cosine, sine = np.kron(slots, np.cos(angle)), np.kron(slots, np.sin(angle))
    rows_inverse = np.block([[cosine, sine], [-sine, cosine]])
    slots[1, 3] = 1.0
    cosine, sine = np.kron(slots, np.cos(angle)), np.kron(slots, np.sin(angle))
    rows_forward = np.block([[cosine, -sine], [sine, cosine]])
    angle = 2.0 * np.pi * np.outer(small, np.tile(small, 4)) / 1024.0
    turn = np.stack([np.cos(angle), np.sin(angle)], axis=1).astype(np.float32)
    return (
        split_table(forward)
        + split_table(inverse)
        + split_table(rows_forward)
        + split_table(rows_inverse)
        + (turn,)
    )


def times(value, angle_index, length, sign):
    real, imag = value
    angle_index = angle_index % length
    if angle_index == 0:
        return value
    angle = 2.0 * np.pi * angle_index / length
    cosine, sine = float(np.cos(angle)), float(sign * np.sin(angle))
    if 4 * angle_index == length or 4 * angle_index == 3 * length:
        return (-imag, real) if sine > 0 else (imag, -real)
    if 2 * angle_index == length:
        return (-real, -imag)
    return (real * cosine - imag * sine, imag * cosine + real * sine)


def plus(first, second):
    return (first[0] + second[0], first[1] + second[1])


def minus(first, second):
    return (first[0] - second[0], first[1] - second[1])


def four(x, sign):
    a, b, c, d = plus(x[0], x[2]), minus(x[0], x[2]), plus(x[1], x[3]), minus(x[1], x[3])
    d = (-d[1], d[0]) if sign > 0 else (d[1], -d[0])
    return [plus(a, c), plus(b, d), minus(a, c), minus(b, d)]


def eight(x, sign):
    even, odd = four(x[0::2], sign), four(x[1::2], sign)
    odd = [odd[0], times(odd[1], 1, 8, sign), times(odd[2], 2, 8, sign), times(odd[3], 3, 8, sign)]
    return [plus(e, o) for e, o in zip(even, odd)] + [minus(e, o) for e, o in zip(even, odd)]


def parts(value):
    high = value.astype(BF16)
    return high, (value - high.astype(F32)).astype(BF16)


def dot(a, b):
    return jnp.dot(a, b, preferred_element_type=F32)


def dot3(a_high, a_low, b_high, b_low):
    return dot(a_high, b_high) + dot(a_high, b_low) + dot(a_low, b_high)


def kernel(
    order_hbm, grain_hbm, phase_hbm, tfh_hbm, tfl_hbm, tih_hbm, til_hbm, bfh_hbm, bfl_hbm, bih_hbm,
    bil_hbm, turn_hbm, mob_s, index_s, stiff_s, eigen_s, macro_s,
    middle, base, outer_in2, final, eig, lame, mob,
    first, grain, phase, tfh, tfl, tih, til, bfh, bfl, bih, bil, turn,
    row_out, row_in, row_out2, row_in2, col_out, col_in, col_out2, col_in2,
    outer_in, lame_in, eig_in,
    strain, eig_t, m1_t, m2_t, green, send1, recv1, send2, recv2, work, both, flat, lxh, lxl,
    load_sem, halo_send, halo_recv, outer_send, outer_recv, core_send, core_recv, all_send, all_recv, meet_sem,
):
    g, r, c = lax.axis_index("grp"), lax.axis_index("row"), lax.axis_index("col")
    inner, outer = g, 1 - g
    mine = jnp.where(c == 0, inner, outer)
    other = 1 - mine
    core_peer = (g, r, 1 - c)
    grp_peer = (1 - g, r, c)
    row_up = (g, (r + ROWS - 1) % ROWS, c)
    row_down = (g, (r + 1) % ROWS, c)

    def remote(source, target, send, recv, device):
        return pltpu.make_async_remote_copy(
            source, target, send, recv, device_id=device, device_id_type=MESH
        )

    loads = [
        pltpu.make_async_copy(grain_hbm, grain, load_sem.at[0]),
        pltpu.make_async_copy(phase_hbm, phase, load_sem.at[1]),
        pltpu.make_async_copy(order_hbm, first.at[:, :, pl.ds(8, 32), :], load_sem.at[2]),
    ]
    pairs = (
        (tfh_hbm, tfh), (tfl_hbm, tfl), (tih_hbm, tih), (til_hbm, til), (bfh_hbm, bfh),
        (bfl_hbm, bfl), (bih_hbm, bih), (bil_hbm, bil), (turn_hbm, turn),
    )
    for place, (source, target) in enumerate(pairs):
        loads.append(pltpu.make_async_copy(source, target, load_sem.at[3 + place]))
    for load in loads:
        load.start()

    barrier = pltpu.get_barrier_semaphore()
    beyond = jnp.where(r % 2 == 1, row_down[1], row_up[1])
    near = [(g, jnp.bitwise_xor(r, 1 << k), c) for k in range(5)]
    for peer in [grp_peer, core_peer, (g, beyond, c)] + near:
        pl.semaphore_signal(barrier, inc=1, device_id=peer, device_id_type=MESH)

    def meet(k):
        if k > 0:
            pl.semaphore_wait(meet_sem.at[k - 1], 1)
        if k < 5:
            pl.semaphore_signal(meet_sem.at[k], inc=1, device_id=near[k], device_id_type=MESH)

    loads[0].wait()
    loads[1].wait()
    for layer in range(2):
        labels = grain[layer]

        def look(k, value):
            return jnp.where(labels == k, mob_s[k], value)

        mob[layer, 8:40, :] = lax.fori_loop(0, 32, look, jnp.zeros((32, 512), F32))
        labels2 = phase[layer]

        def look2(k, values):
            chosen = index_s[k]
            hit = labels2 == k
            return (
                jnp.where(hit, stiff_s[0, chosen], values[0]),
                jnp.where(hit, stiff_s[1, chosen], values[1]),
            )

        empty = jnp.zeros((32, 512), F32)
        lam, shear = lax.fori_loop(0, 8, look2, (empty, empty))
        lame[layer, 0] = lam
        lame[layer, 1] = shear

    lane = lax.broadcasted_iota(jnp.int32, (32, 128), 1)

    def pack(source, rows_to, cols_to):
        def step(i, carry):
            for layer in range(2):
                k = layer * 16 + i
                rows_to[0, k] = source[layer, i, 8:9, :]
                rows_to[1, k] = source[layer, i, 39:40, :]
                cols_to[k] = jnp.where(
                    lane < 64, source[layer, i, 8:40, 0:128], source[layer, i, 8:40, 384:512]
                )
            return carry

        lax.fori_loop(0, 16, step, 0)

    def unpack(target, rows_from):
        def step(i, carry):
            for layer in range(2):
                k = layer * 16 + i
                target[layer, i, 40:41, :] = rows_from[0, k]
                target[layer, i, 7:8, :] = rows_from[1, k]
            return carry

        lax.fori_loop(0, 16, step, 0)

    loads[2].wait()
    pack(first, row_out, col_out)
    for layer in range(2):
        row_out[0, 32 + layer] = mob[layer, 8:9, :]
        row_out[1, 32 + layer] = mob[layer, 39:40, :]
        col_out[32 + layer] = jnp.where(lane < 64, mob[layer, 8:40, 0:128], mob[layer, 8:40, 384:512])

    pl.semaphore_wait(barrier, 8)
    meet(0)

    halo = [
        remote(row_out.at[0], row_in.at[0], halo_send.at[0], halo_recv.at[0], row_up),
        remote(row_out.at[1], row_in.at[1], halo_send.at[1], halo_recv.at[1], row_down),
        remote(col_out, col_in, halo_send.at[2], halo_recv.at[2], core_peer),
    ]
    for copy in halo:
        copy.start()

    def outer_copy(k):
        at = pl.ds(k * CHUNK, CHUNK)
        return remote(
            order_hbm.at[outer, at], outer_in.at[at], outer_send.at[k], outer_recv.at[k], grp_peer
        )

    def outer_copy2(k):
        at = pl.ds(k * CHUNK, CHUNK)
        return remote(
            middle.at[outer, at, pl.ds(8, 32), :], outer_in2.at[at],
            outer_send.at[CHUNKS + k], outer_recv.at[CHUNKS + k], grp_peer,
        )

    for k in range(CHUNKS):
        outer_copy(k).start()
    lame_copy = remote(lame.at[other], lame_in.at[c], core_send.at[0], core_recv.at[0], core_peer)
    lame_copy.start()

    sub16 = lax.broadcasted_iota(jnp.int32, (16, 128), 0)
    lane16 = lax.broadcasted_iota(jnp.int32, (16, 128), 1)
    slot = lane16 // 32
    place = (r % 8) * 16 + sub16
    kind = r // 8
    col_freq = jnp.where(
        kind > 0, kind + 8 * place, jnp.where(place < 64, 8 * place, 4 + 8 * (place - 64))
    )
    col_signed = jnp.where(col_freq >= 512, col_freq - 1024, col_freq).astype(F32)

    def green_step(k1, carry):
        row_freq = k1 + 32 * (lane16 % 32)
        row_signed = jnp.where(row_freq >= 512, row_freq - 1024, row_freq).astype(F32)
        keeper = jnp.where((row_freq != 512) & (col_freq != 512), 1.0, 0.0)
        radius = row_signed * row_signed + col_signed * col_signed
        inverse = keeper * lax.rsqrt(jnp.where(radius > 0, radius, 1.0))
        n1, n2 = row_signed * inverse, col_signed * inverse
        a, b, d = n1 * n1, n2 * n2, n1 * n2
        own = jnp.where(
            slot == 0,
            a / SHEAR_REF - BETA_REF * a * a,
            jnp.where(
                slot == 2,
                b / SHEAR_REF - BETA_REF * b * b,
                0.5 * (a + b) / SHEAR_REF - 2.0 * BETA_REF * d * d,
            ),
        )
        toward_rr = 0.5 * d / SHEAR_REF - BETA_REF * a * d
        toward_cc = 0.5 * d / SHEAR_REF - BETA_REF * b * d
        across = -BETA_REF * d * d
        green[0, k1] = own
        green[1, k1] = jnp.where(
            slot == 1, toward_cc, jnp.where(slot == 3, toward_rr, across)
        )
        green[2, k1] = jnp.where(
            slot == 0,
            2.0 * toward_rr,
            jnp.where(slot == 1, toward_rr, jnp.where(slot == 2, 2.0 * toward_cc, toward_cc)),
        )
        return carry

    meet(1)
    lax.fori_loop(0, 32, green_step, 0)
    meet(2)

    def to_columns(target, half, slots):
        for j in range(4):
            block = jnp.concatenate([field[:, 128 * j : 128 * j + 128] for field in slots], axis=0)
            target[4 * half + j] = block.T

    def stiff_columns(half, lam, shear):
        double = 2.0 * shear
        straight = lam + double
        empty = jnp.zeros_like(lam)
        to_columns(m1_t, half, (straight, double, straight, empty))
        to_columns(m2_t, half, (lam, empty, lam, empty))

    stiff_columns(c, lame[mine, 0], lame[mine, 1])

    for copy in halo:
        copy.wait_recv()
    meet(3)
    unpack(first, row_in)
    for layer in range(2):
        mob[layer, 40:41, :] = row_in[0, 32 + layer]
        mob[layer, 7:8, :] = row_in[1, 32 + layer]

    def update(source, cols, layer, write):
        for s in range(4):
            r0, r1 = 8 + 8 * s, 8 * s
            m = mob[layer, r0 : r0 + 8, :]
            edge = jnp.concatenate([col_in[32 + layer, r1 : r1 + 8, :], m], axis=1)
            w_up = 0.05 * (m + mob[layer, r0 - 1 : r0 + 7, :])
            w_down = 0.05 * (m + mob[layer, r0 + 1 : r0 + 9, :])
            w_left = 0.05 * (m + pltpu.roll(edge, 1, 1)[:, 128:])
            w_right = 0.05 * (m + pltpu.roll(edge, 639, 1)[:, 128:])
            total = jnp.zeros((8, 512), F32)
            for i in range(16):
                v = source[layer, i, r0 : r0 + 8, :]
                total = total + v * v
            c0 = 1.0 - (w_up + w_down + w_left + w_right) - 0.3 * m * total
            c1 = 0.2 * m
            m05 = 0.05 * m

            def step(n, carry):
                for i4 in range(UNROLL):
                    i = n * UNROLL + i4
                    v = source[layer, i, r0 : r0 + 8, :]
                    e = jnp.concatenate([cols[layer * 16 + i, r1 : r1 + 8, :], v], axis=1)
                    write(
                        layer,
                        i,
                        s,
                        v * (c0 + c1 * v * v)
                        + w_up * source[layer, i, r0 - 1 : r0 + 7, :]
                        + w_down * source[layer, i, r0 + 1 : r0 + 9, :]
                        + w_left * pltpu.roll(e, 1, 1)[:, 128:]
                        + w_right * pltpu.roll(e, 639, 1)[:, 128:]
                        + m05 * source[1 - layer, i, r0 : r0 + 8, :],
                    )
                return carry

            lax.fori_loop(0, 16 // UNROLL, step, 0)

    def to_middle(layer, i, s, value):
        middle[layer, i, 8 + 8 * s : 16 + 8 * s, :] = value

    def to_base(layer, i, s, value):
        base[layer, i, 8 * s : 8 * s + 8, :] = value

    update(first, col_in, inner, to_middle)
    meet(4)
    for s in range(4):
        totals = [jnp.zeros((8, 512), F32)] * 3
        for i in range(16):
            v = middle[inner, i, 8 + 8 * s : 16 + 8 * s, :]
            v = v * v
            totals = [totals[k] + v * eigen_s[k, i] for k in range(3)]
        for k in range(3):
            eig[inner, k, 8 * s : 8 * s + 8, :] = totals[k]
            eig[outer, k, 8 * s : 8 * s + 8, :] = jnp.zeros((8, 512), F32)
    eig_copy = remote(eig.at[other], eig_in.at[c], core_send.at[1], core_recv.at[1], core_peer)

    @pl.when(c == 1)
    def _():
        eig_copy.start()

    meet(5)
    update(first, col_in, outer, to_middle)

    lame_copy.wait_recv()
    stiff_columns(1 - c, lame_in[1 - c, 0], lame_in[1 - c, 1])

    lane1 = lax.broadcasted_iota(jnp.int32, (128, 128), 1)
    start = jnp.where(
        lane1 < 32, macro_s[0], jnp.where((lane1 >= 64) & (lane1 < 96), macro_s[1], macro_s[2])
    )
    for n1 in range(8):
        strain[n1] = start

    even16 = (lane16 // 32) % 2 == 0
    lane_all = lax.broadcasted_iota(jnp.int32, (128, 128), 1)
    even = (lane_all // 32) % 2 == 0

    def product(table_high, table_low, kind):
        wide = dot(table_high[kind], both[kind])
        return wide[:, 0:128] + wide[:, 128:256] + dot(table_low[kind], both[kind, :, 0:128])

    def pack3(a):
        slot = lax.broadcasted_iota(jnp.int32, a[0].shape, 1) // 32
        return [jnp.where(slot == 3, pltpu.roll(a[3], 96 - 32 * k, 1), a[k]) for k in range(3)]

    def unpack3(p):
        slot = lax.broadcasted_iota(jnp.int32, p[0].shape, 1) // 32
        x, y, z = (pltpu.roll(p[k], 32 + 32 * k, 1) for k in range(3))
        return list(p) + [jnp.where(slot == 0, x, jnp.where(slot == 1, y, z))]

    def columns_forward(it):
        def stage(t, carry):
            rows = pl.ds(pl.multiple_of(t * 16, 16), 16)
            x = []
            for n1 in range(8):
                d = strain[n1, rows, :] - eig_t[n1, rows, :]
                x.append(m1_t[n1, rows, :] * d + m2_t[n1, rows, :] * pltpu.roll(d, 64, 1))
            s04, d04, s26, d26 = x[0] + x[4], x[0] - x[4], x[2] + x[6], x[2] - x[6]
            s15, d15, s37, d37 = x[1] + x[5], x[1] - x[5], x[3] + x[7], x[3] - x[7]
            evens, odds = s04 + s26, s15 + s37
            turned = HALF * (d15 - d37)
            summed = HALF * (d15 + d37)
            values = (
                (evens + odds, evens - odds),
                (d04 + turned, -d26 - summed),
                (s04 - s26, s37 - s15),
                (d04 - turned, d26 - summed),
            )
            rows2 = pl.ds(pl.multiple_of(128 + t * 16, 16), 16)
            for kind, (real, imag) in enumerate(values):
                both[kind, rows, 0:128], both[kind, rows, 128:256] = parts(real)
                both[kind, rows2, 0:128], both[kind, rows2, 128:256] = parts(imag)
            return carry

        lax.fori_loop(0, 8, stage, 0)

        def forward(kk, carry):
            kind = (r // 8 + kk) % 4
            result = product(tfh, tfl, kind).reshape(2, 8, 2, 8, 128)
            packed = pack3([result[n // 2, :, n % 2].reshape(64, 128) for n in range(4)])
            for n in range(3):
                send1[it, pl.ds(8 * kind, 8), n] = packed[n].reshape(8, 8, 128)

            def post(j, carry):
                peer = 8 * kind + (r % 8 + j) % 8

                @pl.when(peer != r)
                def _():
                    remote(
                        send1.at[it, peer], recv1.at[it, r],
                        all_send.at[2 * it], all_recv.at[2 * it], (g, peer, c),
                    ).start()

                return carry

            lax.fori_loop(0, 8, post, 0)
            return carry

        lax.fori_loop(0, 4, forward, 0)
        pltpu.make_async_copy(send1.at[it, r], recv1.at[it, r], all_recv.at[2 * it]).start()

    def columns_start():
        for load in loads[3:]:
            load.wait()
        eig_copy.wait_recv()
        for half, values in ((c, eig.at[mine]), (1 - c, eig_in.at[1 - c])):
            fields = [values[k] for k in range(3)]
            to_columns(eig_t, half, (fields[0], fields[2], fields[1], fields[2]))
        columns_forward(0)

    @pl.when(c == 0)
    def _():
        columns_start()

    for k in range(CHUNKS):
        outer_copy(k).wait_recv()

        def add(s, carry):
            at, at2 = pl.ds(pl.multiple_of(8 + 8 * s, 8), 8), pl.ds(pl.multiple_of(8 * s, 8), 8)
            m05 = 0.05 * mob[outer, at, :]
            totals = [eig[outer, n, at2, :] for n in range(3)]
            for i in range(CHUNK):
                j = k * CHUNK + i
                v = middle[outer, j, at, :] + m05 * outer_in[j, at2, :]
                middle[outer, j, at, :] = v
                v = v * v
                totals = [totals[n] + v * eigen_s[n, j] for n in range(3)]
            for n in range(3):
                eig[outer, n, at2, :] = totals[n]
            return carry

        lax.fori_loop(0, 4, add, 0)
        if k < EARLY:
            outer_copy2(k).start()

    halo2 = [
        remote(row_out2.at[0], row_in2.at[0], halo_send.at[3], halo_recv.at[3], row_up),
        remote(row_out2.at[1], row_in2.at[1], halo_send.at[4], halo_recv.at[4], row_down),
        remote(col_out2, col_in2, halo_send.at[5], halo_recv.at[5], core_peer),
    ]

    @pl.when(c == 0)
    def _():
        eig_copy.start()

    @pl.when(c == 1)
    def _():
        columns_start()

    def sweep(it, carry):
        outer_copy2(2 * it + 1).start()

        @pl.when(it == 0)
        def _():
            pack(middle, row_out2, col_out2)
            for copy in halo2:
                copy.start()

        pltpu.make_async_copy(recv1.at[it], recv1.at[it], all_recv.at[2 * it]).wait()

        for b in range(8):
            x = []
            for a in range(4):
                v = unpack3([recv1[it, 8 * a + b, n] for n in range(3)])
                x.append((jnp.concatenate(v[0:2], axis=0), jnp.concatenate(v[2:4], axis=0)))
            y = four(x, -1)
            for ka in range(4):
                work[ka, b, 0], work[ka, b, 1] = times(y[ka], b * ka, 32, -1)
        for ka in range(4):
            y = eight([(work[ka, b, 0], work[ka, b, 1]) for b in range(8)], -1)
            for kb in range(8):
                k1 = ka + 4 * kb
                cosine, sine = turn[k1, 0:1, :], turn[k1, 1:2, :]
                real, imag = y[kb]
                z = (real * cosine + imag * sine, imag * cosine - real * sine)
                for half in range(2):
                    at = (slice(16 * k1, 16 * k1 + 16), slice(128 * half, 128 * half + 128))
                    lxh[at], lxl[at] = parts(z[half])

        for q in range(4):
            rows = slice(q * 128, q * 128 + 128)
            spectrum = dot3(lxh[rows, :], lxl[rows, :], bfh[...], bfl[...])
            group = pl.ds(8 * q, 8)
            g0 = green[0, group].reshape(128, 128)
            g1 = green[1, group].reshape(128, 128)
            g2 = green[2, group].reshape(128, 128)
            pieces = []
            for half in range(2):
                s = spectrum[:, 128 * half : 128 * half + 128]
                z = jnp.where(even, pltpu.roll(s, 64, 1), pltpu.roll(s, 96, 1))
                pieces.append(parts(g0 * s + g1 * z + g2 * pltpu.roll(s, 32, 1)))
            oh = jnp.concatenate([pieces[0][0], pieces[1][0]], axis=1)
            ol = jnp.concatenate([pieces[0][1], pieces[1][1]], axis=1)
            back = dot3(oh, ol, bih[...], bil[...])
            for j in range(8):
                k1 = 8 * q + j
                cosine, sine = turn[k1, 0:1, :], turn[k1, 1:2, :]
                real, imag = back[16 * j : 16 * j + 16, 0:128], back[16 * j : 16 * j + 16, 128:256]
                flat[k1, 0] = real * cosine - imag * sine
                flat[k1, 1] = imag * cosine + real * sine

        for ka in range(4):
            y = eight([(flat[ka + 4 * kb, 0], flat[ka + 4 * kb, 1]) for kb in range(8)], 1)
            for b in range(8):
                work[ka, b, 0], work[ka, b, 1] = times(y[b], b * ka, 32, 1)

        def backward(bb, carry):
            b = (r + bb) % 8
            y = four([(work[ka, b, 0], work[ka, b, 1]) for ka in range(4)], 1)
            for a in range(4):
                packed = pack3([y[a][n // 2][8 * (n % 2) : 8 * (n % 2) + 8] for n in range(4)])
                for n in range(3):
                    send2[it, 8 * a + b, n] = packed[n]

            def post(j, carry):
                peer = 8 * ((r // 8 + j) % 4) + b

                @pl.when(peer != r)
                def _():
                    remote(
                        send2.at[it, peer], recv2.at[it, r],
                        all_send.at[2 * it + 1], all_recv.at[2 * it + 1], (g, peer, c),
                    ).start()

                return carry

            lax.fori_loop(0, 4, post, 0)
            return carry

        lax.fori_loop(0, 8, backward, 0)
        pltpu.make_async_copy(send2.at[it, r], recv2.at[it, r], all_recv.at[2 * it + 1]).start()

        @pl.when(it == 0)
        def _():
            outer_copy2(2).start()
            for copy in halo2:
                copy.wait_recv()
            unpack(middle, row_in2)

        update(middle, col_in2, it, to_base)
        pltpu.make_async_copy(recv2.at[it], recv2.at[it], all_recv.at[2 * it + 1]).wait()

        for kind in range(4):
            group = pl.ds(8 * kind, 8)
            v = unpack3([recv2[it, group, n].reshape(64, 128) for n in range(3)])
            for half in range(2):
                at = slice(128 * half, 128 * half + 128)
                pair = [v[2 * half + n].reshape(8, 1, 8, 128) for n in range(2)]
                value = parts(jnp.concatenate(pair, axis=1).reshape(128, 128))
                both[kind, at, 0:128], both[kind, at, 128:256] = value
            result = product(tih, til, kind)
            flat[pl.ds(8 * kind, 8), 0] = result[0:128].reshape(8, 16, 128)
            flat[pl.ds(8 * kind, 8), 1] = result[128:256].reshape(8, 16, 128)

        def unstage(t, carry):
            rows = pl.ds(pl.multiple_of(t * 16, 16), 16)
            z0, z4 = flat[t, 0], flat[t, 1]
            a1, b1 = flat[8 + t, 0], flat[8 + t, 1]
            a2, b2 = flat[16 + t, 0], flat[16 + t, 1]
            a3, b3 = flat[24 + t, 0], flat[24 + t, 1]
            zp, zm = z0 + z4, z0 - z4
            sa, db, da, sb = a1 + a3, b3 - b1, a1 - a3, b1 + b3
            p1, p2 = HALF * (da - sb), HALF * (da + sb)
            values = (
                zp + a2 + sa,
                zm - b2 + p1,
                zp - a2 + db,
                zm + b2 - p2,
                zp + a2 - sa,
                zm - b2 - p1,
                zp - a2 - db,
                zm + b2 + p2,
            )
            for n1 in range(8):
                strain[n1, rows, :] -= values[n1]
            return carry

        lax.fori_loop(0, 8, unstage, 0)

        @pl.when(it < ITERS - 1)
        def _():
            columns_forward(it + 1)

        return carry

    lax.fori_loop(0, ITERS, sweep, 0)

    def to_rows(half, layer, target):
        for j in range(4):
            block = strain[4 * half + j].T
            lanes = slice(128 * j, 128 * j + 128)
            target[layer, 0, :, lanes] = block[0:32]
            target[layer, 1, :, lanes] = block[64:96]
            target[layer, 2, :, lanes] = block[32:64]

    to_rows(1 - c, 0, eig_in)
    final_copy = remote(eig_in.at[0], final.at[mine], core_send.at[2], core_recv.at[2], core_peer)
    final_copy.start()
    to_rows(c, mine, final)
    remote(eig_in.at[0], final.at[other], core_send.at[2], core_recv.at[2], core_peer).wait_recv()
    for k in range(CHUNKS):
        outer_copy2(k).wait_recv()
    for copy in halo + halo2 + [lame_copy, eig_copy, final_copy]:
        copy.wait_send()
    for k in range(CHUNKS):
        outer_copy(k).wait_send()
        outer_copy2(k).wait_send()
    for it in range(ITERS):
        for sent, sem in ((send1, 2 * it), (send2, 2 * it + 1)):
            whole = sent.at[it, pl.ds(0, ROWS - 1)]
            pltpu.make_async_copy(whole, whole, all_send.at[sem]).wait()


def finish(
    middle, base, outer_in2, final, eig, lame, mob, eigen_s, out_hbm, strain_hbm, out, sem
):
    g = lax.axis_index("grp")
    strain_copy = pltpu.make_async_copy(final, strain_hbm, sem.at[8])
    strain_copy.start()
    for place in range(2):
        layer = g if place == 0 else 1 - g

        def at(s, carry):
            rows = pl.ds(pl.multiple_of(8 * s, 8), 8)
            rows2 = pl.ds(pl.multiple_of(8 + 8 * s, 8), 8)
            d = [final[layer, k, rows, :] - eig[layer, k, rows, :] for k in range(3)]
            lam, double = lame[layer, 0, rows, :], 2.0 * lame[layer, 1, rows, :]
            m = mob[layer, rows2, :]
            m05, c1 = 0.05 * m, 0.2 * m
            push = (
                c1 * ((lam + double) * d[0] + lam * d[1]),
                c1 * (lam * d[0] + (lam + double) * d[1]),
                c1 * (2.0 * (double * d[2])),
            )
            for i in range(16):
                v = middle[layer, i, rows2, :]
                value = base[layer, i, rows, :] + v * (
                    push[0] * eigen_s[0, i] + push[1] * eigen_s[1, i] + push[2] * eigen_s[2, i]
                )
                if place == 1:
                    value = value + m05 * outer_in2[i, rows, :]
                out[layer, i, rows, :] = value
            pltpu.make_async_copy(
                out.at[layer, :, rows, :], out_hbm.at[layer, :, rows, :], sem.at[4 * place + s]
            ).start()
            return carry

        lax.fori_loop(0, 4, at, 0)
    for place in range(2):
        layer = g if place == 0 else 1 - g
        for s in range(4):
            rows = pl.ds(8 * s, 8)
            pltpu.make_async_copy(
                out.at[layer, :, rows, :], out_hbm.at[layer, :, rows, :], sem.at[4 * place + s]
            ).wait()
    strain_copy.wait()


def body(order, grain, phase, mobility, index, stiff, eigen, macro):
    constants = tables()
    any_spec = pl.BlockSpec(memory_space=pl.ANY)
    smem = pl.BlockSpec(memory_space=pltpu.SMEM)
    vmem = pl.BlockSpec(memory_space=pltpu.VMEM)
    big = (2, 16, 48, 512)
    every = (ITERS, ROWS, 3, 8, 128)
    columns = (8, 128, 128)
    kept = (
        big, (2, 16, 32, 512), (16, 32, 512), (2, 3, 32, 512), (2, 3, 32, 512), (2, 2, 32, 512),
        (2, 48, 512),
    )
    values = pl.pallas_call(
        kernel,
        out_shape=tuple(pltpu.VMEM(shape, F32) for shape in kept),
        in_specs=[any_spec] * 12 + [smem] * 5,
        out_specs=(vmem,) * len(kept),
        scratch_shapes=[
            pltpu.VMEM(big, F32),
            pltpu.VMEM((2, 32, 512), jnp.int32),
            pltpu.VMEM((2, 32, 512), jnp.int32),
        ]
        + [pltpu.VMEM((4, 256, 256), BF16)] * 4
        + [pltpu.VMEM((256, 256), BF16)] * 4
        + [pltpu.VMEM((32, 2, 128), F32)]
        + [
            pltpu.VMEM((2, 34, 1, 512), F32),
            pltpu.VMEM((2, 34, 1, 512), F32),
            pltpu.VMEM((2, 32, 1, 512), F32),
            pltpu.VMEM((2, 32, 1, 512), F32),
            pltpu.VMEM((34, 32, 128), F32),
            pltpu.VMEM((34, 32, 128), F32),
            pltpu.VMEM((32, 32, 128), F32),
            pltpu.VMEM((32, 32, 128), F32),
            pltpu.VMEM((16, 32, 512), F32),
            pltpu.VMEM((2, 2, 32, 512), F32),
            pltpu.VMEM((2, 3, 32, 512), F32),
        ]
        + [pltpu.VMEM(columns, F32)] * 4
        + [pltpu.VMEM((3, 32, 16, 128), F32)]
        + [pltpu.VMEM(every, F32)] * 4
        + [pltpu.VMEM((4, 8, 2, 16, 128), F32)]
        + [pltpu.VMEM((4, 256, 256), BF16)]
        + [pltpu.VMEM((32, 2, 16, 128), F32)]
        + [pltpu.VMEM((512, 256), BF16)] * 2
        + [
            pltpu.SemaphoreType.DMA((n,))
            for n in (12, 6, 6, 2 * CHUNKS, 2 * CHUNKS, 3, 3, 2 * ITERS, 2 * ITERS)
        ]
        + [pltpu.SemaphoreType.REGULAR((5,))],
        compiler_params=pltpu.CompilerParams(
            collective_id=0, has_side_effects=True, vmem_limit_bytes=48 * 1024 * 1024
        ),
        name="step",
    )(order, grain, phase, *[jnp.asarray(t) for t in constants], mobility, index, stiff.T, eigen.T, macro)
    return pl.pallas_call(
        finish,
        out_shape=(
            jax.ShapeDtypeStruct((2, 16, 32, 512), F32),
            jax.ShapeDtypeStruct((2, 3, 32, 512), F32),
        ),
        in_specs=[vmem] * len(kept) + [smem],
        out_specs=(any_spec, any_spec),
        scratch_shapes=[pltpu.VMEM((2, 16, 32, 512), F32), pltpu.SemaphoreType.DMA((9,))],
        compiler_params=pltpu.CompilerParams(vmem_limit_bytes=6 * 1024 * 1024),
        name="finish",
    )(*values, eigen.T)


def solution(mesh):
    fields = P("grp", None, "row", "col")
    labels = P("grp", "row", "col")
    return jax.shard_map(
        body,
        mesh=mesh,
        in_specs=(fields, labels, labels, P(), P(), P(), P(), P()),
        out_specs=(fields, fields),
        check_vma=False,
    )
```

```python
import jax
import jax.numpy as jnp
import ml_dtypes
import numpy as np
from jax import lax
from jax.experimental import pallas as pl
from jax.experimental.pallas import tpu as pltpu
from jax.sharding import PartitionSpec as P

MESH = pl.DeviceIdType.MESH
ITERS = 2
ROWS = 32
HALF = 0.7071067811865476
LAMBDA_REF = 1.25
SHEAR_REF = 1.25
BETA_REF = (LAMBDA_REF + SHEAR_REF) / (SHEAR_REF * (LAMBDA_REF + 2.0 * SHEAR_REF))
F32 = jnp.float32
BF16 = jnp.bfloat16
CHUNK = 4
CHUNKS = 16 // CHUNK
UNROLL = 4
EARLY = 1


def split_table(values):
    high = values.astype(np.float32).astype(ml_dtypes.bfloat16)
    low = (values - high.astype(np.float64)).astype(np.float32).astype(ml_dtypes.bfloat16)
    return high, low


def tables():
    place = np.arange(128, dtype=np.float64)
    forward = np.zeros((4, 256, 256))
    inverse = np.zeros((4, 256, 256))
    scale = 1.0 / 1048576.0
    half = np.arange(64, dtype=np.float64)
    for first, base in ((0, 0), (64, 4)):
        angle = 2.0 * np.pi * np.outer(base + 8 * half, place) / 1024.0
        source = slice(0, 128) if base == 0 else slice(128, 256)
        forward[0, first : first + 64, source] = np.cos(angle)
        forward[0, 128 + first : 192 + first, source] = -np.sin(angle)
        weight = np.full((64, 1), 2.0 * scale)
        if base == 0:
            weight[0] = scale
        inverse[0, source, first : first + 64] = (weight * np.cos(angle)).T
        inverse[0, source, 128 + first : 192 + first] = (-weight * np.sin(angle)).T
    for kind in (1, 2, 3):
        angle = 2.0 * np.pi * np.outer(kind + 8 * place, place) / 1024.0
        cosine, sine = np.cos(angle), np.sin(angle)
        forward[kind] = np.block([[cosine, sine], [-sine, cosine]])
        inverse[kind] = 2.0 * scale * np.block([[cosine.T, -sine.T], [sine.T, cosine.T]])
    small = np.arange(32, dtype=np.float64)
    angle = 2.0 * np.pi * np.outer(small, small) / 32.0
    slots = np.eye(4)
    slots[3, 3] = 0.0
    cosine, sine = np.kron(slots, np.cos(angle)), np.kron(slots, np.sin(angle))
    rows_inverse = np.block([[cosine, sine], [-sine, cosine]])
    slots[1, 3] = 1.0
    cosine, sine = np.kron(slots, np.cos(angle)), np.kron(slots, np.sin(angle))
    rows_forward = np.block([[cosine, -sine], [sine, cosine]])
    angle = 2.0 * np.pi * np.outer(small, np.tile(small, 4)) / 1024.0
    turn = np.stack([np.cos(angle), np.sin(angle)], axis=1).astype(np.float32)
    return (
        split_table(forward)
        + split_table(inverse)
        + split_table(rows_forward)
        + split_table(rows_inverse)
        + (turn,)
    )


def times(value, angle_index, length, sign):
    real, imag = value
    angle_index = angle_index % length
    if angle_index == 0:
        return value
    angle = 2.0 * np.pi * angle_index / length
    cosine, sine = float(np.cos(angle)), float(sign * np.sin(angle))
    if 4 * angle_index == length or 4 * angle_index == 3 * length:
        return (-imag, real) if sine > 0 else (imag, -real)
    if 2 * angle_index == length:
        return (-real, -imag)
    return (real * cosine - imag * sine, imag * cosine + real * sine)


def plus(first, second):
    return (first[0] + second[0], first[1] + second[1])


def minus(first, second):
    return (first[0] - second[0], first[1] - second[1])


def four(x, sign):
    a, b, c, d = plus(x[0], x[2]), minus(x[0], x[2]), plus(x[1], x[3]), minus(x[1], x[3])
    d = (-d[1], d[0]) if sign > 0 else (d[1], -d[0])
    return [plus(a, c), plus(b, d), minus(a, c), minus(b, d)]


def eight(x, sign):
    even, odd = four(x[0::2], sign), four(x[1::2], sign)
    odd = [odd[0], times(odd[1], 1, 8, sign), times(odd[2], 2, 8, sign), times(odd[3], 3, 8, sign)]
    return [plus(e, o) for e, o in zip(even, odd)] + [minus(e, o) for e, o in zip(even, odd)]


def parts(value):
    high = value.astype(BF16)
    return high, (value - high.astype(F32)).astype(BF16)


def dot(a, b):
    return jnp.dot(a, b, preferred_element_type=F32)


def dot3(a_high, a_low, b_high, b_low):
    return dot(a_high, b_high) + dot(a_high, b_low) + dot(a_low, b_high)


def kernel(
    order_hbm, grain_hbm, phase_hbm, tfh_hbm, tfl_hbm, tih_hbm, til_hbm, bfh_hbm, bfl_hbm, bih_hbm,
    bil_hbm, turn_hbm, mob_s, index_s, stiff_s, eigen_s, macro_s,
    middle, base, outer_in2, final, eig, lame, mob,
    first, grain, phase, tfh, tfl, tih, til, bfh, bfl, bih, bil, turn,
    row_out, row_in, row_out2, row_in2, col_out, col_in, col_out2, col_in2,
    outer_in, lame_in, eig_in,
    strain, eig_t, m1_t, m2_t, green, send1, recv1, send2, recv2, work, both, flat, lxh, lxl,
    load_sem, halo_send, halo_recv, outer_send, outer_recv, core_send, core_recv, all_send, all_recv, meet_sem,
):
    g, r, c = lax.axis_index("grp"), lax.axis_index("row"), lax.axis_index("col")
    inner, outer = g, 1 - g
    mine = jnp.where(c == 0, inner, outer)
    other = 1 - mine
    core_peer = (g, r, 1 - c)
    grp_peer = (1 - g, r, c)
    row_up = (g, (r + ROWS - 1) % ROWS, c)
    row_down = (g, (r + 1) % ROWS, c)

    def remote(source, target, send, recv, device):
        return pltpu.make_async_remote_copy(
            source, target, send, recv, device_id=device, device_id_type=MESH
        )

    loads = [
        pltpu.make_async_copy(grain_hbm, grain, load_sem.at[0]),
        pltpu.make_async_copy(phase_hbm, phase, load_sem.at[1]),
        pltpu.make_async_copy(order_hbm, first.at[:, :, pl.ds(8, 32), :], load_sem.at[2]),
    ]
    pairs = (
        (tfh_hbm, tfh), (tfl_hbm, tfl), (tih_hbm, tih), (til_hbm, til), (bfh_hbm, bfh),
        (bfl_hbm, bfl), (bih_hbm, bih), (bil_hbm, bil), (turn_hbm, turn),
    )
    for place, (source, target) in enumerate(pairs):
        loads.append(pltpu.make_async_copy(source, target, load_sem.at[3 + place]))
    for load in loads:
        load.start()

    barrier = pltpu.get_barrier_semaphore()
    beyond = jnp.where(r % 2 == 1, row_down[1], row_up[1])
    near = [(g, jnp.bitwise_xor(r, 1 << k), c) for k in range(5)]
    for peer in [grp_peer, core_peer, (g, beyond, c)] + near:
        pl.semaphore_signal(barrier, inc=1, device_id=peer, device_id_type=MESH)

    def meet(k):
        if k > 0:
            pl.semaphore_wait(meet_sem.at[k - 1], 1)
        if k < 5:
            pl.semaphore_signal(meet_sem.at[k], inc=1, device_id=near[k], device_id_type=MESH)

    loads[0].wait()
    loads[1].wait()
    for layer in range(2):
        labels = grain[layer]

        def look(k, value):
            return jnp.where(labels == k, mob_s[k], value)

        mob[layer, 8:40, :] = lax.fori_loop(0, 32, look, jnp.zeros((32, 512), F32))
        labels2 = phase[layer]

        def look2(k, values):
            chosen = index_s[k]
            hit = labels2 == k
            return (
                jnp.where(hit, stiff_s[0, chosen], values[0]),
                jnp.where(hit, stiff_s[1, chosen], values[1]),
            )

        empty = jnp.zeros((32, 512), F32)
        lam, shear = lax.fori_loop(0, 8, look2, (empty, empty))
        lame[layer, 0] = lam
        lame[layer, 1] = shear

    lane = lax.broadcasted_iota(jnp.int32, (32, 128), 1)

    def pack(source, rows_to, cols_to):
        def step(i, carry):
            for layer in range(2):
                k = layer * 16 + i
                rows_to[0, k] = source[layer, i, 8:9, :]
                rows_to[1, k] = source[layer, i, 39:40, :]
                cols_to[k] = jnp.where(
                    lane < 64, source[layer, i, 8:40, 0:128], source[layer, i, 8:40, 384:512]
                )
            return carry

        lax.fori_loop(0, 16, step, 0)

    def unpack(target, rows_from):
        def step(i, carry):
            for layer in range(2):
                k = layer * 16 + i
                target[layer, i, 40:41, :] = rows_from[0, k]
                target[layer, i, 7:8, :] = rows_from[1, k]
            return carry

        lax.fori_loop(0, 16, step, 0)

    loads[2].wait()
    pack(first, row_out, col_out)
    for layer in range(2):
        row_out[0, 32 + layer] = mob[layer, 8:9, :]
        row_out[1, 32 + layer] = mob[layer, 39:40, :]
        col_out[32 + layer] = jnp.where(lane < 64, mob[layer, 8:40, 0:128], mob[layer, 8:40, 384:512])

    pl.semaphore_wait(barrier, 8)
    meet(0)

    halo = [
        remote(row_out.at[0], row_in.at[0], halo_send.at[0], halo_recv.at[0], row_up),
        remote(row_out.at[1], row_in.at[1], halo_send.at[1], halo_recv.at[1], row_down),
        remote(col_out, col_in, halo_send.at[2], halo_recv.at[2], core_peer),
    ]
    for copy in halo:
        copy.start()

    def outer_copy(k):
        at = pl.ds(k * CHUNK, CHUNK)
        return remote(
            order_hbm.at[outer, at], outer_in.at[at], outer_send.at[k], outer_recv.at[k], grp_peer
        )

    def outer_copy2(k):
        at = pl.ds(k * CHUNK, CHUNK)
        return remote(
            middle.at[outer, at, pl.ds(8, 32), :], outer_in2.at[at],
            outer_send.at[CHUNKS + k], outer_recv.at[CHUNKS + k], grp_peer,
        )

    for k in range(CHUNKS):
        outer_copy(k).start()
    lame_copy = remote(lame.at[other], lame_in.at[c], core_send.at[0], core_recv.at[0], core_peer)
    lame_copy.start()

    sub16 = lax.broadcasted_iota(jnp.int32, (16, 128), 0)
    lane16 = lax.broadcasted_iota(jnp.int32, (16, 128), 1)
    slot = lane16 // 32
    place = (r % 8) * 16 + sub16
    kind = r // 8
    col_freq = jnp.where(
        kind > 0, kind + 8 * place, jnp.where(place < 64, 8 * place, 4 + 8 * (place - 64))
    )
    col_signed = jnp.where(col_freq >= 512, col_freq - 1024, col_freq).astype(F32)

    def green_step(k1, carry):
        row_freq = k1 + 32 * (lane16 % 32)
        row_signed = jnp.where(row_freq >= 512, row_freq - 1024, row_freq).astype(F32)
        keeper = jnp.where((row_freq != 512) & (col_freq != 512), 1.0, 0.0)
        radius = row_signed * row_signed + col_signed * col_signed
        inverse = keeper * lax.rsqrt(jnp.where(radius > 0, radius, 1.0))
        n1, n2 = row_signed * inverse, col_signed * inverse
        a, b, d = n1 * n1, n2 * n2, n1 * n2
        own = jnp.where(
            slot == 0,
            a / SHEAR_REF - BETA_REF * a * a,
            jnp.where(
                slot == 2,
                b / SHEAR_REF - BETA_REF * b * b,
                0.5 * (a + b) / SHEAR_REF - 2.0 * BETA_REF * d * d,
            ),
        )
        toward_rr = 0.5 * d / SHEAR_REF - BETA_REF * a * d
        toward_cc = 0.5 * d / SHEAR_REF - BETA_REF * b * d
        across = -BETA_REF * d * d
        green[0, k1] = own
        green[1, k1] = jnp.where(
            slot == 1, toward_cc, jnp.where(slot == 3, toward_rr, across)
        )
        green[2, k1] = jnp.where(
            slot == 0,
            2.0 * toward_rr,
            jnp.where(slot == 1, toward_rr, jnp.where(slot == 2, 2.0 * toward_cc, toward_cc)),
        )
        return carry

    meet(1)
    lax.fori_loop(0, 32, green_step, 0)
    meet(2)

    def to_columns(target, half, slots):
        for j in range(4):
            block = jnp.concatenate([field[:, 128 * j : 128 * j + 128] for field in slots], axis=0)
            target[4 * half + j] = block.T

    def stiff_columns(half, lam, shear):
        double = 2.0 * shear
        straight = lam + double
        empty = jnp.zeros_like(lam)
        to_columns(m1_t, half, (straight, double, straight, empty))
        to_columns(m2_t, half, (lam, empty, lam, empty))

    stiff_columns(c, lame[mine, 0], lame[mine, 1])

    for copy in halo:
        copy.wait_recv()
    meet(3)
    unpack(first, row_in)
    for layer in range(2):
        mob[layer, 40:41, :] = row_in[0, 32 + layer]
        mob[layer, 7:8, :] = row_in[1, 32 + layer]

    def update(source, cols, layer, write):
        for s in range(4):
            r0, r1 = 8 + 8 * s, 8 * s
            m = mob[layer, r0 : r0 + 8, :]
            edge = jnp.concatenate([col_in[32 + layer, r1 : r1 + 8, :], m], axis=1)
            w_up = 0.05 * (m + mob[layer, r0 - 1 : r0 + 7, :])
            w_down = 0.05 * (m + mob[layer, r0 + 1 : r0 + 9, :])
            w_left = 0.05 * (m + pltpu.roll(edge, 1, 1)[:, 128:])
            w_right = 0.05 * (m + pltpu.roll(edge, 639, 1)[:, 128:])
            total = jnp.zeros((8, 512), F32)
            for i in range(16):
                v = source[layer, i, r0 : r0 + 8, :]
                total = total + v * v
            c0 = 1.0 - (w_up + w_down + w_left + w_right) - 0.3 * m * total
            c1 = 0.2 * m
            m05 = 0.05 * m

            def step(n, carry):
                for i4 in range(UNROLL):
                    i = n * UNROLL + i4
                    v = source[layer, i, r0 : r0 + 8, :]
                    e = jnp.concatenate([cols[layer * 16 + i, r1 : r1 + 8, :], v], axis=1)
                    write(
                        layer,
                        i,
                        s,
                        v * (c0 + c1 * v * v)
                        + w_up * source[layer, i, r0 - 1 : r0 + 7, :]
                        + w_down * source[layer, i, r0 + 1 : r0 + 9, :]
                        + w_left * pltpu.roll(e, 1, 1)[:, 128:]
                        + w_right * pltpu.roll(e, 639, 1)[:, 128:]
                        + m05 * source[1 - layer, i, r0 : r0 + 8, :],
                    )
                return carry

            lax.fori_loop(0, 16 // UNROLL, step, 0)

    def to_middle(layer, i, s, value):
        middle[layer, i, 8 + 8 * s : 16 + 8 * s, :] = value

    def to_base(layer, i, s, value):
        base[layer, i, 8 * s : 8 * s + 8, :] = value

    update(first, col_in, inner, to_middle)
    meet(4)
    for s in range(4):
        totals = [jnp.zeros((8, 512), F32)] * 3
        for i in range(16):
            v = middle[inner, i, 8 + 8 * s : 16 + 8 * s, :]
            v = v * v
            totals = [totals[k] + v * eigen_s[k, i] for k in range(3)]
        for k in range(3):
            eig[inner, k, 8 * s : 8 * s + 8, :] = totals[k]
            eig[outer, k, 8 * s : 8 * s + 8, :] = jnp.zeros((8, 512), F32)
    eig_copy = remote(eig.at[other], eig_in.at[c], core_send.at[1], core_recv.at[1], core_peer)

    @pl.when(c == 1)
    def _():
        eig_copy.start()

    meet(5)
    update(first, col_in, outer, to_middle)

    lame_copy.wait_recv()
    stiff_columns(1 - c, lame_in[1 - c, 0], lame_in[1 - c, 1])

    lane1 = lax.broadcasted_iota(jnp.int32, (128, 128), 1)
    start = jnp.where(
        lane1 < 32, macro_s[0], jnp.where((lane1 >= 64) & (lane1 < 96), macro_s[1], macro_s[2])
    )
    for n1 in range(8):
        strain[n1] = start

    even16 = (lane16 // 32) % 2 == 0
    lane_all = lax.broadcasted_iota(jnp.int32, (128, 128), 1)
    even = (lane_all // 32) % 2 == 0

    def product(table_high, table_low, kind):
        wide = dot(table_high[kind], both[kind])
        return wide[:, 0:128] + wide[:, 128:256] + dot(table_low[kind], both[kind, :, 0:128])

    def pack3(a):
        slot = lax.broadcasted_iota(jnp.int32, a[0].shape, 1) // 32
        return [jnp.where(slot == 3, pltpu.roll(a[3], 96 - 32 * k, 1), a[k]) for k in range(3)]

    def unpack3(p):
        slot = lax.broadcasted_iota(jnp.int32, p[0].shape, 1) // 32
        x, y, z = (pltpu.roll(p[k], 32 + 32 * k, 1) for k in range(3))
        return list(p) + [jnp.where(slot == 0, x, jnp.where(slot == 1, y, z))]

    def columns_forward(it):
        def stage(t, carry):
            rows = pl.ds(pl.multiple_of(t * 16, 16), 16)
            x = []
            for n1 in range(8):
                d = strain[n1, rows, :] - eig_t[n1, rows, :]
                x.append(m1_t[n1, rows, :] * d + m2_t[n1, rows, :] * pltpu.roll(d, 64, 1))
            s04, d04, s26, d26 = x[0] + x[4], x[0] - x[4], x[2] + x[6], x[2] - x[6]
            s15, d15, s37, d37 = x[1] + x[5], x[1] - x[5], x[3] + x[7], x[3] - x[7]
            evens, odds = s04 + s26, s15 + s37
            turned = HALF * (d15 - d37)
            summed = HALF * (d15 + d37)
            values = (
                (evens + odds, evens - odds),
                (d04 + turned, -d26 - summed),
                (s04 - s26, s37 - s15),
                (d04 - turned, d26 - summed),
            )
            rows2 = pl.ds(pl.multiple_of(128 + t * 16, 16), 16)
            for kind, (real, imag) in enumerate(values):
                both[kind, rows, 0:128], both[kind, rows, 128:256] = parts(real)
                both[kind, rows2, 0:128], both[kind, rows2, 128:256] = parts(imag)
            return carry

        lax.fori_loop(0, 8, stage, 0)

        def forward(kk, carry):
            kind = (r // 8 + kk) % 4
            result = product(tfh, tfl, kind).reshape(2, 8, 2, 8, 128)
            packed = pack3([result[n // 2, :, n % 2].reshape(64, 128) for n in range(4)])
            for n in range(3):
                send1[it, pl.ds(8 * kind, 8), n] = packed[n].reshape(8, 8, 128)

            def post(j, carry):
                peer = 8 * kind + (r % 8 + j) % 8

                @pl.when(peer != r)
                def _():
                    remote(
                        send1.at[it, peer], recv1.at[it, r],
                        all_send.at[2 * it], all_recv.at[2 * it], (g, peer, c),
                    ).start()

                return carry

            lax.fori_loop(0, 8, post, 0)
            return carry

        lax.fori_loop(0, 4, forward, 0)
        pltpu.make_async_copy(send1.at[it, r], recv1.at[it, r], all_recv.at[2 * it]).start()

    def columns_start():
        for load in loads[3:]:
            load.wait()
        for half, values in ((c, eig.at[mine]), (1 - c, eig_in.at[1 - c])):
            if half is not c:
                eig_copy.wait_recv()
            fields = [values[k] for k in range(3)]
            to_columns(eig_t, half, (fields[0], fields[2], fields[1], fields[2]))
        columns_forward(0)

    @pl.when(c == 0)
    def _():
        columns_start()

    for k in range(CHUNKS):
        outer_copy(k).wait_recv()

        def add(s, carry):
            at, at2 = pl.ds(pl.multiple_of(8 + 8 * s, 8), 8), pl.ds(pl.multiple_of(8 * s, 8), 8)
            m05 = 0.05 * mob[outer, at, :]
            totals = [eig[outer, n, at2, :] for n in range(3)]
            for i in range(CHUNK):
                j = k * CHUNK + i
                v = middle[outer, j, at, :] + m05 * outer_in[j, at2, :]
                middle[outer, j, at, :] = v
                v = v * v
                totals = [totals[n] + v * eigen_s[n, j] for n in range(3)]
            for n in range(3):
                eig[outer, n, at2, :] = totals[n]
            return carry

        lax.fori_loop(0, 4, add, 0)
        if k < EARLY:
            outer_copy2(k).start()

    halo2 = [
        remote(row_out2.at[0], row_in2.at[0], halo_send.at[3], halo_recv.at[3], row_up),
        remote(row_out2.at[1], row_in2.at[1], halo_send.at[4], halo_recv.at[4], row_down),
        remote(col_out2, col_in2, halo_send.at[5], halo_recv.at[5], core_peer),
    ]

    @pl.when(c == 0)
    def _():
        eig_copy.start()

    @pl.when(c == 1)
    def _():
        columns_start()

    def sweep(it, carry):

        @pl.when(it == 1)
        def _():
            outer_copy2(2).start()


        @pl.when(it == 0)
        def _():
            pack(middle, row_out2, col_out2)
            for copy in halo2:
                copy.start()

        pltpu.make_async_copy(recv1.at[it], recv1.at[it], all_recv.at[2 * it]).wait()

        for b in range(8):
            x = []
            for a in range(4):
                v = unpack3([recv1[it, 8 * a + b, n] for n in range(3)])
                x.append((jnp.concatenate(v[0:2], axis=0), jnp.concatenate(v[2:4], axis=0)))
            y = four(x, -1)
            for ka in range(4):
                work[ka, b, 0], work[ka, b, 1] = times(y[ka], b * ka, 32, -1)
        for ka in range(4):
            y = eight([(work[ka, b, 0], work[ka, b, 1]) for b in range(8)], -1)
            for kb in range(8):
                k1 = ka + 4 * kb
                cosine, sine = turn[k1, 0:1, :], turn[k1, 1:2, :]
                real, imag = y[kb]
                z = (real * cosine + imag * sine, imag * cosine - real * sine)
                for half in range(2):
                    at = (slice(16 * k1, 16 * k1 + 16), slice(128 * half, 128 * half + 128))
                    lxh[at], lxl[at] = parts(z[half])

        for q in range(4):
            rows = slice(q * 128, q * 128 + 128)
            spectrum = dot3(lxh[rows, :], lxl[rows, :], bfh[...], bfl[...])
            group = pl.ds(8 * q, 8)
            g0 = green[0, group].reshape(128, 128)
            g1 = green[1, group].reshape(128, 128)
            g2 = green[2, group].reshape(128, 128)
            pieces = []
            for half in range(2):
                s = spectrum[:, 128 * half : 128 * half + 128]
                z = jnp.where(even, pltpu.roll(s, 64, 1), pltpu.roll(s, 96, 1))
                pieces.append(parts(g0 * s + g1 * z + g2 * pltpu.roll(s, 32, 1)))
            oh = jnp.concatenate([pieces[0][0], pieces[1][0]], axis=1)
            ol = jnp.concatenate([pieces[0][1], pieces[1][1]], axis=1)
            back = dot3(oh, ol, bih[...], bil[...])
            for j in range(8):
                k1 = 8 * q + j
                cosine, sine = turn[k1, 0:1, :], turn[k1, 1:2, :]
                real, imag = back[16 * j : 16 * j + 16, 0:128], back[16 * j : 16 * j + 16, 128:256]
                flat[k1, 0] = real * cosine - imag * sine
                flat[k1, 1] = imag * cosine + real * sine

        for ka in range(4):
            y = eight([(flat[ka + 4 * kb, 0], flat[ka + 4 * kb, 1]) for kb in range(8)], 1)
            for b in range(8):
                work[ka, b, 0], work[ka, b, 1] = times(y[b], b * ka, 32, 1)

        def backward(bb, carry):
            b = (r + bb) % 8
            y = four([(work[ka, b, 0], work[ka, b, 1]) for ka in range(4)], 1)
            for a in range(4):
                packed = pack3([y[a][n // 2][8 * (n % 2) : 8 * (n % 2) + 8] for n in range(4)])
                for n in range(3):
                    send2[it, 8 * a + b, n] = packed[n]

            def post(j, carry):
                peer = 8 * ((r // 8 + j) % 4) + b

                @pl.when(peer != r)
                def _():
                    remote(
                        send2.at[it, peer], recv2.at[it, r],
                        all_send.at[2 * it + 1], all_recv.at[2 * it + 1], (g, peer, c),
                    ).start()

                return carry

            lax.fori_loop(0, 4, post, 0)
            return carry

        lax.fori_loop(0, 8, backward, 0)
        pltpu.make_async_copy(send2.at[it, r], recv2.at[it, r], all_recv.at[2 * it + 1]).start()

        @pl.when(it == 0)
        def _():
            for copy in halo2:
                copy.wait_recv()
            unpack(middle, row_in2)

        outer_copy2(2 * it + 1).start()
        update(middle, col_in2, it, to_base)
        pltpu.make_async_copy(recv2.at[it], recv2.at[it], all_recv.at[2 * it + 1]).wait()

        for kind in range(4):
            group = pl.ds(8 * kind, 8)
            v = unpack3([recv2[it, group, n].reshape(64, 128) for n in range(3)])
            for half in range(2):
                at = slice(128 * half, 128 * half + 128)
                pair = [v[2 * half + n].reshape(8, 1, 8, 128) for n in range(2)]
                value = parts(jnp.concatenate(pair, axis=1).reshape(128, 128))
                both[kind, at, 0:128], both[kind, at, 128:256] = value
            result = product(tih, til, kind)
            flat[pl.ds(8 * kind, 8), 0] = result[0:128].reshape(8, 16, 128)
            flat[pl.ds(8 * kind, 8), 1] = result[128:256].reshape(8, 16, 128)

        def unstage(t, carry):
            rows = pl.ds(pl.multiple_of(t * 16, 16), 16)
            z0, z4 = flat[t, 0], flat[t, 1]
            a1, b1 = flat[8 + t, 0], flat[8 + t, 1]
            a2, b2 = flat[16 + t, 0], flat[16 + t, 1]
            a3, b3 = flat[24 + t, 0], flat[24 + t, 1]
            zp, zm = z0 + z4, z0 - z4
            sa, db, da, sb = a1 + a3, b3 - b1, a1 - a3, b1 + b3
            p1, p2 = HALF * (da - sb), HALF * (da + sb)
            values = (
                zp + a2 + sa,
                zm - b2 + p1,
                zp - a2 + db,
                zm + b2 - p2,
                zp + a2 - sa,
                zm - b2 - p1,
                zp - a2 - db,
                zm + b2 + p2,
            )
            for n1 in range(8):
                strain[n1, rows, :] -= values[n1]
            return carry

        lax.fori_loop(0, 8, unstage, 0)

        @pl.when(it < ITERS - 1)
        def _():
            columns_forward(it + 1)

        return carry

    lax.fori_loop(0, ITERS, sweep, 0)

    def to_rows(half, layer, target, j):
        block = strain[4 * half + j].T
        lanes = slice(128 * j, 128 * j + 128)
        target[layer, 0, :, lanes] = block[0:32]
        target[layer, 1, :, lanes] = block[64:96]
        target[layer, 2, :, lanes] = block[32:64]

    def final_copy(layer, j):
        lanes = pl.ds(128 * j, 128)
        return remote(
            eig_in.at[0, :, :, lanes], final.at[layer, :, :, lanes],
            core_send.at[2 + j], core_recv.at[2 + j], core_peer,
        )

    for j in range(4):
        to_rows(1 - c, 0, eig_in, j)
        final_copy(mine, j).start()
    for j in range(4):
        to_rows(c, mine, final, j)
    for j in range(4):
        final_copy(other, j).wait_recv()
    for k in range(CHUNKS):
        outer_copy2(k).wait_recv()
    for copy in halo + halo2 + [lame_copy, eig_copy] + [final_copy(mine, j) for j in range(4)]:
        copy.wait_send()
    for k in range(CHUNKS):
        outer_copy(k).wait_send()
        outer_copy2(k).wait_send()
    for it in range(ITERS):
        for sent, sem in ((send1, 2 * it), (send2, 2 * it + 1)):
            whole = sent.at[it, pl.ds(0, ROWS - 1)]
            pltpu.make_async_copy(whole, whole, all_send.at[sem]).wait()


def finish(
    middle, base, outer_in2, final, eig, lame, mob, eigen_s, out_hbm, strain_hbm, out, sem
):
    g = lax.axis_index("grp")
    strain_copy = pltpu.make_async_copy(final, strain_hbm, sem.at[8])
    strain_copy.start()
    for place in range(2):
        layer = g if place == 0 else 1 - g

        def at(s, carry):
            rows = pl.ds(pl.multiple_of(8 * s, 8), 8)
            rows2 = pl.ds(pl.multiple_of(8 + 8 * s, 8), 8)
            d = [final[layer, k, rows, :] - eig[layer, k, rows, :] for k in range(3)]
            lam, double = lame[layer, 0, rows, :], 2.0 * lame[layer, 1, rows, :]
            m = mob[layer, rows2, :]
            m05, c1 = 0.05 * m, 0.2 * m
            push = (
                c1 * ((lam + double) * d[0] + lam * d[1]),
                c1 * (lam * d[0] + (lam + double) * d[1]),
                c1 * (2.0 * (double * d[2])),
            )
            for i in range(16):
                v = middle[layer, i, rows2, :]
                value = base[layer, i, rows, :] + v * (
                    push[0] * eigen_s[0, i] + push[1] * eigen_s[1, i] + push[2] * eigen_s[2, i]
                )
                if place == 1:
                    value = value + m05 * outer_in2[i, rows, :]
                out[layer, i, rows, :] = value
            pltpu.make_async_copy(
                out.at[layer, :, rows, :], out_hbm.at[layer, :, rows, :], sem.at[4 * place + s]
            ).start()
            return carry

        lax.fori_loop(0, 4, at, 0)
    for place in range(2):
        layer = g if place == 0 else 1 - g
        for s in range(4):
            rows = pl.ds(8 * s, 8)
            pltpu.make_async_copy(
                out.at[layer, :, rows, :], out_hbm.at[layer, :, rows, :], sem.at[4 * place + s]
            ).wait()
    strain_copy.wait()


def body(order, grain, phase, mobility, index, stiff, eigen, macro):
    constants = tables()
    any_spec = pl.BlockSpec(memory_space=pl.ANY)
    smem = pl.BlockSpec(memory_space=pltpu.SMEM)
    vmem = pl.BlockSpec(memory_space=pltpu.VMEM)
    big = (2, 16, 48, 512)
    every = (ITERS, ROWS, 3, 8, 128)
    columns = (8, 128, 128)
    kept = (
        big, (2, 16, 32, 512), (16, 32, 512), (2, 3, 32, 512), (2, 3, 32, 512), (2, 2, 32, 512),
        (2, 48, 512),
    )
    values = pl.pallas_call(
        kernel,
        out_shape=tuple(pltpu.VMEM(shape, F32) for shape in kept),
        in_specs=[any_spec] * 12 + [smem] * 5,
        out_specs=(vmem,) * len(kept),
        scratch_shapes=[
            pltpu.VMEM(big, F32),
            pltpu.VMEM((2, 32, 512), jnp.int32),
            pltpu.VMEM((2, 32, 512), jnp.int32),
        ]
        + [pltpu.VMEM((4, 256, 256), BF16)] * 4
        + [pltpu.VMEM((256, 256), BF16)] * 4
        + [pltpu.VMEM((32, 2, 128), F32)]
        + [
            pltpu.VMEM((2, 34, 1, 512), F32),
            pltpu.VMEM((2, 34, 1, 512), F32),
            pltpu.VMEM((2, 32, 1, 512), F32),
            pltpu.VMEM((2, 32, 1, 512), F32),
            pltpu.VMEM((34, 32, 128), F32),
            pltpu.VMEM((34, 32, 128), F32),
            pltpu.VMEM((32, 32, 128), F32),
            pltpu.VMEM((32, 32, 128), F32),
            pltpu.VMEM((16, 32, 512), F32),
            pltpu.VMEM((2, 2, 32, 512), F32),
            pltpu.VMEM((2, 3, 32, 512), F32),
        ]
        + [pltpu.VMEM(columns, F32)] * 4
        + [pltpu.VMEM((3, 32, 16, 128), F32)]
        + [pltpu.VMEM(every, F32)] * 4
        + [pltpu.VMEM((4, 8, 2, 16, 128), F32)]
        + [pltpu.VMEM((4, 256, 256), BF16)]
        + [pltpu.VMEM((32, 2, 16, 128), F32)]
        + [pltpu.VMEM((512, 256), BF16)] * 2
        + [
            pltpu.SemaphoreType.DMA((n,))
            for n in (12, 6, 6, 2 * CHUNKS, 2 * CHUNKS, 6, 6, 2 * ITERS, 2 * ITERS)
        ]
        + [pltpu.SemaphoreType.REGULAR((5,))],
        compiler_params=pltpu.CompilerParams(
            collective_id=0, has_side_effects=True, vmem_limit_bytes=48 * 1024 * 1024
        ),
        name="step",
    )(order, grain, phase, *[jnp.asarray(t) for t in constants], mobility, index, stiff.T, eigen.T, macro)
    return pl.pallas_call(
        finish,
        out_shape=(
            jax.ShapeDtypeStruct((2, 16, 32, 512), F32),
            jax.ShapeDtypeStruct((2, 3, 32, 512), F32),
        ),
        in_specs=[vmem] * len(kept) + [smem],
        out_specs=(any_spec, any_spec),
        scratch_shapes=[pltpu.VMEM((2, 16, 32, 512), F32), pltpu.SemaphoreType.DMA((9,))],
        compiler_params=pltpu.CompilerParams(vmem_limit_bytes=6 * 1024 * 1024),
        name="finish",
    )(*values, eigen.T)


def solution(mesh):
    fields = P("grp", None, "row", "col")
    labels = P("grp", "row", "col")
    return jax.shard_map(
        body,
        mesh=mesh,
        in_specs=(fields, labels, labels, P(), P(), P(), P(), P()),
        out_specs=(fields, fields),
        check_vma=False,
    )
```

```python
import jax
import jax.numpy as jnp
import ml_dtypes
import numpy as np
from jax import lax
from jax.experimental import pallas as pl
from jax.experimental.pallas import tpu as pltpu
from jax.sharding import PartitionSpec as P

MESH = pl.DeviceIdType.MESH
ITERS = 2
ROWS = 32
HALF = 0.7071067811865476
LAMBDA_REF = 1.25
SHEAR_REF = 1.25
BETA_REF = (LAMBDA_REF + SHEAR_REF) / (SHEAR_REF * (LAMBDA_REF + 2.0 * SHEAR_REF))
F32 = jnp.float32
BF16 = jnp.bfloat16
CHUNK = 4
CHUNKS = 16 // CHUNK
UNROLL = 4
EARLY = 0


def split_table(values):
    high = values.astype(np.float32).astype(ml_dtypes.bfloat16)
    low = (values - high.astype(np.float64)).astype(np.float32).astype(ml_dtypes.bfloat16)
    return high, low


def tables():
    place = np.arange(128, dtype=np.float64)
    forward = np.zeros((4, 256, 256))
    inverse = np.zeros((4, 256, 256))
    scale = 1.0 / 1048576.0
    half = np.arange(64, dtype=np.float64)
    for first, base in ((0, 0), (64, 4)):
        angle = 2.0 * np.pi * np.outer(base + 8 * half, place) / 1024.0
        source = slice(0, 128) if base == 0 else slice(128, 256)
        forward[0, first : first + 64, source] = np.cos(angle)
        forward[0, 128 + first : 192 + first, source] = -np.sin(angle)
        weight = np.full((64, 1), 2.0 * scale)
        if base == 0:
            weight[0] = scale
        inverse[0, source, first : first + 64] = (weight * np.cos(angle)).T
        inverse[0, source, 128 + first : 192 + first] = (-weight * np.sin(angle)).T
    for kind in (1, 2, 3):
        angle = 2.0 * np.pi * np.outer(kind + 8 * place, place) / 1024.0
        cosine, sine = np.cos(angle), np.sin(angle)
        forward[kind] = np.block([[cosine, sine], [-sine, cosine]])
        inverse[kind] = 2.0 * scale * np.block([[cosine.T, -sine.T], [sine.T, cosine.T]])
    small = np.arange(32, dtype=np.float64)
    angle = 2.0 * np.pi * np.outer(small, small) / 32.0
    slots = np.eye(4)
    slots[3, 3] = 0.0
    cosine, sine = np.kron(slots, np.cos(angle)), np.kron(slots, np.sin(angle))
    rows_inverse = np.block([[cosine, sine], [-sine, cosine]])
    slots[1, 3] = 1.0
    cosine, sine = np.kron(slots, np.cos(angle)), np.kron(slots, np.sin(angle))
    rows_forward = np.block([[cosine, -sine], [sine, cosine]])
    angle = 2.0 * np.pi * np.outer(small, np.tile(small, 4)) / 1024.0
    turn = np.stack([np.cos(angle), np.sin(angle)], axis=1).astype(np.float32)
    return (
        split_table(forward)
        + split_table(inverse)
        + split_table(rows_forward)
        + split_table(rows_inverse)
        + (turn,)
    )


def times(value, angle_index, length, sign):
    real, imag = value
    angle_index = angle_index % length
    if angle_index == 0:
        return value
    angle = 2.0 * np.pi * angle_index / length
    cosine, sine = float(np.cos(angle)), float(sign * np.sin(angle))
    if 4 * angle_index == length or 4 * angle_index == 3 * length:
        return (-imag, real) if sine > 0 else (imag, -real)
    if 2 * angle_index == length:
        return (-real, -imag)
    return (real * cosine - imag * sine, imag * cosine + real * sine)


def plus(first, second):
    return (first[0] + second[0], first[1] + second[1])


def minus(first, second):
    return (first[0] - second[0], first[1] - second[1])


def four(x, sign):
    a, b, c, d = plus(x[0], x[2]), minus(x[0], x[2]), plus(x[1], x[3]), minus(x[1], x[3])
    d = (-d[1], d[0]) if sign > 0 else (d[1], -d[0])
    return [plus(a, c), plus(b, d), minus(a, c), minus(b, d)]


def eight(x, sign):
    even, odd = four(x[0::2], sign), four(x[1::2], sign)
    odd = [odd[0], times(odd[1], 1, 8, sign), times(odd[2], 2, 8, sign), times(odd[3], 3, 8, sign)]
    return [plus(e, o) for e, o in zip(even, odd)] + [minus(e, o) for e, o in zip(even, odd)]


def parts(value):
    high = value.astype(BF16)
    return high, (value - high.astype(F32)).astype(BF16)


def dot(a, b):
    return jnp.dot(a, b, preferred_element_type=F32)


def dot3(a_high, a_low, b_high, b_low):
    return dot(a_high, b_high) + dot(a_high, b_low) + dot(a_low, b_high)


def kernel(
    order_hbm, grain_hbm, phase_hbm, tfh_hbm, tfl_hbm, tih_hbm, til_hbm, bfh_hbm, bfl_hbm, bih_hbm,
    bil_hbm, turn_hbm, mob_s, index_s, stiff_s, eigen_s, macro_s,
    middle, base, outer_in2, final, eig, lame, mob,
    first, grain, phase, tfh, tfl, tih, til, bfh, bfl, bih, bil, turn,
    row_out, row_in, row_out2, row_in2, col_out, col_in, col_out2, col_in2,
    outer_in, lame_in, eig_in,
    strain, eig_t, m1_t, m2_t, green, send1, recv1, send2, recv2, work, both, flat, lxh, lxl,
    load_sem, halo_send, halo_recv, outer_send, outer_recv, core_send, core_recv, all_send, all_recv, meet_sem,
):
    g, r, c = lax.axis_index("grp"), lax.axis_index("row"), lax.axis_index("col")
    inner, outer = g, 1 - g
    mine = jnp.where(c == 0, inner, outer)
    other = 1 - mine
    core_peer = (g, r, 1 - c)
    grp_peer = (1 - g, r, c)
    row_up = (g, (r + ROWS - 1) % ROWS, c)
    row_down = (g, (r + 1) % ROWS, c)

    def remote(source, target, send, recv, device):
        return pltpu.make_async_remote_copy(
            source, target, send, recv, device_id=device, device_id_type=MESH
        )

    loads = [
        pltpu.make_async_copy(grain_hbm, grain, load_sem.at[0]),
        pltpu.make_async_copy(phase_hbm, phase, load_sem.at[1]),
        pltpu.make_async_copy(order_hbm, first.at[:, :, pl.ds(8, 32), :], load_sem.at[2]),
    ]
    pairs = (
        (tfh_hbm, tfh), (tfl_hbm, tfl), (tih_hbm, tih), (til_hbm, til), (bfh_hbm, bfh),
        (bfl_hbm, bfl), (bih_hbm, bih), (bil_hbm, bil), (turn_hbm, turn),
    )
    for place, (source, target) in enumerate(pairs):
        loads.append(pltpu.make_async_copy(source, target, load_sem.at[3 + place]))
    for load in loads:
        load.start()

    barrier = pltpu.get_barrier_semaphore()
    beyond = jnp.where(r % 2 == 1, row_down[1], row_up[1])
    near = [(g, jnp.bitwise_xor(r, 1 << k), c) for k in range(5)]
    for peer in [grp_peer, core_peer, (g, beyond, c)] + near:
        pl.semaphore_signal(barrier, inc=1, device_id=peer, device_id_type=MESH)

    def meet(k):
        if k > 0:
            pl.semaphore_wait(meet_sem.at[k - 1], 1)
        if k < 5:
            pl.semaphore_signal(meet_sem.at[k], inc=1, device_id=near[k], device_id_type=MESH)

    loads[0].wait()
    loads[1].wait()
    for layer in range(2):
        labels = grain[layer]

        def look(k, value):
            return jnp.where(labels == k, mob_s[k], value)

        mob[layer, 8:40, :] = lax.fori_loop(0, 32, look, jnp.zeros((32, 512), F32))
        labels2 = phase[layer]

        def look2(k, values):
            chosen = index_s[k]
            hit = labels2 == k
            return (
                jnp.where(hit, stiff_s[0, chosen], values[0]),
                jnp.where(hit, stiff_s[1, chosen], values[1]),
            )

        empty = jnp.zeros((32, 512), F32)
        lam, shear = lax.fori_loop(0, 8, look2, (empty, empty))
        lame[layer, 0] = lam
        lame[layer, 1] = shear

    lane = lax.broadcasted_iota(jnp.int32, (32, 128), 1)

    def pack(source, rows_to, cols_to):
        def step(i, carry):
            for layer in range(2):
                k = layer * 16 + i
                rows_to[0, k] = source[layer, i, 8:9, :]
                rows_to[1, k] = source[layer, i, 39:40, :]
                cols_to[k] = jnp.where(
                    lane < 64, source[layer, i, 8:40, 0:128], source[layer, i, 8:40, 384:512]
                )
            return carry

        lax.fori_loop(0, 16, step, 0)

    def unpack(target, rows_from):
        def step(i, carry):
            for layer in range(2):
                k = layer * 16 + i
                target[layer, i, 40:41, :] = rows_from[0, k]
                target[layer, i, 7:8, :] = rows_from[1, k]
            return carry

        lax.fori_loop(0, 16, step, 0)

    loads[2].wait()
    pack(first, row_out, col_out)
    for layer in range(2):
        row_out[0, 32 + layer] = mob[layer, 8:9, :]
        row_out[1, 32 + layer] = mob[layer, 39:40, :]
        col_out[32 + layer] = jnp.where(lane < 64, mob[layer, 8:40, 0:128], mob[layer, 8:40, 384:512])

    pl.semaphore_wait(barrier, 8)
    meet(0)

    halo = [
        remote(row_out.at[0], row_in.at[0], halo_send.at[0], halo_recv.at[0], row_up),
        remote(row_out.at[1], row_in.at[1], halo_send.at[1], halo_recv.at[1], row_down),
        remote(col_out, col_in, halo_send.at[2], halo_recv.at[2], core_peer),
    ]
    for copy in halo:
        copy.start()

    def outer_copy(k):
        at = pl.ds(k * CHUNK, CHUNK)
        return remote(
            order_hbm.at[outer, at], outer_in.at[at], outer_send.at[k], outer_recv.at[k], grp_peer
        )

    def outer_copy2(k):
        at = pl.ds(k * CHUNK, CHUNK)
        return remote(
            middle.at[outer, at, pl.ds(8, 32), :], outer_in2.at[at],
            outer_send.at[CHUNKS + k], outer_recv.at[CHUNKS + k], grp_peer,
        )

    for k in range(CHUNKS):
        outer_copy(k).start()
    lame_copy = remote(lame.at[other], lame_in.at[c], core_send.at[0], core_recv.at[0], core_peer)
    lame_copy.start()

    sub16 = lax.broadcasted_iota(jnp.int32, (16, 128), 0)
    lane16 = lax.broadcasted_iota(jnp.int32, (16, 128), 1)
    slot = lane16 // 32
    place = (r % 8) * 16 + sub16
    kind = r // 8
    col_freq = jnp.where(
        kind > 0, kind + 8 * place, jnp.where(place < 64, 8 * place, 4 + 8 * (place - 64))
    )
    col_signed = jnp.where(col_freq >= 512, col_freq - 1024, col_freq).astype(F32)

    def green_step(k1, carry):
        row_freq = k1 + 32 * (lane16 % 32)
        row_signed = jnp.where(row_freq >= 512, row_freq - 1024, row_freq).astype(F32)
        keeper = jnp.where((row_freq != 512) & (col_freq != 512), 1.0, 0.0)
        radius = row_signed * row_signed + col_signed * col_signed
        inverse = keeper * lax.rsqrt(jnp.where(radius > 0, radius, 1.0))
        n1, n2 = row_signed * inverse, col_signed * inverse
        a, b, d = n1 * n1, n2 * n2, n1 * n2
        own = jnp.where(
            slot == 0,
            a / SHEAR_REF - BETA_REF * a * a,
            jnp.where(
                slot == 2,
                b / SHEAR_REF - BETA_REF * b * b,
                0.5 * (a + b) / SHEAR_REF - 2.0 * BETA_REF * d * d,
            ),
        )
        toward_rr = 0.5 * d / SHEAR_REF - BETA_REF * a * d
        toward_cc = 0.5 * d / SHEAR_REF - BETA_REF * b * d
        across = -BETA_REF * d * d
        green[0, k1] = own
        green[1, k1] = jnp.where(
            slot == 1, toward_cc, jnp.where(slot == 3, toward_rr, across)
        )
        green[2, k1] = jnp.where(
            slot == 0,
            2.0 * toward_rr,
            jnp.where(slot == 1, toward_rr, jnp.where(slot == 2, 2.0 * toward_cc, toward_cc)),
        )
        return carry

    meet(1)
    lax.fori_loop(0, 32, green_step, 0)
    meet(2)

    def to_columns(target, half, slots):
        for j in range(4):
            block = jnp.concatenate([field[:, 128 * j : 128 * j + 128] for field in slots], axis=0)
            target[4 * half + j] = block.T

    def stiff_columns(half, lam, shear):
        double = 2.0 * shear
        straight = lam + double
        empty = jnp.zeros_like(lam)
        to_columns(m1_t, half, (straight, double, straight, empty))
        to_columns(m2_t, half, (lam, empty, lam, empty))

    stiff_columns(c, lame[mine, 0], lame[mine, 1])

    for copy in halo:
        copy.wait_recv()
    meet(3)
    unpack(first, row_in)
    for layer in range(2):
        mob[layer, 40:41, :] = row_in[0, 32 + layer]
        mob[layer, 7:8, :] = row_in[1, 32 + layer]

    def update(source, cols, layer, write):
        for s in range(4):
            r0, r1 = 8 + 8 * s, 8 * s
            m = mob[layer, r0 : r0 + 8, :]
            edge = jnp.concatenate([col_in[32 + layer, r1 : r1 + 8, :], m], axis=1)
            w_up = 0.05 * (m + mob[layer, r0 - 1 : r0 + 7, :])
            w_down = 0.05 * (m + mob[layer, r0 + 1 : r0 + 9, :])
            w_left = 0.05 * (m + pltpu.roll(edge, 1, 1)[:, 128:])
            w_right = 0.05 * (m + pltpu.roll(edge, 639, 1)[:, 128:])
            total = jnp.zeros((8, 512), F32)
            for i in range(16):
                v = source[layer, i, r0 : r0 + 8, :]
                total = total + v * v
            c0 = 1.0 - (w_up + w_down + w_left + w_right) - 0.3 * m * total
            c1 = 0.2 * m
            m05 = 0.05 * m

            def step(n, carry):
                for i4 in range(UNROLL):
                    i = n * UNROLL + i4
                    v = source[layer, i, r0 : r0 + 8, :]
                    e = jnp.concatenate([cols[layer * 16 + i, r1 : r1 + 8, :], v], axis=1)
                    write(
                        layer,
                        i,
                        s,
                        v * (c0 + c1 * v * v)
                        + w_up * source[layer, i, r0 - 1 : r0 + 7, :]
                        + w_down * source[layer, i, r0 + 1 : r0 + 9, :]
                        + w_left * pltpu.roll(e, 1, 1)[:, 128:]
                        + w_right * pltpu.roll(e, 639, 1)[:, 128:]
                        + m05 * source[1 - layer, i, r0 : r0 + 8, :],
                    )
                return carry

            lax.fori_loop(0, 16 // UNROLL, step, 0)

    def to_middle(layer, i, s, value):
        middle[layer, i, 8 + 8 * s : 16 + 8 * s, :] = value

    def to_base(layer, i, s, value):
        base[layer, i, 8 * s : 8 * s + 8, :] = value

    update(first, col_in, inner, to_middle)
    meet(4)
    for s in range(4):
        totals = [jnp.zeros((8, 512), F32)] * 3
        for i in range(16):
            v = middle[inner, i, 8 + 8 * s : 16 + 8 * s, :]
            v = v * v
            totals = [totals[k] + v * eigen_s[k, i] for k in range(3)]
        for k in range(3):
            eig[inner, k, 8 * s : 8 * s + 8, :] = totals[k]
            eig[outer, k, 8 * s : 8 * s + 8, :] = jnp.zeros((8, 512), F32)
    eig_copy = remote(eig.at[other], eig_in.at[c], core_send.at[1], core_recv.at[1], core_peer)

    @pl.when(c == 1)
    def _():
        eig_copy.start()

    meet(5)
    update(first, col_in, outer, to_middle)

    lame_copy.wait_recv()
    stiff_columns(1 - c, lame_in[1 - c, 0], lame_in[1 - c, 1])

    lane1 = lax.broadcasted_iota(jnp.int32, (128, 128), 1)
    start = jnp.where(
        lane1 < 32, macro_s[0], jnp.where((lane1 >= 64) & (lane1 < 96), macro_s[1], macro_s[2])
    )
    for n1 in range(8):
        strain[n1] = start

    even16 = (lane16 // 32) % 2 == 0
    lane_all = lax.broadcasted_iota(jnp.int32, (128, 128), 1)
    even = (lane_all // 32) % 2 == 0

    def product(table_high, table_low, kind):
        wide = dot(table_high[kind], both[kind])
        return wide[:, 0:128] + wide[:, 128:256] + dot(table_low[kind], both[kind, :, 0:128])

    def pack3(a):
        slot = lax.broadcasted_iota(jnp.int32, a[0].shape, 1) // 32
        return [jnp.where(slot == 3, pltpu.roll(a[3], 96 - 32 * k, 1), a[k]) for k in range(3)]

    def unpack3(p):
        slot = lax.broadcasted_iota(jnp.int32, p[0].shape, 1) // 32
        x, y, z = (pltpu.roll(p[k], 32 + 32 * k, 1) for k in range(3))
        return list(p) + [jnp.where(slot == 0, x, jnp.where(slot == 1, y, z))]

    def columns_forward(it):
        def stage(t, carry):
            rows = pl.ds(pl.multiple_of(t * 16, 16), 16)
            x = []
            for n1 in range(8):
                d = strain[n1, rows, :] - eig_t[n1, rows, :]
                x.append(m1_t[n1, rows, :] * d + m2_t[n1, rows, :] * pltpu.roll(d, 64, 1))
            s04, d04, s26, d26 = x[0] + x[4], x[0] - x[4], x[2] + x[6], x[2] - x[6]
            s15, d15, s37, d37 = x[1] + x[5], x[1] - x[5], x[3] + x[7], x[3] - x[7]
            evens, odds = s04 + s26, s15 + s37
            turned = HALF * (d15 - d37)
            summed = HALF * (d15 + d37)
            values = (
                (evens + odds, evens - odds),
                (d04 + turned, -d26 - summed),
                (s04 - s26, s37 - s15),
                (d04 - turned, d26 - summed),
            )
            rows2 = pl.ds(pl.multiple_of(128 + t * 16, 16), 16)
            for kind, (real, imag) in enumerate(values):
                both[kind, rows, 0:128], both[kind, rows, 128:256] = parts(real)
                both[kind, rows2, 0:128], both[kind, rows2, 128:256] = parts(imag)
            return carry

        lax.fori_loop(0, 8, stage, 0)

        def forward(kk, carry):
            kind = (r // 8 + kk) % 4
            result = product(tfh, tfl, kind).reshape(2, 8, 2, 8, 128)
            packed = pack3([result[n // 2, :, n % 2].reshape(64, 128) for n in range(4)])
            for n in range(3):
                send1[it, pl.ds(8 * kind, 8), n] = packed[n].reshape(8, 8, 128)

            def post(j, carry):
                peer = 8 * kind + (r % 8 + j) % 8

                @pl.when(peer != r)
                def _():
                    remote(
                        send1.at[it, peer], recv1.at[it, r],
                        all_send.at[2 * it], all_recv.at[2 * it], (g, peer, c),
                    ).start()

                return carry

            lax.fori_loop(0, 8, post, 0)
            return carry

        lax.fori_loop(0, 4, forward, 0)
        pltpu.make_async_copy(send1.at[it, r], recv1.at[it, r], all_recv.at[2 * it]).start()

    def columns_start():
        for load in loads[3:]:
            load.wait()
        for half, values in ((c, eig.at[mine]), (1 - c, eig_in.at[1 - c])):
            if half is not c:
                eig_copy.wait_recv()
            fields = [values[k] for k in range(3)]
            to_columns(eig_t, half, (fields[0], fields[2], fields[1], fields[2]))
        columns_forward(0)

    @pl.when(c == 0)
    def _():
        columns_start()

    for k in range(CHUNKS):
        outer_copy(k).wait_recv()

        def add(s, carry):
            at, at2 = pl.ds(pl.multiple_of(8 + 8 * s, 8), 8), pl.ds(pl.multiple_of(8 * s, 8), 8)
            m05 = 0.05 * mob[outer, at, :]
            totals = [eig[outer, n, at2, :] for n in range(3)]
            for i in range(CHUNK):
                j = k * CHUNK + i
                v = middle[outer, j, at, :] + m05 * outer_in[j, at2, :]
                middle[outer, j, at, :] = v
                v = v * v
                totals = [totals[n] + v * eigen_s[n, j] for n in range(3)]
            for n in range(3):
                eig[outer, n, at2, :] = totals[n]
            return carry

        lax.fori_loop(0, 4, add, 0)
        if k < EARLY:
            outer_copy2(k).start()

    halo2 = [
        remote(row_out2.at[0], row_in2.at[0], halo_send.at[3], halo_recv.at[3], row_up),
        remote(row_out2.at[1], row_in2.at[1], halo_send.at[4], halo_recv.at[4], row_down),
        remote(col_out2, col_in2, halo_send.at[5], halo_recv.at[5], core_peer),
    ]

    @pl.when(c == 0)
    def _():
        eig_copy.start()

    @pl.when(c == 1)
    def _():
        columns_start()

    def sweep(it, carry):
        outer_copy2(2 * it).start()

        @pl.when(it == 0)
        def _():
            pack(middle, row_out2, col_out2)
            for copy in halo2:
                copy.start()

        pltpu.make_async_copy(recv1.at[it], recv1.at[it], all_recv.at[2 * it]).wait()

        for b in range(8):
            x = []
            for a in range(4):
                v = unpack3([recv1[it, 8 * a + b, n] for n in range(3)])
                x.append((jnp.concatenate(v[0:2], axis=0), jnp.concatenate(v[2:4], axis=0)))
            y = four(x, -1)
            for ka in range(4):
                work[ka, b, 0], work[ka, b, 1] = times(y[ka], b * ka, 32, -1)
        for ka in range(4):
            y = eight([(work[ka, b, 0], work[ka, b, 1]) for b in range(8)], -1)
            for kb in range(8):
                k1 = ka + 4 * kb
                cosine, sine = turn[k1, 0:1, :], turn[k1, 1:2, :]
                real, imag = y[kb]
                z = (real * cosine + imag * sine, imag * cosine - real * sine)
                for half in range(2):
                    at = (slice(16 * k1, 16 * k1 + 16), slice(128 * half, 128 * half + 128))
                    lxh[at], lxl[at] = parts(z[half])

        for q in range(4):
            rows = slice(q * 128, q * 128 + 128)
            spectrum = dot3(lxh[rows, :], lxl[rows, :], bfh[...], bfl[...])
            group = pl.ds(8 * q, 8)
            g0 = green[0, group].reshape(128, 128)
            g1 = green[1, group].reshape(128, 128)
            g2 = green[2, group].reshape(128, 128)
            pieces = []
            for half in range(2):
                s = spectrum[:, 128 * half : 128 * half + 128]
                z = jnp.where(even, pltpu.roll(s, 64, 1), pltpu.roll(s, 96, 1))
                pieces.append(parts(g0 * s + g1 * z + g2 * pltpu.roll(s, 32, 1)))
            oh = jnp.concatenate([pieces[0][0], pieces[1][0]], axis=1)
            ol = jnp.concatenate([pieces[0][1], pieces[1][1]], axis=1)
            back = dot3(oh, ol, bih[...], bil[...])
            for j in range(8):
                k1 = 8 * q + j
                cosine, sine = turn[k1, 0:1, :], turn[k1, 1:2, :]
                real, imag = back[16 * j : 16 * j + 16, 0:128], back[16 * j : 16 * j + 16, 128:256]
                flat[k1, 0] = real * cosine - imag * sine
                flat[k1, 1] = imag * cosine + real * sine

        for ka in range(4):
            y = eight([(flat[ka + 4 * kb, 0], flat[ka + 4 * kb, 1]) for kb in range(8)], 1)
            for b in range(8):
                work[ka, b, 0], work[ka, b, 1] = times(y[b], b * ka, 32, 1)

        def backward(bb, carry):
            b = (r + bb) % 8
            y = four([(work[ka, b, 0], work[ka, b, 1]) for ka in range(4)], 1)
            for a in range(4):
                packed = pack3([y[a][n // 2][8 * (n % 2) : 8 * (n % 2) + 8] for n in range(4)])
                for n in range(3):
                    send2[it, 8 * a + b, n] = packed[n]

            def post(j, carry):
                peer = 8 * ((r // 8 + j) % 4) + b

                @pl.when(peer != r)
                def _():
                    remote(
                        send2.at[it, peer], recv2.at[it, r],
                        all_send.at[2 * it + 1], all_recv.at[2 * it + 1], (g, peer, c),
                    ).start()

                return carry

            lax.fori_loop(0, 4, post, 0)
            return carry

        lax.fori_loop(0, 8, backward, 0)
        pltpu.make_async_copy(send2.at[it, r], recv2.at[it, r], all_recv.at[2 * it + 1]).start()

        @pl.when(it == 0)
        def _():
            for copy in halo2:
                copy.wait_recv()
            unpack(middle, row_in2)

        outer_copy2(2 * it + 1).start()
        update(middle, col_in2, it, to_base)
        pltpu.make_async_copy(recv2.at[it], recv2.at[it], all_recv.at[2 * it + 1]).wait()

        for kind in range(4):
            group = pl.ds(8 * kind, 8)
            v = unpack3([recv2[it, group, n].reshape(64, 128) for n in range(3)])
            for half in range(2):
                at = slice(128 * half, 128 * half + 128)
                pair = [v[2 * half + n].reshape(8, 1, 8, 128) for n in range(2)]
                value = parts(jnp.concatenate(pair, axis=1).reshape(128, 128))
                both[kind, at, 0:128], both[kind, at, 128:256] = value
            result = product(tih, til, kind)
            flat[pl.ds(8 * kind, 8), 0] = result[0:128].reshape(8, 16, 128)
            flat[pl.ds(8 * kind, 8), 1] = result[128:256].reshape(8, 16, 128)

        def unstage(t, carry):
            rows = pl.ds(pl.multiple_of(t * 16, 16), 16)
            z0, z4 = flat[t, 0], flat[t, 1]
            a1, b1 = flat[8 + t, 0], flat[8 + t, 1]
            a2, b2 = flat[16 + t, 0], flat[16 + t, 1]
            a3, b3 = flat[24 + t, 0], flat[24 + t, 1]
            zp, zm = z0 + z4, z0 - z4
            sa, db, da, sb = a1 + a3, b3 - b1, a1 - a3, b1 + b3
            p1, p2 = HALF * (da - sb), HALF * (da + sb)
            values = (
                zp + a2 + sa,
                zm - b2 + p1,
                zp - a2 + db,
                zm + b2 - p2,
                zp + a2 - sa,
                zm - b2 - p1,
                zp - a2 - db,
                zm + b2 + p2,
            )
            for n1 in range(8):
                strain[n1, rows, :] -= values[n1]
            return carry

        lax.fori_loop(0, 8, unstage, 0)

        @pl.when(it < ITERS - 1)
        def _():
            columns_forward(it + 1)

        return carry

    lax.fori_loop(0, ITERS, sweep, 0)

    def to_rows(half, layer, target):
        for j in range(4):
            block = strain[4 * half + j].T
            lanes = slice(128 * j, 128 * j + 128)
            target[layer, 0, :, lanes] = block[0:32]
            target[layer, 1, :, lanes] = block[64:96]
            target[layer, 2, :, lanes] = block[32:64]

    to_rows(1 - c, 0, eig_in)
    final_copy = remote(eig_in.at[0], final.at[mine], core_send.at[2], core_recv.at[2], core_peer)
    final_copy.start()
    to_rows(c, mine, final)
    remote(eig_in.at[0], final.at[other], core_send.at[2], core_recv.at[2], core_peer).wait_recv()
    for k in range(CHUNKS):
        outer_copy2(k).wait_recv()
    for copy in halo + halo2 + [lame_copy, eig_copy, final_copy]:
        copy.wait_send()
    for k in range(CHUNKS):
        outer_copy(k).wait_send()
        outer_copy2(k).wait_send()
    for it in range(ITERS):
        for sent, sem in ((send1, 2 * it), (send2, 2 * it + 1)):
            whole = sent.at[it, pl.ds(0, ROWS - 1)]
            pltpu.make_async_copy(whole, whole, all_send.at[sem]).wait()


def finish(
    middle, base, outer_in2, final, eig, lame, mob, eigen_s, out_hbm, strain_hbm, out, sem
):
    g = lax.axis_index("grp")
    strain_copy = pltpu.make_async_copy(final, strain_hbm, sem.at[8])
    strain_copy.start()
    for place in range(2):
        layer = g if place == 0 else 1 - g

        def at(s, carry):
            rows = pl.ds(pl.multiple_of(8 * s, 8), 8)
            rows2 = pl.ds(pl.multiple_of(8 + 8 * s, 8), 8)
            d = [final[layer, k, rows, :] - eig[layer, k, rows, :] for k in range(3)]
            lam, double = lame[layer, 0, rows, :], 2.0 * lame[layer, 1, rows, :]
            m = mob[layer, rows2, :]
            m05, c1 = 0.05 * m, 0.2 * m
            push = (
                c1 * ((lam + double) * d[0] + lam * d[1]),
                c1 * (lam * d[0] + (lam + double) * d[1]),
                c1 * (2.0 * (double * d[2])),
            )
            for i in range(16):
                v = middle[layer, i, rows2, :]
                value = base[layer, i, rows, :] + v * (
                    push[0] * eigen_s[0, i] + push[1] * eigen_s[1, i] + push[2] * eigen_s[2, i]
                )
                if place == 1:
                    value = value + m05 * outer_in2[i, rows, :]
                out[layer, i, rows, :] = value
            pltpu.make_async_copy(
                out.at[layer, :, rows, :], out_hbm.at[layer, :, rows, :], sem.at[4 * place + s]
            ).start()
            return carry

        lax.fori_loop(0, 4, at, 0)
    for place in range(2):
        layer = g if place == 0 else 1 - g
        for s in range(4):
            rows = pl.ds(8 * s, 8)
            pltpu.make_async_copy(
                out.at[layer, :, rows, :], out_hbm.at[layer, :, rows, :], sem.at[4 * place + s]
            ).wait()
    strain_copy.wait()


def body(order, grain, phase, mobility, index, stiff, eigen, macro):
    constants = tables()
    any_spec = pl.BlockSpec(memory_space=pl.ANY)
    smem = pl.BlockSpec(memory_space=pltpu.SMEM)
    vmem = pl.BlockSpec(memory_space=pltpu.VMEM)
    big = (2, 16, 48, 512)
    every = (ITERS, ROWS, 3, 8, 128)
    columns = (8, 128, 128)
    kept = (
        big, (2, 16, 32, 512), (16, 32, 512), (2, 3, 32, 512), (2, 3, 32, 512), (2, 2, 32, 512),
        (2, 48, 512),
    )
    values = pl.pallas_call(
        kernel,
        out_shape=tuple(pltpu.VMEM(shape, F32) for shape in kept),
        in_specs=[any_spec] * 12 + [smem] * 5,
        out_specs=(vmem,) * len(kept),
        scratch_shapes=[
            pltpu.VMEM(big, F32),
            pltpu.VMEM((2, 32, 512), jnp.int32),
            pltpu.VMEM((2, 32, 512), jnp.int32),
        ]
        + [pltpu.VMEM((4, 256, 256), BF16)] * 4
        + [pltpu.VMEM((256, 256), BF16)] * 4
        + [pltpu.VMEM((32, 2, 128), F32)]
        + [
            pltpu.VMEM((2, 34, 1, 512), F32),
            pltpu.VMEM((2, 34, 1, 512), F32),
            pltpu.VMEM((2, 32, 1, 512), F32),
            pltpu.VMEM((2, 32, 1, 512), F32),
            pltpu.VMEM((34, 32, 128), F32),
            pltpu.VMEM((34, 32, 128), F32),
            pltpu.VMEM((32, 32, 128), F32),
            pltpu.VMEM((32, 32, 128), F32),
            pltpu.VMEM((16, 32, 512), F32),
            pltpu.VMEM((2, 2, 32, 512), F32),
            pltpu.VMEM((2, 3, 32, 512), F32),
        ]
        + [pltpu.VMEM(columns, F32)] * 4
        + [pltpu.VMEM((3, 32, 16, 128), F32)]
        + [pltpu.VMEM(every, F32)] * 4
        + [pltpu.VMEM((4, 8, 2, 16, 128), F32)]
        + [pltpu.VMEM((4, 256, 256), BF16)]
        + [pltpu.VMEM((32, 2, 16, 128), F32)]
        + [pltpu.VMEM((512, 256), BF16)] * 2
        + [
            pltpu.SemaphoreType.DMA((n,))
            for n in (12, 6, 6, 2 * CHUNKS, 2 * CHUNKS, 3, 3, 2 * ITERS, 2 * ITERS)
        ]
        + [pltpu.SemaphoreType.REGULAR((5,))],
        compiler_params=pltpu.CompilerParams(
            collective_id=0, has_side_effects=True, vmem_limit_bytes=48 * 1024 * 1024
        ),
        name="step",
    )(order, grain, phase, *[jnp.asarray(t) for t in constants], mobility, index, stiff.T, eigen.T, macro)
    return pl.pallas_call(
        finish,
        out_shape=(
            jax.ShapeDtypeStruct((2, 16, 32, 512), F32),
            jax.ShapeDtypeStruct((2, 3, 32, 512), F32),
        ),
        in_specs=[vmem] * len(kept) + [smem],
        out_specs=(any_spec, any_spec),
        scratch_shapes=[pltpu.VMEM((2, 16, 32, 512), F32), pltpu.SemaphoreType.DMA((9,))],
        compiler_params=pltpu.CompilerParams(vmem_limit_bytes=6 * 1024 * 1024),
        name="finish",
    )(*values, eigen.T)


def solution(mesh):
    fields = P("grp", None, "row", "col")
    labels = P("grp", "row", "col")
    return jax.shard_map(
        body,
        mesh=mesh,
        in_specs=(fields, labels, labels, P(), P(), P(), P(), P()),
        out_specs=(fields, fields),
        check_vma=False,
    )
```
